128 devices in a mesh: frames: 128 (over y, z, x, core).
Axes of the slice: x: 4, y: 4, z: 4, core: 2. Of those that a mesh axis runs over, the one named last changes fastest.
Arguments:
- mel_frames: bfloat16 [98304, 80], P('frames'), may hold values from -6 to 6
- clip_lengths: int32 [96], replicated, may hold values from 1 to 1500, 49152 in all
- valid_keys: int32 [96], replicated, may hold values from 150 to 1500
- stem_weight: bfloat16 [240, 512], replicated, may hold values from -0.375 to 0.375
- stem_bias: bfloat16 [512], replicated, may hold values from -1.25 to 1.25
- stride_weight: bfloat16 [1536, 512], replicated, may hold values from -0.15625 to 0.15625
- stride_bias: bfloat16 [512], replicated, may hold values from -1.25 to 1.25
- attn_gain: bfloat16 [512], replicated, may hold values from 0.5 to 1.5
- attn_shift: bfloat16 [512], replicated, may hold values from -1.25 to 1.25
- attn_weight: bfloat16 [512, 1536], replicated, may hold values from -0.25 to 0.25
- query_bias: bfloat16 [512], replicated, may hold values from -1.75 to 1.75
- value_bias: bfloat16 [512], replicated, may hold values from -1.75 to 1.75
- output_weight: bfloat16 [512, 512], replicated, may hold values from -2 to 2
- output_bias: bfloat16 [512], replicated, may hold values from -1.25 to 1.25
- mlp_gain: bfloat16 [512], replicated, may hold values from 0.5 to 1.5
- mlp_shift: bfloat16 [512], replicated, may hold values from -1.25 to 1.25
- hidden_weight: bfloat16 [512, 2048], replicated, may hold values from -0.25 to 0.25
- hidden_bias: bfloat16 [2048], replicated, may hold values from -1.25 to 1.25
- return_weight: bfloat16 [2048, 512], replicated, may hold values from -0.125 to 0.125
- return_bias: bfloat16 [512], replicated, may hold values from -1.25 to 1.25
- cotangent: bfloat16 [49152, 512], P('frames'), may hold values from -6 to 6
Outputs:
- layer_out: bfloat16 [49152, 512], P('frames')
- mel_grad: float32 [98304, 80], P('frames')
- grad_stem_weight: float32 [240, 512], replicated
- grad_stem_bias: float32 [512], replicated
- grad_stride_weight: float32 [1536, 512], replicated
- grad_stride_bias: float32 [512], replicated
- grad_attn_gain: float32 [512], replicated
- grad_attn_shift: float32 [512], replicated
- grad_attn_weight: float32 [512, 1536], replicated
- grad_query_bias: float32 [512], replicated
- grad_value_bias: float32 [512], replicated
- grad_output_weight: float32 [512, 512], replicated
- grad_output_bias: float32 [512], replicated
- grad_mlp_gain: float32 [512], replicated
- grad_mlp_shift: float32 [512], replicated
- grad_hidden_weight: float32 [512, 2048], replicated
- grad_hidden_bias: float32 [2048], replicated
- grad_return_weight: float32 [2048, 512], replicated
- grad_return_bias: float32 [512], replicated
The draws below stay inside these ranges and needn't reach their ends.
Inputs may be any that keep to these rules, and one draw needn't show every extreme that they name: `clip_lengths`: the clips fill all 49152 tokens, and one clip has exactly 1500 tokens.
All inputs are finite; a program needn't handle non-finite values.
Results may differ from the reference program's by a relative error of at most 0.014.
Values may be sent and summed in bfloat16 or wider, within the bound.
No kernel may reach another device: no remote copies, remote signals or barrier semaphores. Data moves between devices by JAX's collectives and lax.ppermute only.
A program may use at most 320 MiB of HBM per device.

```python
import math
import jax
import jax.numpy as jnp
import numpy as np
from jax import lax

D = 512
HEADS = 8
FF = 2048
MELS = 80
MAXLEN = 1500
TOK_DEV = 384
MINVALID = 150
TOKENS = 49152
CLIPS = 96


def plant(array, own_key, smallest, largest):
    spot = [jax.random.randint(jax.random.fold_in(own_key, axis), (), 0, length) for axis, length in enumerate(array.shape)]
    main_axis = array.shape.index(max(array.shape))
    neighbour = spot[:main_axis] + [(spot[main_axis] + 1) % array.shape[main_axis]] + spot[main_axis + 1:]
    return array.at[tuple(spot)].set(smallest).at[tuple(neighbour)].set(largest)


def steps_of(rng, shape, shards, least, high):
    def one(axis_at, blocks):
        heights = jax.random.uniform(jax.random.fold_in(jax.random.fold_in(rng, 6), axis_at), (blocks,), jnp.float32, least / len(shards), high / len(shards))
        return jnp.repeat(jnp.exp(heights), shape[axis_at] // blocks).reshape((-1,) + (1,) * (len(shape) - axis_at - 1))

    level = one(*shards[0])
    for cut in shards[1:]:
        level = level * one(*cut)
    return level


def profile(number_of, total, bound, lean):
    portions = [(1 << 20) // math.isqrt(standing ** lean) + 1 for standing in range(2, number_of + 1)]
    spare, given = total - bound - (number_of - 1), [1] * (number_of - 1)
    while spare > 0:
        candidates = [i for i in range(number_of - 1) if given[i] < bound]
        whole, budget = sum([portions[i] for i in candidates]), spare
        for i in candidates:
            extra = min(bound - given[i], max(1, budget * portions[i] // whole), spare)
            given[i] = given[i] + extra
            spare = spare - extra
    return np.array([bound] + given)


def uneven(rng, amount, total, bound, slope):
    if amount == 2:
        one = jax.random.randint(rng, (), max(1, total - bound), min(bound, total - 1) + 1)
        return jnp.stack([one, total - one])
    sizes = jnp.asarray(profile(amount, total, bound, slope), jnp.int32)
    pairs = (amount - 1) // 2
    giver, taker = sizes[1:1 + 2 * pairs:2], sizes[2:2 + 2 * pairs:2]
    slack = jnp.minimum(giver - 1, bound - taker)
    shifted = jax.random.randint(jax.random.fold_in(rng, 1), (pairs,), 0, 1 << 20) % (slack + 1)
    sizes = sizes.at[1:1 + 2 * pairs:2].set(giver - shifted).at[2:2 + 2 * pairs:2].set(taker + shifted)
    return sizes[jax.random.permutation(jax.random.fold_in(rng, 2), amount)]


def scatter_about(stream_key, extent, scale, reach, shards=(), kind=jnp.bfloat16):
    factor_of = steps_of(stream_key, extent, shards, -0.22, 0.18) if shards else 1.0
    drawn = jax.random.normal(stream_key, extent, jnp.float32) * scale * factor_of
    return jnp.minimum(jnp.maximum(drawn, -reach), reach).astype(kind)


def setup_inputs(seed: int = 0) -> dict:
    seeds = jax.random.split(jax.random.key(seed), 22)
    return {
        "mel_frames": scatter_about(seeds[0], (2 * TOKENS, MELS), 1.0, 6.0, ((0, 128),)),
        "clip_lengths": uneven(seeds[1], CLIPS, TOKENS, MAXLEN, 2).astype(jnp.int32),
        "valid_keys": plant(jax.random.randint(seeds[2], (CLIPS,), MINVALID, MAXLEN + 1), jax.random.fold_in(seeds[2], 1), MINVALID, MAXLEN).astype(jnp.int32),
        "stem_weight": scatter_about(seeds[3], (3 * MELS, D), (3 * MELS) ** -0.5, 0.375),
        "stem_bias": scatter_about(seeds[4], (D,), 0.2, 1.25),
        "stride_weight": scatter_about(seeds[5], (3 * D, D), (3 * D) ** -0.5, 0.15625),
        "stride_bias": scatter_about(seeds[6], (D,), 0.2, 1.25),
        "attn_gain": jnp.clip(1.0 + 0.1 * jax.random.normal(seeds[7], (D,), jnp.float32), 0.5, 1.5).astype(jnp.bfloat16),
        "attn_shift": scatter_about(seeds[8], (D,), 0.2, 1.25),
        "attn_weight": scatter_about(seeds[9], (D, 3 * D), D ** -0.5, 0.25),
        "query_bias": scatter_about(seeds[10], (D,), 0.3, 1.75),
        "value_bias": scatter_about(seeds[11], (D,), 0.3, 1.75),
        "output_weight": scatter_about(seeds[12], (D, D), (D // 64) ** -0.5, 2.0),
        "output_bias": scatter_about(seeds[13], (D,), 0.2, 1.25),
        "mlp_gain": jnp.clip(1.0 + 0.1 * jax.random.normal(seeds[14], (D,), jnp.float32), 0.5, 1.5).astype(jnp.bfloat16),
        "mlp_shift": scatter_about(seeds[15], (D,), 0.2, 1.25),
        "hidden_weight": scatter_about(seeds[16], (D, FF), D ** -0.5, 0.25),
        "hidden_bias": scatter_about(seeds[17], (FF,), 0.2, 1.25),
        "return_weight": scatter_about(seeds[18], (FF, D), FF ** -0.5, 0.125),
        "return_bias": scatter_about(seeds[19], (D,), 0.2, 1.25),
        "cotangent": scatter_about(seeds[20], (TOKENS, D), 1.0, 6.0, ((0, 128),)),
    }


@jax.custom_vjp
def low(v):
    return lax.optimization_barrier(v.astype(jnp.bfloat16)).astype(jnp.float32)

@jax.custom_vjp
def low_back(v):
    return v

def low_keep(v):
    return (low(v), None)

def low_pass(kept, grad):
    return (grad,)

def back_keep(v):
    return (v, None)

def back_low(kept, grad):
    return (low(grad),)
low.defvjp(low_keep, low_pass)
low_back.defvjp(back_keep, back_low)

def product(left, right):
    return jnp.dot(left, right, precision=lax.Precision.HIGHEST, preferred_element_type=jnp.float32)

def layer_norm(values, gain, shift):
    center = lax.optimization_barrier(jnp.mean(values, axis=-1, keepdims=True))
    centered = values - center
    spread = lax.optimization_barrier(jnp.mean(centered * centered, axis=-1, keepdims=True))
    return centered * lax.rsqrt(spread + 1e-05) * gain + shift

def gelu_exact(values):
    return jax.nn.gelu(values, approximate=False)

def sinusoid(position, model_width):
    half_width = model_width // 2
    increment = math.log(10000.0) / (half_width - 1)
    rates = jnp.exp(-increment * jnp.arange(half_width, dtype=jnp.float32))
    angles = position.astype(jnp.float32)[:, None] * rates[None, :]
    return jnp.concatenate([jnp.sin(angles), jnp.cos(angles)], axis=1)

def clip_tables(clip_lengths, token_index):
    clip_starts = jnp.cumsum(clip_lengths) - clip_lengths
    member = (clip_starts[None, :] <= token_index[:, None]).astype(jnp.int32)
    clip_of = lax.optimization_barrier(jnp.sum(member, axis=1)) - 1
    numbers = jnp.arange(clip_lengths.shape[0], dtype=jnp.int32)
    onehot = (clip_of[:, None] == numbers[None, :]).astype(jnp.int32)
    position = token_index - lax.optimization_barrier(jnp.sum(onehot * clip_starts[None, :], axis=1))
    return (clip_of, position, onehot)

def frame_masks(first_flag, token_count):
    opened = 1.0 - first_flag.astype(jnp.float32)
    always = jnp.ones((token_count,), jnp.float32)
    left_open = jnp.stack([opened[:token_count], always], axis=1).reshape(-1)
    right_open = jnp.stack([always, opened[1:]], axis=1).reshape(-1)
    return (opened, left_open, right_open)

def attend(projected, clip_of, key_open):
    head_size = D // HEADS
    score_scale = 1.0 / math.sqrt(head_size)
    query_heads = projected[:, :D].reshape(TOKENS, HEADS, head_size)
    padding = ((MAXLEN, MAXLEN), (0, 0), (0, 0))
    key_heads = jnp.pad(projected[:, D:2 * D].reshape(TOKENS, HEADS, head_size), padding)
    value_heads = jnp.pad(projected[:, 2 * D:].reshape(TOKENS, HEADS, head_size), padding)
    key_clip = jnp.pad(clip_of, (MAXLEN, MAXLEN), constant_values=-1)
    key_usable = jnp.pad(key_open, (MAXLEN, MAXLEN))
    span_rows = TOK_DEV + 2 * MAXLEN

    def one_block(block_number):
        first_row = (block_number * TOK_DEV).astype(jnp.int32)
        query_block = lax.dynamic_slice_in_dim(query_heads, first_row, TOK_DEV, 0)
        query_clip = lax.dynamic_slice_in_dim(clip_of, first_row, TOK_DEV, 0)
        key_block = lax.dynamic_slice_in_dim(key_heads, first_row, span_rows, 0)
        value_block = lax.dynamic_slice_in_dim(value_heads, first_row, span_rows, 0)
        clip_block = lax.dynamic_slice_in_dim(key_clip, first_row, span_rows, 0)
        usable_block = lax.dynamic_slice_in_dim(key_usable, first_row, span_rows, 0)
        scores = low_back(jnp.einsum('qhe,khe->hqk', query_block, key_block, precision=lax.Precision.HIGHEST, preferred_element_type=jnp.float32) * score_scale)
        allowed = (query_clip[:, None] == clip_block[None, :]) & usable_block[None, :]
        masked = jnp.where(allowed[None], scores, -1e+30)
        row_max = lax.optimization_barrier(jnp.max(masked, axis=-1, keepdims=True))
        expanded = jnp.exp(masked - row_max)
        softmax_out = expanded / lax.optimization_barrier(jnp.sum(expanded, axis=-1, keepdims=True))
        return jnp.einsum('hqk,khe->qhe', low(softmax_out), value_block, precision=lax.Precision.HIGHEST, preferred_element_type=jnp.float32)
    block_outs = lax.map(jax.checkpoint(one_block), jnp.arange(TOKENS // TOK_DEV, dtype=jnp.int32))
    return block_outs.reshape(TOKENS, D)

def reference(mel_frames, clip_lengths, valid_keys, stem_weight, stem_bias, stride_weight, stride_bias, attn_gain, attn_shift, attn_weight, query_bias, value_bias, output_weight, output_bias, mlp_gain, mlp_shift, hidden_weight, hidden_bias, return_weight, return_bias, cotangent):
    token_index = jnp.arange(TOKENS + 1, dtype=jnp.int32)
    clip_all, position_all, onehot_all = clip_tables(clip_lengths, token_index)
    first_flag = (position_all == 0) | (token_index >= TOKENS)
    opened, left_open, right_open = frame_masks(first_flag, TOKENS)
    clip_of = clip_all[:TOKENS]
    position = position_all[:TOKENS]
    valid_of = lax.optimization_barrier(jnp.sum(onehot_all[:TOKENS] * valid_keys[None, :], axis=1))
    key_open = position < valid_of
    table = sinusoid(position, D)

    def forward(mel_values, w_stem, b_stem, w_stride, b_stride, gain_one, shift_one, w_attn, b_query, b_value, w_output, b_output, gain_two, shift_two, w_hidden, b_hidden, w_return, b_return):
        nothing_mel = jnp.zeros((1, MELS), jnp.float32)
        earlier_mel = jnp.concatenate([nothing_mel, mel_values[:-1]], axis=0) * left_open[:, None]
        later_mel = jnp.concatenate([mel_values[1:], nothing_mel], axis=0) * right_open[:, None]
        stem_columns = jnp.concatenate([earlier_mel, mel_values, later_mel], axis=1)
        stem_act = low(gelu_exact(low_back(product(stem_columns, w_stem) + b_stem)))
        frame_pairs = stem_act.reshape(TOKENS, 2 * D)
        earlier_odd = jnp.concatenate([jnp.zeros((1, D), jnp.float32), frame_pairs[:-1, D:]], axis=0) * opened[:TOKENS, None]
        stride_columns = jnp.concatenate([earlier_odd, frame_pairs], axis=1)
        layer_in = gelu_exact(low_back(product(stride_columns, w_stride) + b_stride)) + table
        attn_in = low(layer_norm(layer_in, gain_one, shift_one))
        joint_bias = jnp.concatenate([b_query, jnp.zeros((D,), jnp.float32), b_value])
        projected = low(low_back(product(attn_in, w_attn) + joint_bias))
        context = low(low_back(attend(projected, clip_of, key_open)))
        middle = layer_in + low_back(product(context, w_output) + b_output)
        mlp_in = low(layer_norm(middle, gain_two, shift_two))
        hidden_act = low(gelu_exact(low_back(product(mlp_in, w_hidden) + b_hidden)))
        return middle + low_back(product(hidden_act, w_return) + b_return)
    primals = (mel_frames.astype(jnp.float32), stem_weight.astype(jnp.float32), stem_bias.astype(jnp.float32), stride_weight.astype(jnp.float32), stride_bias.astype(jnp.float32), attn_gain.astype(jnp.float32), attn_shift.astype(jnp.float32), attn_weight.astype(jnp.float32), query_bias.astype(jnp.float32), value_bias.astype(jnp.float32), output_weight.astype(jnp.float32), output_bias.astype(jnp.float32), mlp_gain.astype(jnp.float32), mlp_shift.astype(jnp.float32), hidden_weight.astype(jnp.float32), hidden_bias.astype(jnp.float32), return_weight.astype(jnp.float32), return_bias.astype(jnp.float32))
    layer_out, pullback = jax.vjp(forward, *primals)
    grads = pullback(cotangent.astype(jnp.float32))
    return (layer_out.astype(jnp.bfloat16), grads[0], grads[1], grads[2], grads[3], grads[4], grads[5], grads[6], grads[7], grads[8], grads[9], grads[10], grads[11], grads[12], grads[13], grads[14], grads[15], grads[16], grads[17])
```

```python
import functools
import math

import jax
import jax.numpy as jnp
from jax import lax
from jax.experimental import pallas as pl
from jax.experimental.pallas import tpu as pltpu
from jax.sharding import PartitionSpec as P

HEADS = 8
SIDE = 2
QB = 128
KB = 256
PAD = 16
SLOT = 128
NEG = -1e30
BF = jnp.bfloat16
F32 = jnp.float32
MIB = 1 << 20


def nn(a, b):
    return lax.dot_general(a, b, (((1,), (0,)), ((), ())), preferred_element_type=F32)


def nt(a, b):
    return lax.dot_general(a, b, (((1,), (1,)), ((), ())), preferred_element_type=F32)


def tn(a, b):
    return lax.dot_general(a, b, (((0,), (0,)), ((), ())), preferred_element_type=F32)


def gelu_pair(x):
    bell = jnp.exp(-0.5 * x * x)
    t = 1.0 / (1.0 + 0.2316419 * jnp.abs(x))
    poly = 0.127414796 + t * (-0.142248368 + t * (0.7107068705 + t * (-0.7265760135 + t * 0.5307027145)))
    tail = bell * t * poly
    phi = jnp.where(x >= 0, 1.0 - tail, tail)
    return x * phi, phi + 0.3989422804 * x * bell


def norm_parts(x):
    center = jnp.mean(x, axis=-1, keepdims=True)
    centered = x - center
    rstd = lax.rsqrt(jnp.mean(centered * centered, axis=-1, keepdims=True) + 1e-05)
    return centered * rstd, rstd


def norm_back(grad, xhat, rstd, gain):
    inner = grad * gain
    m1 = jnp.mean(inner, axis=-1, keepdims=True)
    m2 = jnp.mean(inner * xhat, axis=-1, keepdims=True)
    return rstd * (inner - m1 - xhat * m2)


def vector(ref):
    return ref[...].astype(F32).reshape(1, -1)


def colsum(x):
    return jnp.sum(x, axis=0, keepdims=True)


def halves(x, low):
    zero = jnp.zeros_like(x)
    return jnp.concatenate([jnp.where(low, x, zero), jnp.where(low, zero, x)], axis=0)


def pick(x, low):
    return jnp.where(low, x[:QB], x[QB:])


def wide(x):
    return jnp.concatenate([x, x], axis=1)


def tall(x):
    return jnp.concatenate([x, x], axis=0)


def tables_kernel(device, lengths, valids, spans_o, pack_o, table_o, keys_o, queries_o, start_s, length_s, valid_s, *, total):
    count, width = table_o.shape
    base = (device[0] - device[0] % 2 - 2 * SIDE) * count
    first = device[0] * count
    token = first + lax.broadcasted_iota(jnp.int32, (count, 128), 0)
    row = lax.broadcasted_iota(jnp.int32, pack_o.shape, 0) + lax.broadcasted_iota(jnp.int32, pack_o.shape, 1) - PAD
    here = (row >= 0) & (row <= count) & (first + row < total)
    pack_o[...] = jnp.where(here, 1.0, 0.0)
    keys_o[0] = queries_o[0] = device[0] % 2

    def clip(c, start):
        length = lengths[c]
        valid = jnp.minimum(valids[c], length)
        end = start + length

        @pl.when((start < first + count) & (end > first))
        def _():
            inside = (token >= start) & (token < end)
            start_s[...] = jnp.where(inside, start, start_s[...])
            length_s[...] = jnp.where(inside, length, length_s[...])
            valid_s[...] = jnp.where(inside, valid, valid_s[...])
            for n in range(count // QB):
                at = first + n * QB

                @pl.when((start <= at) & (at < end))
                def _():
                    keys_o[4 + 2 * n] = queries_o[4 + 2 * n] = ((start - base) >> 7) << 7

                @pl.when((start < at + QB) & (at + QB <= end))
                def _():
                    keys_o[5 + 2 * n] = start + valid - base
                    queries_o[5 + 2 * n] = end - base

        @pl.when((start >= first) & (start <= first + count))
        def _():
            pack_o[...] = jnp.where(first + row == start, 0.0, pack_o[...])

        return end

    lax.fori_loop(0, lengths.shape[0], clip, 0)
    for plan in (keys_o, queries_o):
        low, high = plan[4], 0
        for n in range(count // QB):
            steps = (plan[5 + 2 * n] - plan[4 + 2 * n] + KB - 1) // KB
            plan[5 + 2 * n] = steps
            low = jnp.minimum(low, plan[4 + 2 * n])
            high = jnp.maximum(high, plan[4 + 2 * n] + steps * KB)
        plan[1], plan[2] = low, high
    lane = lax.broadcasted_iota(jnp.int32, (count, 128), 1)
    key_lo = start_s[...] - base
    position = token - start_s[...]
    is_key = position < valid_s[...]
    query_lo = jnp.where(is_key, key_lo, 1 << 20)
    query_hi = jnp.where(is_key, key_lo + length_s[...], 0)
    first_two = jnp.where(lane == 0, key_lo, key_lo + valid_s[...])
    spans_o[...] = jnp.where(lane < 2, first_two, jnp.where(lane == 2, query_lo, query_hi))
    half = width // 2
    number = lax.broadcasted_iota(jnp.int32, (1, half), 1).astype(F32)
    rates = jnp.exp(number * (-math.log(10000.0) / (half - 1)))
    angles = wide(position.astype(F32)) * rates
    table_o[:, :half] = jnp.sin(angles)
    table_o[:, half:] = jnp.cos(angles)


def taps_of(wbig, sw):
    mels, width = sw.shape[0] // 3, sw.shape[1]
    wbig[...] = jnp.zeros_like(wbig)
    for t in range(3):
        tap = sw[t * mels : (t + 1) * mels, :]
        wbig[t * SLOT : t * SLOT + mels, :width] = tap
        wbig[(t + 1) * SLOT : (t + 1) * SLOT + mels, width:] = tap


def stem_kernel(
    mel, left, right, sw, sbias, vw, vbias, gain, shift, pack, table,
    x_o, act_o, dstem_o, dstride_o, lin_o, ain_o, m, wbig, y0,
):
    count, width = lin_o.shape
    frames, mels = mel.shape
    ext = x_o.shape[0]
    taps_of(wbig, sw)
    top = 2 * PAD + 8
    m[...] = jnp.zeros_like(m)
    m[top : top + frames, :mels] = mel[...].astype(F32)
    m[top - 2 : top, :mels] = left[...].astype(F32)
    m[top + frames : top + frames + 2, :mels] = right[...].astype(F32)
    opn, opn_next = pack[:, 0:1], pack[:, 1:2]
    x_o[:, :SLOT] = (m[pl.ds(7, ext, stride=2), :] * opn).astype(BF)
    x_o[:, SLOT : 2 * SLOT] = m[pl.ds(8, ext, stride=2), :].astype(BF)
    x_o[:, 2 * SLOT : 3 * SLOT] = m[pl.ds(9, ext, stride=2), :].astype(BF)
    x_o[:, 3 * SLOT :] = (m[pl.ds(10, ext, stride=2), :] * opn_next).astype(BF)
    for half in range(2):
        cols = slice(half * width, (half + 1) * width)
        act, dact = gelu_pair(nn(x_o[...], wbig[:, cols]) + vector(sbias))
        act_o[:, cols] = act.astype(BF)
        dstem_o[:, cols] = dact
    y0[...] = nn(act_o[:, width:], vw[:width, :])
    pre = nn(act_o[PAD : PAD + count, :], vw[width:, :]) + vector(vbias)
    pre = pre + y0[PAD - 1 : PAD + count - 1, :] * pack[PAD : PAD + count, 0:1]
    act2, dact2 = gelu_pair(pre)
    dstride_o[...] = dact2
    lin = act2 + table[...]
    lin_o[...] = lin
    xhat, _ = norm_parts(lin)
    ain_o[...] = (xhat * vector(gain) + vector(shift)).astype(BF)


def needed(sc, block, count):
    return (block * count < sc[2]) & ((block + 1) * count > sc[1])


def start_copies(sc, pairs, sem, count):
    for block, copies in pairs:
        @pl.when(needed(sc, block, count))
        def _():
            for m, (src, dst) in enumerate(copies):
                pltpu.make_async_copy(src, dst, sem.at[block, m]).start()


def wait_until(sc, end, copies, sem, count, there):
    def one(block, _):
        @pl.when(needed(sc, block, count))
        def _():
            for m, (src, dst) in enumerate(copies(block)):
                pltpu.make_async_copy(src, dst, sem.at[block, m]).wait()

        return 0

    upto = jnp.minimum((end + count - 1) // count, 2 * (2 * SIDE + 1))
    lax.fori_loop(there[0], upto, one, 0)
    there[0] = jnp.maximum(there[0], upto)


def window(sc, own, sib):
    core = sc[0]
    out = []
    for k in range(2 * SIDE + 1):
        out += [(2 * k + core, own[k]), (2 * k + 1 - core, sib[k])]
    return out


def rows_of(block, count):
    return pl.ds(pl.multiple_of(block * count, count), count)


def in_range(lo, hi, start):
    col = start + lax.broadcasted_iota(jnp.int32, (QB, KB), 1)
    return jnp.where((col >= lo) & (col < hi), 0.0, NEG)


def chunks(first, steps, step, wait):
    def two(n, _):
        wait(first + (2 * n + 2) * KB)
        step(2 * n, 2)
        return 0

    lax.fori_loop(0, steps // 2, two, 0)

    @pl.when(steps % 2 == 1)
    def _():
        wait(first + steps * KB)
        step(steps - 1, 1)


def forward_kernel(*refs):
    nb = 2 * SIDE + 1
    sc, span_ref = refs[:2]
    own, sib = refs[2 : 2 + nb], refs[2 + nb : 2 + 2 * nb]
    ctx_o, lse_o, local_ref, kv, q2, acc, peak, total, scale, s, e, there, sem, sem2 = refs[2 + 2 * nb :]
    count, width = ctx_o.shape
    span = 2 * nb * count
    pairs = width // 128
    kv[span:, :] = jnp.zeros((kv.shape[0] - span, 2 * width), BF)
    there[0] = 0

    def copies(block, src=own[0]):
        return [(src.at[:, pl.ds(width, 2 * width)], kv.at[rows_of(block, count), :])]

    local = pltpu.make_async_copy(own[SIDE].at[:, pl.ds(0, width)], local_ref, sem2.at[0])
    local.start()
    start_copies(sc, [(block, copies(block, src)) for block, src in window(sc, own, sib)], sem, count)
    local.wait()

    def wait(end):
        wait_until(sc, end, copies, sem, count, there)

    low = lax.broadcasted_iota(jnp.int32, (QB, 128), 1) < 64
    lanes = lax.broadcasted_iota(jnp.int32, (QB, 128), 1)

    def one(i, _):
        rows = pl.ds(pl.multiple_of(i * QB, QB), QB)
        for p in range(pairs):
            q2[p] = halves(local_ref[rows, p * 128 : (p + 1) * 128], low) * jnp.asarray(0.125, BF)
            acc[p] = jnp.zeros_like(acc[p])
            peak[p] = jnp.full_like(peak[p], NEG)
            total[p] = jnp.zeros_like(total[p])
        lo, hi = span_ref[rows, 0:1], span_ref[rows, 1:2]

        def step(n, parts):
            start = sc[4 + 2 * i] + n * KB
            keys = [pl.ds(pl.multiple_of(start + u * KB, 128), KB) for u in range(parts)]
            for u in range(parts):
                bias = tall(in_range(lo, hi, start + u * KB))
                for p in range(pairs):
                    s[u, p] = nt(q2[p], kv[keys[u], p * 128 : (p + 1) * 128]) + bias
            for p in range(pairs):
                best = functools.reduce(jnp.maximum, [s[u, p] for u in range(parts)])
                old = peak[p]
                top = jnp.maximum(old, jnp.max(best, axis=1, keepdims=True))
                peak[p] = top
                scale[p] = jnp.exp(old - top)
            for p in range(pairs):
                total[p] = scale[p] * total[p]
                for u in range(parts):
                    grown = jnp.exp(s[u, p] - wide(peak[p]))
                    e[u, p] = grown.astype(BF)
                    total[p] = total[p] + (grown[:, :128] + grown[:, 128:])
            for p in range(pairs):
                value = [kv[keys[u], width + p * 128 : width + (p + 1) * 128] for u in range(parts)]
                acc[p] = scale[p] * acc[p] + functools.reduce(jnp.add, [nn(e[u, p], value[u]) for u in range(parts)])

        chunks(sc[4 + 2 * i], sc[5 + 2 * i], step, wait)
        lse = jnp.zeros((QB, 128), F32)
        for p in range(pairs):
            row_total = jnp.sum(total[p], axis=1, keepdims=True)
            ctx_o[rows, p * 128 : (p + 1) * 128] = pick(acc[p] / row_total, low)
            both = peak[p] + jnp.log(row_total)
            lse = jnp.where(lanes == 2 * p, both[:QB], lse)
            lse = jnp.where(lanes == 2 * p + 1, both[QB:], lse)
        lse_o[rows, :] = lse
        return 0

    lax.fori_loop(0, count // QB, one, 0)
    wait(span)


def query_kernel(*refs):
    nb = 2 * SIDE + 1
    sc, span_ref, pay_ref, lse_ref, dlt_ref = refs[:5]
    own, sib = refs[5 : 5 + nb], refs[5 + nb : 5 + 2 * nb]
    dq_o, local_ref, kv, q2, do2, acc, lse2, dlt2, s, d, ds, there, sem, sem2 = refs[5 + 2 * nb :]
    count, width = dq_o.shape
    span = 2 * nb * count
    pairs = width // 128
    kv[span:, :] = jnp.zeros((kv.shape[0] - span, 2 * width), BF)
    there[0] = 0

    def copies(block, src=own[0]):
        return [(src.at[:, pl.ds(width, 2 * width)], kv.at[rows_of(block, count), :])]

    local = pltpu.make_async_copy(own[SIDE].at[:, pl.ds(0, width)], local_ref, sem2.at[0])
    local.start()
    start_copies(sc, [(block, copies(block, src)) for block, src in window(sc, own, sib)], sem, count)
    local.wait()

    def wait(end):
        wait_until(sc, end, copies, sem, count, there)

    low = lax.broadcasted_iota(jnp.int32, (QB, 128), 1) < 64

    def one(i, _):
        rows = pl.ds(pl.multiple_of(i * QB, QB), QB)
        lse, dlt = lse_ref[rows, :], dlt_ref[rows, :]
        for p in range(pairs):
            q2[p] = halves(local_ref[rows, p * 128 : (p + 1) * 128], low) * jnp.asarray(0.125, BF)
            do2[p] = halves(pay_ref[rows, p * 128 : (p + 1) * 128], low)
            acc[p] = jnp.zeros_like(acc[p])
            for h in range(2):
                part = pl.ds(h * QB, QB)
                lse2[p, part, :] = jnp.broadcast_to(lse[:, 2 * p + h : 2 * p + h + 1], (QB, 128))
                dlt2[p, part, :] = jnp.broadcast_to(dlt[:, 2 * p + h : 2 * p + h + 1], (QB, 128))
        lo, hi = span_ref[rows, 0:1], span_ref[rows, 1:2]

        def step(n, parts):
            start = sc[4 + 2 * i] + n * KB
            keys = [pl.ds(pl.multiple_of(start + u * KB, 128), KB) for u in range(parts)]
            for u in range(parts):
                bias = tall(in_range(lo, hi, start + u * KB))
                for p in range(pairs):
                    s[u, p] = nt(q2[p], kv[keys[u], p * 128 : (p + 1) * 128]) + bias
                    d[u, p] = nt(do2[p], kv[keys[u], width + p * 128 : width + (p + 1) * 128])
            for u in range(parts):
                for p in range(pairs):
                    e = jnp.exp(s[u, p] - wide(lse2[p]))
                    ds[u, p] = (e * (d[u, p] - wide(dlt2[p]))).astype(BF)
            for p in range(pairs):
                more = [nn(ds[u, p], kv[keys[u], p * 128 : (p + 1) * 128]) for u in range(parts)]
                acc[p] = acc[p] + functools.reduce(jnp.add, more)

        chunks(sc[4 + 2 * i], sc[5 + 2 * i], step, wait)
        for p in range(pairs):
            dq_o[rows, p * 128 : (p + 1) * 128] = (pick(acc[p], low) * 0.125).astype(BF)
        return 0

    lax.fori_loop(0, count // QB, one, 0)
    wait(span)


def key_kernel(*refs):
    nb = 2 * SIDE + 1
    sc, span_ref, dq_ref, w_ref, lin_ref, gm_ref, gain, dstride_ref = refs[:8]
    own, sib = refs[8 : 8 + nb], refs[8 + nb : 8 + 2 * nb]
    ownp, sibp = refs[8 + 2 * nb : 8 + 3 * nb], refs[8 + 3 * nb : 8 + 4 * nb]
    gp_o, gsp_o, sums_o, kvl, q, do, stat, lse, dlt, k2, v2, dk, dv, s, d, e, ds, there, sem, sem2, sem3 = refs[8 + 4 * nb :]
    count, width = gsp_o.shape
    span = 2 * nb * count
    pairs = width // 128
    rest = q.shape[0] - span
    q[span:, :] = jnp.zeros((rest, width), BF)
    do[span:, :] = jnp.zeros((rest, width), BF)
    stat[:, span:] = jnp.zeros((stat.shape[0], rest), BF)
    there[0] = 0

    def copies(block, src=own[0], pay=ownp[0]):
        return [
            (src.at[:, pl.ds(0, width)], q.at[rows_of(block, count), :]),
            (pay.at[pl.ds(0, count), :], do.at[rows_of(block, count), :]),
        ]

    def side(block, pay=ownp[0]):
        return [(pay.at[pl.ds(count, 48), pl.ds(0, count)], stat.at[:, rows_of(block, count)])]

    local = pltpu.make_async_copy(own[SIDE].at[:, pl.ds(width, 2 * width)], kvl, sem3.at[0])
    local.start()
    sources = list(zip(window(sc, own, sib), window(sc, ownp, sibp)))
    start_copies(sc, [(block, side(block, pay)) for _, (block, pay) in sources], sem2, count)
    start_copies(sc, [(block, copies(block, src, pay)) for (block, src), (_, pay) in sources], sem, count)

    def wait(end):
        wait_until(sc, end, copies, sem, count, there)

    local.wait()
    wait_until(sc, span, side, sem2, count, there)
    there[0] = 0
    lse[...] = stat[0:8, :].astype(F32) + stat[8:16, :].astype(F32) + stat[16:24, :].astype(F32)
    dlt[...] = stat[24:32, :].astype(F32) + stat[32:40, :].astype(F32) + stat[40:48, :].astype(F32)
    low = lax.broadcasted_iota(jnp.int32, (QB, 128), 1) < 64

    def one(i, _):
        rows = pl.ds(pl.multiple_of(i * QB, QB), QB)
        for p in range(pairs):
            k2[p] = halves(kvl[rows, p * 128 : (p + 1) * 128], low) * jnp.asarray(0.125, BF)
            v2[p] = halves(kvl[rows, width + p * 128 : width + (p + 1) * 128], low)
            dk[p] = jnp.zeros_like(dk[p])
            dv[p] = jnp.zeros_like(dv[p])
        lo, hi = span_ref[rows, 2:3], span_ref[rows, 3:4]

        def step(n, parts):
            start = sc[4 + 2 * i] + n * KB
            queries = [pl.ds(pl.multiple_of(start + u * KB, 128), KB) for u in range(parts)]
            for u in range(parts):
                for p in range(pairs):
                    lanes = slice(p * 128, (p + 1) * 128)
                    s[u, p] = nt(k2[p], q[queries[u], lanes])
                    d[u, p] = nt(v2[p], do[queries[u], lanes])
            for u in range(parts):
                bias = in_range(lo, hi, start + u * KB)
                for p in range(pairs):
                    for h in range(2):
                        part = slice(h * QB, (h + 1) * QB)
                        head = slice(2 * p + h, 2 * p + h + 1)
                        grown = jnp.exp(s[u, p, part] + (bias - lse[head, queries[u]]))
                        e[u, p, part] = grown.astype(BF)
                        ds[u, p, part] = (grown * (d[u, p, part] - dlt[head, queries[u]])).astype(BF)
            for p in range(pairs):
                lanes = slice(p * 128, (p + 1) * 128)
                dv[p] = dv[p] + functools.reduce(jnp.add, [nn(e[u, p], do[queries[u], lanes]) for u in range(parts)])
                dk[p] = dk[p] + functools.reduce(jnp.add, [nn(ds[u, p], q[queries[u], lanes]) for u in range(parts)])

        chunks(sc[4 + 2 * i], sc[5 + 2 * i], step, wait)
        for p in range(pairs):
            gp_o[rows, width + p * 128 : width + (p + 1) * 128] = (pick(dk[p], low) * 0.125).astype(BF)
            gp_o[rows, 2 * width + p * 128 : 2 * width + (p + 1) * 128] = pick(dv[p], low).astype(BF)
        return 0

    lax.fori_loop(0, count // QB, one, 0)
    wait(span)
    gp_o[:, :width] = dq_ref[...]
    grad = nt(gp_o[...], w_ref[...])
    xhat, rstd = norm_parts(lin_ref[...])
    total = gm_ref[...] + norm_back(grad, xhat, rstd, vector(gain))
    gsp_o[...] = (total * dstride_ref[...]).astype(BF)
    sums_o[0:1, :] = colsum(grad * xhat)
    sums_o[1:2, :] = colsum(grad)
    sums_o[2:3, :] = colsum(gp_o[:, :width].astype(F32))
    sums_o[3:4, :] = colsum(gp_o[:, 2 * width :].astype(F32))
    sums_o[4:8, :] = jnp.zeros((4, width), F32)


def pieces(x, n):
    out = []
    for _ in range(n):
        part = x.astype(BF)
        out.append(part)
        x = x - part.astype(F32)
    return out


def mlp_kernel(
    ctx, lin, dy, lse, wo, w1, w2, bo, b1, b2, gain_ref, shift,
    out_o, act_o, ghp_o, mi_o, gm_o, gb_o, ctx_o, pay_o, dlt_o, sums_o, out_acc, gmi_acc,
):
    count, width = lin.shape
    ff = w1.shape[1]
    context = ctx[...]
    ctx_o[...] = context.astype(BF)
    middle = lin[...] + nn(ctx_o[...], wo[...]) + vector(bo)
    xhat, rstd = norm_parts(middle)
    gain = vector(gain_ref)
    mi_o[...] = (xhat * gain + vector(shift)).astype(BF)
    grad_out = dy[...].astype(F32)
    sums_o[7:8, :] = colsum(grad_out)
    for f in range(ff // width):
        cols = slice(f * width, (f + 1) * width)
        act, dact = gelu_pair(nn(mi_o[...], w1[:, cols]) + vector(b1.at[cols]))
        act_o[:, cols] = act.astype(BF)
        ghp = (nt(dy[...], w2[cols, :]) * dact).astype(BF)
        ghp_o[:, cols] = ghp
        sums_o[3 + f : 4 + f, :] = colsum(ghp.astype(F32))
        more = nn(act_o[:, cols], w2[cols, :])
        gmore = nt(ghp_o[:, cols], w1[:, cols])
        if f == 0:
            out_acc[...] = middle + vector(b2) + more
            gmi_acc[...] = gmore
        else:
            out_acc[...] = out_acc[...] + more
            gmi_acc[...] = gmi_acc[...] + gmore
    out_o[...] = out_acc[...].astype(BF)
    gmi = gmi_acc[...]
    sums_o[1:2, :] = colsum(gmi * xhat)
    sums_o[2:3, :] = colsum(gmi)
    grad_middle = grad_out + norm_back(gmi, xhat, rstd, gain)
    gm_o[...] = grad_middle
    branch = grad_middle.astype(BF)
    gb_o[...] = branch
    sums_o[0:1, :] = colsum(branch.astype(F32))
    gctx = nt(gb_o[...], wo[...]).astype(BF)
    pay_o[:count, :] = gctx
    prod = pieces(gctx.astype(F32) * context, 3)
    head = width // HEADS

    def is_head(shape, feature, number):
        feature, number = (lax.broadcasted_iota(jnp.int32, shape, n) for n in (feature, number))
        return jnp.where(feature // head == number, 1.0, 0.0).astype(BF)

    onehot, onehot_t = is_head((width, 128), 0, 1), is_head((16, width), 1, 0)
    eye = lax.broadcasted_iota(jnp.int32, (16, 128), 0) == lax.broadcasted_iota(jnp.int32, (16, 128), 1)
    eye = jnp.where(eye, 1.0, 0.0).astype(BF)
    dlt_o[...] = nn(prod[0], onehot) + nn(prod[1], onehot) + nn(prod[2], onehot)
    across = nt(onehot_t, prod[0]) + nt(onehot_t, prod[1]) + nt(onehot_t, prod[2])
    pay_o[count:, :] = jnp.zeros((48, width), BF)
    lse_t = [nt(eye, part)[:8].astype(BF) for part in pieces(lse[...], 3)]
    pay_o[count : count + 24, :count] = jnp.concatenate(lse_t, axis=0)
    pay_o[count + 24 : count + 48, :count] = jnp.concatenate(pieces(across[:8], 3), axis=0)


def by_lanes(out, value):
    for n in range(out.shape[0]):
        out[n, : value.shape[0], :] = value[:, n * 128 : (n + 1) * 128].astype(BF)


def mlp_weights_kernel(core, act, dy, mi, ghp, ctx, gb, send_o, keep_o):
    step = pl.program_id(0)
    per = pl.num_programs(0) // 2
    sending = step < per
    first = jnp.where(sending, 1 - core[0], core[0]) == 0
    j = step % per

    def put(wanted, left, right):
        @pl.when(wanted & sending)
        def _():
            by_lanes(send_o, tn(left[...], right[...]))

        @pl.when(wanted & jnp.logical_not(sending))
        def _():
            by_lanes(keep_o, tn(left[...], right[...]))

    put((j < per - 1) & first, act, dy)
    put((j < per - 1) & jnp.logical_not(first), mi, ghp)
    put(j == per - 1, ctx, gb)


def attn_weights_kernel(ain, gp, out_o):
    by_lanes(out_o, tn(ain[...], gp[...]))


def stem_back_kernel(gsp, left, right, vw, act, dstem, x, pack, sums1, sums2, gpre, stride_o, ends_o, g, gext, gup, stem):
    count, width = gsp.shape
    ext = gext.shape[0]
    inner = slice(PAD, PAD + count)
    even, odd = slice(0, width), slice(width, 2 * width)
    g[...] = jnp.zeros_like(g)
    g[inner, :] = gsp[...].astype(F32)
    g[PAD - 1 : PAD, :] = left[...].astype(F32)
    g[PAD + count : PAD + count + 1, :] = right[...].astype(F32)
    gext[...] = g[:ext, :].astype(BF)
    gup[...] = (g[1 : ext + 1, :] * pack[:, 1:2]).astype(BF)
    gpre[:, even] = (nt(gext[...], vw[width : 2 * width, :]) * dstem[:, even]).astype(BF)
    grad_odd = nt(gext[...], vw[2 * width :, :]) + nt(gup[...], vw[:width, :])
    gpre[:, odd] = (grad_odd * dstem[:, odd]).astype(BF)
    row = lax.broadcasted_iota(jnp.int32, (ext, width), 0)
    gup[...] = jnp.where(row < PAD + count - 1, gup[...].astype(F32), 0.0).astype(BF)
    lanes = width // 128
    by_lanes(stride_o.at[0:lanes], tn(act[:, odd], gup[...]))
    by_lanes(stride_o.at[lanes : 2 * lanes], tn(act[inner, even], gsp[...]))
    by_lanes(stride_o.at[2 * lanes :], tn(act[inner, odd], gsp[...]))
    taps = tn(x[inner, : 3 * SLOT], gpre[inner, even]) + tn(x[inner, SLOT:], gpre[inner, odd])
    mels = (stem.shape[0] - 16) // 3
    for t in range(3):
        stem[t * mels : (t + 1) * mels, :] = taps[t * SLOT : t * SLOT + mels, :]
    stem_sum = colsum(gpre[inner, even].astype(F32)) + colsum(gpre[inner, odd].astype(F32))
    stride_sum = colsum(gsp[...].astype(F32))
    rows = [stem_sum, stride_sum, sums2[0:4, :], sums1[...], jnp.zeros((2, width), F32)]
    stem[3 * mels :, :] = jnp.concatenate(rows, axis=0)
    half = stem.shape[0] // 2
    for n in range(2):
        by_lanes(ends_o.at[n], stem[n * half : (n + 1) * half, :])


def mel_kernel(gpre, sw, pack, mel_o, wbig, gx):
    count = mel_o.shape[0] // 2
    mels = mel_o.shape[1]
    inner = slice(PAD, PAD + count)
    taps_of(wbig, sw)
    gx[...] = nt(gpre[...], wbig[...])
    on_even = gx[inner, SLOT : 2 * SLOT] + pack[inner, 0:1] * gx[PAD - 1 : PAD + count - 1, 3 * SLOT :]
    on_odd = gx[inner, 2 * SLOT : 3 * SLOT] + pack[inner, 1:2] * gx[PAD + 1 : PAD + count + 1, :SLOT]
    mel_o[pl.ds(0, count, stride=2), :] = on_even[:, :mels]
    mel_o[pl.ds(1, count, stride=2), :] = on_odd[:, :mels]


def merge_kernel(core, attn, attn_pair, stride, stride_pair, ends, ends_pair, out_o):
    blocks, rows, _ = attn.shape

    def put(a, b):
        for n in range(blocks):
            out_o[n * rows : (n + 1) * rows, :] = (a[n].astype(F32) + b[n].astype(F32)).astype(BF)

    @pl.when(core[0] == 0)
    def _():
        put(attn, attn_pair)

    @pl.when(core[0] != 0)
    def _():
        put(stride, stride_pair)

    few = ends.shape[2]
    for n in range(ends.shape[1]):
        at = blocks * rows + n * few
        out_o[at : at + few, :] = (ends[core[0], n].astype(F32) + ends_pair[core[0], n].astype(F32)).astype(BF)


def spread_kernel(parts, out_o):
    total = parts[0].astype(F32)
    for n in range(1, parts.shape[0]):
        total = total + parts[n].astype(F32)
    total = total.astype(BF)
    for n in range(parts.shape[0]):
        out_o[n] = total


def unpack_kernel(core, mine, theirs, attn_o, stride_o, stem_o, *rest):
    vectors, ends = rest[:-1], rest[-1]
    rows, width = stride_o.shape
    lanes = width // 128
    few = ends.shape[0] // 2

    def put(first, second):
        for b in range(rows // width):
            for n in range(lanes):
                at = slice((b * lanes + n) * width, (b * lanes + n + 1) * width)
                cols = slice(n * 128, (n + 1) * 128)
                attn_o[:, b * width + n * 128 : b * width + (n + 1) * 128] = first[at, :].astype(F32)
                stride_o[b * width : (b + 1) * width, cols] = second[at, :].astype(F32)
        for h, part in enumerate((first, second)):
            for n in range(lanes):
                at = rows * lanes + n * few
                ends[h * few : (h + 1) * few, n * 128 : (n + 1) * 128] = part[at : at + few, :].astype(F32)

    @pl.when(core[0] == 0)
    def _():
        put(mine, theirs)

    @pl.when(core[0] != 0)
    def _():
        put(theirs, mine)

    mels = stem_o.shape[0]
    stem_o[...] = ends[:mels, :]
    row = mels
    for out in vectors:
        for n in range(out.shape[0] // width):
            out[n * width : (n + 1) * width] = ends[row + n : row + n + 1, :].reshape(width)
        row += out.shape[0] // width


def after(value, *others):
    return lax.optimization_barrier((value, *others))[0]


def move(block, distance):
    count = lax.axis_size("frames")
    return lax.ppermute(block, "frames", [(d, (d + distance) % count) for d in range(count)])


def swap(block):
    count = lax.axis_size("frames")
    return lax.ppermute(block, "frames", [(d, d ^ 1) for d in range(count)])


def cost(us):
    return pl.CostEstimate(flops=int(us * 1.1e9), bytes_accessed=int(us * 2e6), transcendentals=0)


def call(kernel, outs, args, scratch=(), specs=None, limit=56, us=10):
    vmem = pl.BlockSpec(memory_space=pltpu.VMEM)
    return pl.pallas_call(
        kernel,
        out_shape=[jax.ShapeDtypeStruct(s, d) for s, d in outs],
        in_specs=specs if specs is not None else [vmem] * len(args),
        out_specs=[vmem] * len(outs),
        scratch_shapes=list(scratch),
        compiler_params=pltpu.CompilerParams(vmem_limit_bytes=limit * MIB),
        cost_estimate=cost(us),
    )(*args)


def chip_groups():
    chips = lax.axis_size("frames") // 2
    return [[2 * n + core for n in range(chips)] for core in range(2)]


def scatter_sum(both, beside):
    chips = lax.axis_size("frames") // 2
    parts = both.reshape(chips, both.shape[0] // chips, 128)
    parts = lax.all_to_all(parts, "frames", 0, 0, axis_index_groups=chip_groups(), tiled=True)
    return jnp.sum(after(parts, beside).astype(F32), axis=0).astype(BF)


def add(a, b):
    return (a.astype(F32) + b.astype(F32)).astype(BF)


def unlanes(x):
    return jnp.concatenate([x[n] for n in range(x.shape[0])], axis=1)


def local(
    mel_frames, clip_lengths, valid_keys, stem_weight, stem_bias, stride_weight, stride_bias, attn_gain, attn_shift,
    attn_weight, query_bias, value_bias, output_weight, output_bias, mlp_gain, mlp_shift, hidden_weight, hidden_bias,
    return_weight, return_bias, cotangent,
):
    count, width = cotangent.shape
    ff = hidden_weight.shape[1]
    mels = mel_frames.shape[1]
    devices = lax.axis_size("frames")
    device = lax.axis_index("frames")
    core = device % 2
    nb = 2 * SIDE + 1
    ext = count + 2 * PAD
    base = (device - core - 2 * SIDE) * count

    left, right = move(mel_frames[-2:], 1), move(mel_frames[:2], -1)

    smem = pl.BlockSpec(memory_space=pltpu.SMEM)
    vmem = pl.BlockSpec(memory_space=pltpu.VMEM)
    hbm = pl.BlockSpec(memory_space=pl.ANY)
    whole = pltpu.VMEM((count, 128), jnp.int32)
    spans, pack, table, key_plan, query_plan = pl.pallas_call(
        functools.partial(tables_kernel, total=devices * count),
        out_shape=[
            jax.ShapeDtypeStruct(s, d)
            for s, d in (
                ((count, 128), jnp.int32), ((ext, 128), F32), ((count, width), F32), ((16,), jnp.int32), ((16,), jnp.int32)
            )
        ],
        in_specs=[smem] * 3,
        out_specs=[vmem] * 3 + [smem] * 2,
        scratch_shapes=[whole] * 3,
        cost_estimate=cost(4),
    )(device[None].astype(jnp.int32), clip_lengths, valid_keys)

    x, act, dstem, dstride, layer_in, attn_in = call(
        stem_kernel,
        [
            ((ext, 4 * SLOT), BF), ((ext, 2 * width), BF), ((ext, 2 * width), F32), ((count, width), F32), ((count, width), F32),
            ((count, width), BF),
        ],
        (
            mel_frames, left, right, stem_weight, stem_bias, stride_weight, stride_bias, attn_gain, attn_shift, pack, table,
        ),
        [pltpu.VMEM((2 * ext + 16, SLOT), F32), pltpu.VMEM((4 * SLOT, 2 * width), BF), pltpu.VMEM((ext, width), F32)],
        us=7,
    )

    joint = jnp.concatenate([query_bias.astype(F32), jnp.zeros((width,), F32), value_bias.astype(F32)])

    def project(block):
        return (nn(block, attn_weight) + joint).astype(BF)

    def gather(block, on_hop, on_block):
        own, sib = {0: block}, {0: swap(block)}
        ends = block, block
        done = [on_block(own[0], ()), on_block(sib[0], ())]
        out_own, out_sib = {0: done[0]}, {0: done[1]}
        for k in range(1, SIDE + 1):
            ends = on_hop(k, move(ends[0], 2), move(ends[1], -2))
            for n, b in zip((-k, k), ends):
                own[n], sib[n] = b, swap(b)
            for n in (-k, k):
                out_own[n] = on_block(own[n], done if k == SIDE else ())
            for n in (-k, k):
                out_sib[n] = on_block(sib[n], [out_own[-k], out_own[k]] if k == SIDE else ())
            done += [out[n] for out in (out_own, out_sib) for n in (-k, k)]
        order = range(-SIDE, SIDE + 1)
        return [out_own[n] for n in order], [out_sib[n] for n in order]

    own, sib = gather(
        attn_in, lambda k, left, right: (left, right), lambda b, first: project(after(b, *first) if first else b)
    )

    reach = 2 * nb * count + KB
    pairs = width // 128
    sems = pltpu.SemaphoreType.DMA((2 * nb, 2))
    count_of = pltpu.SMEM((1,), jnp.int32)

    stacked = pltpu.VMEM((pairs, 2 * QB, 128), BF)
    summed = pltpu.VMEM((pairs, 2 * QB, 128), F32)
    score = pltpu.VMEM((2, pairs, 2 * QB, KB), F32)
    weight = pltpu.VMEM((2, pairs, 2 * QB, KB), BF)
    one_sem = pltpu.SemaphoreType.DMA((1,))
    local_query = pltpu.VMEM((count, width), BF)

    ctx, lse = call(
        forward_kernel,
        [((count, width), F32), ((count, 128), F32)],
        (key_plan, spans, *own, *sib),
        [
            local_query, pltpu.VMEM((reach, 2 * width), BF), stacked, summed, summed, summed, summed, score, weight, count_of,
            sems, one_sem,
        ],
        [smem, vmem] + [hbm] * (2 * nb),
        us=15,
    )

    layer_out, hidden_act, ghp, mlp_in, grad_middle, branch, ctx_b, pay, dlt, sums1 = call(
        mlp_kernel,
        [
            ((count, width), BF), ((count, ff), BF), ((count, ff), BF), ((count, width), BF), ((count, width), F32),
            ((count, width), BF), ((count, width), BF), ((count + 48, width), BF), ((count, 128), F32), ((8, width), F32),
        ],
        (
            ctx, layer_in, cotangent, lse, output_weight, hidden_weight, return_weight, output_bias, hidden_bias, return_bias,
            mlp_gain, mlp_shift,
        ),
        [pltpu.VMEM((count, width), F32), pltpu.VMEM((count, width), F32)],
        us=11,
    )

    core1 = core[None].astype(jnp.int32)
    part = width
    per = ff // part + 1
    rows = per * part

    def half_of(i, core):
        return jnp.where(i < per, 1 - core[0], core[0])

    def by_column(i, core):
        return (0, jnp.minimum(i % per, per - 2))

    def fixed(i, core):
        return (0, 0)

    send, keep = pl.pallas_call(
        mlp_weights_kernel,
        out_shape=[jax.ShapeDtypeStruct((pairs, rows, 128), BF)] * 2,
        grid_spec=pltpu.PrefetchScalarGridSpec(
            num_scalar_prefetch=1,
            grid=(2 * per,),
            in_specs=[
                pl.BlockSpec((count, part), by_column),
                pl.BlockSpec((count, width), fixed),
                pl.BlockSpec((count, width), fixed),
                pl.BlockSpec((count, part), by_column),
                pl.BlockSpec((count, width // 2), lambda i, core: (0, half_of(i, core))),
                pl.BlockSpec((count, width), fixed),
            ],
            out_specs=[
                pl.BlockSpec((pairs, part, 128), lambda i, core: (0, jnp.minimum(i, per - 1), 0)),
                pl.BlockSpec((pairs, part, 128), lambda i, core: (0, jnp.maximum(i - per, 0), 0)),
            ],
        ),
        compiler_params=pltpu.CompilerParams(vmem_limit_bytes=40 * MIB),
        cost_estimate=cost(7),
    )(core1, hidden_act, cotangent, mlp_in, ghp, ctx_b, branch)

    first_hop = []

    def on_hop(k, left, right):
        if k == 1:
            left, right = after(left, right, send), after(right, left, send)
            first_hop.extend((left, right))
        return left, right

    own_pay, sib_pay = gather(pay, on_hop, lambda b, first: b)
    (grad_query,) = call(
        query_kernel,
        [((count, width), BF)],
        (key_plan, after(spans, *first_hop), pay, lse, dlt, *own, *sib),
        [
            local_query, pltpu.VMEM((reach, 2 * width), BF), stacked, stacked, summed, summed, summed, score, score, weight,
            count_of, sems, one_sem,
        ],
        [smem] + [vmem] * 4 + [hbm] * (2 * nb),
        us=15,
    )

    mlp_both = add(keep, after(swap(send), grad_query)).reshape(-1, 128)
    mlp_both = after(mlp_both, own_pay, sib_pay)

    grad_projected, gsp, sums2 = call(
        key_kernel,
        [((count, 3 * width), BF), ((count, width), BF), ((8, width), F32)],
        (
            query_plan, spans, after(grad_query, mlp_both), attn_weight, layer_in, grad_middle, attn_gain,
            dstride, *own, *sib, *own_pay, *sib_pay,
        ),
        [
            pltpu.VMEM((count, 2 * width), BF), pltpu.VMEM((reach, width), BF), pltpu.VMEM((reach, width), BF),
            pltpu.VMEM((48, reach), BF), pltpu.VMEM((8, reach), F32), pltpu.VMEM((8, reach), F32), stacked, stacked, summed, summed, score, score, weight,
            weight, count_of, sems, pltpu.SemaphoreType.DMA((2 * nb, 1)),
            one_sem,
        ],
        [smem] + [vmem] * 7 + [hbm] * (4 * nb),
        us=18,
    )
    mlp_share = scatter_sum(mlp_both, gsp)

    left, right = move(gsp[-1:], 1), move(gsp[:1], -1)
    attn_rows = pl.pallas_call(
        attn_weights_kernel,
        out_shape=jax.ShapeDtypeStruct((3 * pairs, width, 128), BF),
        grid=(3,),
        in_specs=[pl.BlockSpec((count, width), lambda i: (0, 0)), pl.BlockSpec((count, width), lambda i: (0, i))],
        out_specs=pl.BlockSpec((pairs, width, 128), lambda i: (i, 0, 0)),
        compiler_params=pltpu.CompilerParams(vmem_limit_bytes=40 * MIB),
        cost_estimate=cost(3),
    )(attn_in, grad_projected)
    attn_in_pair = lax.ppermute(attn_rows, "frames", [(d + 1, d) for d in range(0, devices, 2)])

    gpre, stride_rows, ends = call(
        stem_back_kernel,
        [((ext, 2 * width), BF), ((3 * pairs, width, 128), BF), ((2, pairs, (3 * mels + 16) // 2, 128), BF)],
        (gsp, left, right, stride_weight, act, dstem, x, pack, sums1, sums2),
        [
            pltpu.VMEM((ext + 8, width), F32), pltpu.VMEM((ext, width), BF), pltpu.VMEM((ext, width), BF),
            pltpu.VMEM((3 * mels + 16, width), F32),
        ],
        us=6,
    )
    stride_in_pair = lax.ppermute(stride_rows, "frames", [(d, d + 1) for d in range(0, devices, 2)])
    both_rows = 6 * width * pairs // 2 + ends.shape[2] * pairs
    (both,) = call(
        merge_kernel,
        [((both_rows, 128), BF)],
        (core1, attn_rows, attn_in_pair, stride_rows, stride_in_pair, ends, swap(ends)),
        specs=[smem] + [vmem] * 6,
        us=3,
    )

    (mel_grad,) = call(
        mel_kernel,
        [((2 * count, mels), F32)],
        (after(gpre, both), stem_weight, pack),
        [pltpu.VMEM((4 * SLOT, 2 * width), BF), pltpu.VMEM((ext, 4 * SLOT), F32)],
        us=3,
    )

    chips = devices // 2
    parts = both.reshape(chips, both_rows // chips, 128)
    parts = lax.all_to_all(parts, "frames", 0, 0, axis_index_groups=chip_groups(), tiled=True)
    (spread,) = call(spread_kernel, [(parts.shape, BF)], (after(parts, mel_grad),), us=2)
    mine = lax.all_to_all(spread, "frames", 0, 0, axis_index_groups=chip_groups(), tiled=True).reshape(-1, 128)

    every = lax.all_gather(mlp_share, "frames", axis=0, tiled=False)
    every = after(every, spread).reshape(chips, 2, -1, 128)
    first, second = (every[:, n].reshape(pairs, rows, 128) for n in range(2))
    grad_return_weight = unlanes(first[:, :ff]).astype(F32)
    grad_hidden_weight = jnp.concatenate(
        [unlanes(second[:, b * width : (b + 1) * width]) for b in range(ff // width)], axis=1
    ).astype(F32)
    half = slice(ff, ff + width // 2)
    grad_output_weight = jnp.concatenate([unlanes(first[:, half]), unlanes(second[:, half])], axis=0).astype(F32)

    mine = after(mine, grad_return_weight, grad_hidden_weight, grad_output_weight)
    sizes = [width] * 9 + [ff, width]
    grad_attn_weight, grad_stride_weight, grad_stem_weight, *bias = call(
        unpack_kernel,
        [((width, 3 * width), F32), ((3 * width, width), F32), ((3 * mels, width), F32)] + [((n,), F32) for n in sizes],
        (core1, mine, swap(mine)),
        [pltpu.VMEM((3 * mels + 16, width), F32)],
        [smem, vmem, vmem],
        us=4,
    )
    return (
        layer_out, mel_grad, grad_stem_weight, bias[0], grad_stride_weight, bias[1], bias[2], bias[3], grad_attn_weight,
        bias[4], bias[5], grad_output_weight, bias[6], bias[7], bias[8], grad_hidden_weight, bias[9],
        grad_return_weight, bias[10],
    )


def solution(mesh):
    split = P("frames", None)
    in_specs = (split,) + (P(),) * 19 + (split,)
    out_specs = (split, split) + (P(),) * 17
    return jax.shard_map(local, mesh=mesh, in_specs=in_specs, out_specs=out_specs, check_vma=False)
```

```python
import functools
import math

import jax
import jax.numpy as jnp
from jax import lax
from jax.experimental import pallas as pl
from jax.experimental.pallas import tpu as pltpu
from jax.sharding import PartitionSpec as P

HEADS = 8
SIDE = 2
QB = 128
KB = 256
PAD = 16
SLOT = 128
NEG = -1e30
BF = jnp.bfloat16
F32 = jnp.float32
MIB = 1 << 20


def nn(a, b):
    return lax.dot_general(a, b, (((1,), (0,)), ((), ())), preferred_element_type=F32)


def nt(a, b):
    return lax.dot_general(a, b, (((1,), (1,)), ((), ())), preferred_element_type=F32)


def tn(a, b):
    return lax.dot_general(a, b, (((0,), (0,)), ((), ())), preferred_element_type=F32)


def gelu_pair(x):
    bell = jnp.exp(-0.5 * x * x)
    t = 1.0 / (1.0 + 0.2316419 * jnp.abs(x))
    poly = 0.127414796 + t * (-0.142248368 + t * (0.7107068705 + t * (-0.7265760135 + t * 0.5307027145)))
    tail = bell * t * poly
    phi = jnp.where(x >= 0, 1.0 - tail, tail)
    return x * phi, phi + 0.3989422804 * x * bell


def norm_parts(x):
    center = jnp.mean(x, axis=-1, keepdims=True)
    centered = x - center
    rstd = lax.rsqrt(jnp.mean(centered * centered, axis=-1, keepdims=True) + 1e-05)
    return centered * rstd, rstd


def norm_back(grad, xhat, rstd, gain):
    inner = grad * gain
    m1 = jnp.mean(inner, axis=-1, keepdims=True)
    m2 = jnp.mean(inner * xhat, axis=-1, keepdims=True)
    return rstd * (inner - m1 - xhat * m2)


def vector(ref):
    return ref[...].astype(F32).reshape(1, -1)


def colsum(x):
    return jnp.sum(x, axis=0, keepdims=True)


def halves(x, low):
    zero = jnp.zeros_like(x)
    return jnp.concatenate([jnp.where(low, x, zero), jnp.where(low, zero, x)], axis=0)


def pick(x, low):
    return jnp.where(low, x[:QB], x[QB:])


def wide(x):
    return jnp.concatenate([x, x], axis=1)


def tall(x):
    return jnp.concatenate([x, x], axis=0)


def tables_kernel(device, lengths, valids, spans_o, pack_o, table_o, keys_o, queries_o, start_s, length_s, valid_s, *, total):
    count, width = table_o.shape
    base = (device[0] - device[0] % 2 - 2 * SIDE) * count
    first = device[0] * count
    token = first + lax.broadcasted_iota(jnp.int32, (count, 128), 0)
    row = lax.broadcasted_iota(jnp.int32, pack_o.shape, 0) + lax.broadcasted_iota(jnp.int32, pack_o.shape, 1) - PAD
    here = (row >= 0) & (row <= count) & (first + row < total)
    pack_o[...] = jnp.where(here, 1.0, 0.0)
    keys_o[0] = queries_o[0] = device[0] % 2

    def clip(c, start):
        length = lengths[c]
        valid = jnp.minimum(valids[c], length)
        end = start + length

        @pl.when((start < first + count) & (end > first))
        def _():
            inside = (token >= start) & (token < end)
            start_s[...] = jnp.where(inside, start, start_s[...])
            length_s[...] = jnp.where(inside, length, length_s[...])
            valid_s[...] = jnp.where(inside, valid, valid_s[...])
            for n in range(count // QB):
                at = first + n * QB

                @pl.when((start <= at) & (at < end))
                def _():
                    keys_o[4 + 2 * n] = queries_o[4 + 2 * n] = ((start - base) >> 7) << 7

                @pl.when((start < at + QB) & (at + QB <= end))
                def _():
                    keys_o[5 + 2 * n] = start + valid - base
                    queries_o[5 + 2 * n] = end - base

        @pl.when((start >= first) & (start <= first + count))
        def _():
            pack_o[...] = jnp.where(first + row == start, 0.0, pack_o[...])

        return end

    lax.fori_loop(0, lengths.shape[0], clip, 0)
    for plan in (keys_o, queries_o):
        low, high = plan[4], 0
        for n in range(count // QB):
            steps = (plan[5 + 2 * n] - plan[4 + 2 * n] + KB - 1) // KB
            plan[5 + 2 * n] = steps
            low = jnp.minimum(low, plan[4 + 2 * n])
            high = jnp.maximum(high, plan[4 + 2 * n] + steps * KB)
        plan[1], plan[2] = low, high
    lane = lax.broadcasted_iota(jnp.int32, (count, 128), 1)
    key_lo = start_s[...] - base
    position = token - start_s[...]
    is_key = position < valid_s[...]
    query_lo = jnp.where(is_key, key_lo, 1 << 20)
    query_hi = jnp.where(is_key, key_lo + length_s[...], 0)
    first_two = jnp.where(lane == 0, key_lo, key_lo + valid_s[...])
    spans_o[...] = jnp.where(lane < 2, first_two, jnp.where(lane == 2, query_lo, query_hi))
    half = width // 2
    number = lax.broadcasted_iota(jnp.int32, (1, half), 1).astype(F32)
    rates = jnp.exp(number * (-math.log(10000.0) / (half - 1)))
    angles = wide(position.astype(F32)) * rates
    table_o[:, :half] = jnp.sin(angles)
    table_o[:, half:] = jnp.cos(angles)


def taps_of(wbig, sw):
    mels, width = sw.shape[0] // 3, sw.shape[1]
    wbig[...] = jnp.zeros_like(wbig)
    for t in range(3):
        tap = sw[t * mels : (t + 1) * mels, :]
        wbig[t * SLOT : t * SLOT + mels, :width] = tap
        wbig[(t + 1) * SLOT : (t + 1) * SLOT + mels, width:] = tap


def stem_kernel(
    mel, left, right, sw, sbias, vw, vbias, gain, shift, pack, table,
    x_o, cols_o, dstem_o, dstride_o, lin_o, ain_o, m, wbig, shifted,
):
    count, width = lin_o.shape
    frames, mels = mel.shape
    ext = x_o.shape[0]
    taps_of(wbig, sw)
    top = 2 * PAD + 8
    m[...] = jnp.zeros_like(m)
    m[top : top + frames, :mels] = mel[...].astype(F32)
    m[top - 2 : top, :mels] = left[...].astype(F32)
    m[top + frames : top + frames + 2, :mels] = right[...].astype(F32)
    opn, opn_next = pack[:, 0:1], pack[:, 1:2]
    x_o[:, :SLOT] = (m[pl.ds(7, ext, stride=2), :] * opn).astype(BF)
    x_o[:, SLOT : 2 * SLOT] = m[pl.ds(8, ext, stride=2), :].astype(BF)
    x_o[:, 2 * SLOT : 3 * SLOT] = m[pl.ds(9, ext, stride=2), :].astype(BF)
    x_o[:, 3 * SLOT :] = (m[pl.ds(10, ext, stride=2), :] * opn_next).astype(BF)
    inner = slice(PAD, PAD + count)
    even, odd = slice(0, width), slice(width, 2 * width)
    act, dact = gelu_pair(nn(x_o[...], wbig[:, even]) + vector(sbias))
    dstem_o[:, even] = dact
    cols_o[:, width : 2 * width] = act[inner].astype(BF)
    act, dact = gelu_pair(nn(x_o[...], wbig[:, odd]) + vector(sbias))
    dstem_o[:, odd] = dact
    cols_o[:, 2 * width :] = act[inner].astype(BF)
    shifted[...] = act
    cols_o[:, :width] = (shifted[PAD - 1 : PAD + count - 1, :] * pack[inner, 0:1]).astype(BF)
    pre = nn(cols_o[...], vw[...]) + vector(vbias)
    act2, dact2 = gelu_pair(pre)
    dstride_o[...] = dact2
    lin = act2 + table[...]
    lin_o[...] = lin
    xhat, _ = norm_parts(lin)
    ain_o[...] = (xhat * vector(gain) + vector(shift)).astype(BF)


def needed(sc, block, count):
    return (block * count < sc[2]) & ((block + 1) * count > sc[1])


def start_copies(sc, pairs, sem, count):
    for block, copies in pairs:
        @pl.when(needed(sc, block, count))
        def _():
            for m, (src, dst) in enumerate(copies):
                pltpu.make_async_copy(src, dst, sem.at[block, m]).start()


def wait_until(sc, end, copies, sem, count, there):
    def one(block, _):
        @pl.when(needed(sc, block, count))
        def _():
            for m, (src, dst) in enumerate(copies(block)):
                pltpu.make_async_copy(src, dst, sem.at[block, m]).wait()

        return 0

    upto = jnp.minimum((end + count - 1) // count, 2 * (2 * SIDE + 1))
    lax.fori_loop(there[0], upto, one, 0)
    there[0] = jnp.maximum(there[0], upto)


def window(sc, own, sib):
    core = sc[0]
    out = []
    for k in range(2 * SIDE + 1):
        out += [(2 * k + core, own[k]), (2 * k + 1 - core, sib[k])]
    return out


def rows_of(block, count):
    return pl.ds(pl.multiple_of(block * count, count), count)


def in_range(lo, hi, start):
    col = start + lax.broadcasted_iota(jnp.int32, (QB, KB), 1)
    return jnp.where((col >= lo) & (col < hi), 0.0, NEG)


def chunks(first, steps, step, wait):
    def two(n, _):
        wait(first + (2 * n + 2) * KB)
        step(2 * n, 2)
        return 0

    lax.fori_loop(0, steps // 2, two, 0)

    @pl.when(steps % 2 == 1)
    def _():
        wait(first + steps * KB)
        step(steps - 1, 1)


def forward_kernel(*refs):
    nb = 2 * SIDE + 1
    sc, span_ref = refs[:2]
    own, sib = refs[2 : 2 + nb], refs[2 + nb : 2 + 2 * nb]
    ctx_o, lse_o, local_ref, kv, q2, acc, peak, total, scale, s, e, there, sem, sem2 = refs[2 + 2 * nb :]
    count, width = ctx_o.shape
    span = 2 * nb * count
    pairs = width // 128
    kv[span:, :] = jnp.zeros((kv.shape[0] - span, 2 * width), BF)
    there[0] = 0

    def copies(block, src=own[0]):
        return [(src.at[:, pl.ds(width, 2 * width)], kv.at[rows_of(block, count), :])]

    local = pltpu.make_async_copy(own[SIDE].at[:, pl.ds(0, width)], local_ref, sem2.at[0])
    local.start()
    start_copies(sc, [(block, copies(block, src)) for block, src in window(sc, own, sib)], sem, count)
    local.wait()

    def wait(end):
        wait_until(sc, end, copies, sem, count, there)

    low = lax.broadcasted_iota(jnp.int32, (QB, 128), 1) < 64
    lanes = lax.broadcasted_iota(jnp.int32, (QB, 128), 1)

    def one(i, _):
        rows = pl.ds(pl.multiple_of(i * QB, QB), QB)
        for p in range(pairs):
            q2[p] = halves(local_ref[rows, p * 128 : (p + 1) * 128], low) * jnp.asarray(0.125, BF)
            acc[p] = jnp.zeros_like(acc[p])
            peak[p] = jnp.full_like(peak[p], NEG)
            total[p] = jnp.zeros_like(total[p])
        lo, hi = span_ref[rows, 0:1], span_ref[rows, 1:2]

        def step(n, parts):
            start = sc[4 + 2 * i] + n * KB
            keys = [pl.ds(pl.multiple_of(start + u * KB, 128), KB) for u in range(parts)]
            for u in range(parts):
                bias = tall(in_range(lo, hi, start + u * KB))
                for p in range(pairs):
                    s[u, p] = nt(q2[p], kv[keys[u], p * 128 : (p + 1) * 128]) + bias
            for p in range(pairs):
                best = functools.reduce(jnp.maximum, [s[u, p] for u in range(parts)])
                old = peak[p]
                top = jnp.maximum(old, jnp.max(best, axis=1, keepdims=True))
                peak[p] = top
                scale[p] = jnp.exp(old - top)
            for p in range(pairs):
                total[p] = scale[p] * total[p]
                for u in range(parts):
                    grown = jnp.exp(s[u, p] - wide(peak[p]))
                    e[u, p] = grown.astype(BF)
                    total[p] = total[p] + (grown[:, :128] + grown[:, 128:])
            for p in range(pairs):
                value = [kv[keys[u], width + p * 128 : width + (p + 1) * 128] for u in range(parts)]
                acc[p] = scale[p] * acc[p] + functools.reduce(jnp.add, [nn(e[u, p], value[u]) for u in range(parts)])

        chunks(sc[4 + 2 * i], sc[5 + 2 * i], step, wait)
        lse = jnp.zeros((QB, 128), F32)
        for p in range(pairs):
            row_total = jnp.sum(total[p], axis=1, keepdims=True)
            ctx_o[rows, p * 128 : (p + 1) * 128] = pick(acc[p] / row_total, low)
            both = peak[p] + jnp.log(row_total)
            lse = jnp.where(lanes == 2 * p, both[:QB], lse)
            lse = jnp.where(lanes == 2 * p + 1, both[QB:], lse)
        lse_o[rows, :] = lse
        return 0

    lax.fori_loop(0, count // QB, one, 0)
    wait(span)


def query_kernel(*refs):
    nb = 2 * SIDE + 1
    sc, span_ref, pay_ref, lse_ref, dlt_ref = refs[:5]
    own, sib = refs[5 : 5 + nb], refs[5 + nb : 5 + 2 * nb]
    dq_o, local_ref, kv, q2, do2, acc, lse2, dlt2, s, d, ds, there, sem, sem2 = refs[5 + 2 * nb :]
    count, width = dq_o.shape
    span = 2 * nb * count
    pairs = width // 128
    kv[span:, :] = jnp.zeros((kv.shape[0] - span, 2 * width), BF)
    there[0] = 0

    def copies(block, src=own[0]):
        return [(src.at[:, pl.ds(width, 2 * width)], kv.at[rows_of(block, count), :])]

    local = pltpu.make_async_copy(own[SIDE].at[:, pl.ds(0, width)], local_ref, sem2.at[0])
    local.start()
    start_copies(sc, [(block, copies(block, src)) for block, src in window(sc, own, sib)], sem, count)
    local.wait()

    def wait(end):
        wait_until(sc, end, copies, sem, count, there)

    low = lax.broadcasted_iota(jnp.int32, (QB, 128), 1) < 64

    def one(i, _):
        rows = pl.ds(pl.multiple_of(i * QB, QB), QB)
        lse, dlt = lse_ref[rows, :], dlt_ref[rows, :]
        for p in range(pairs):
            q2[p] = halves(local_ref[rows, p * 128 : (p + 1) * 128], low) * jnp.asarray(0.125, BF)
            do2[p] = halves(pay_ref[rows, p * 128 : (p + 1) * 128], low)
            acc[p] = jnp.zeros_like(acc[p])
            for h in range(2):
                part = pl.ds(h * QB, QB)
                lse2[p, part, :] = jnp.broadcast_to(lse[:, 2 * p + h : 2 * p + h + 1], (QB, 128))
                dlt2[p, part, :] = jnp.broadcast_to(dlt[:, 2 * p + h : 2 * p + h + 1], (QB, 128))
        lo, hi = span_ref[rows, 0:1], span_ref[rows, 1:2]

        def step(n, parts):
            start = sc[4 + 2 * i] + n * KB
            keys = [pl.ds(pl.multiple_of(start + u * KB, 128), KB) for u in range(parts)]
            for u in range(parts):
                bias = tall(in_range(lo, hi, start + u * KB))
                for p in range(pairs):
                    s[u, p] = nt(q2[p], kv[keys[u], p * 128 : (p + 1) * 128]) + bias
                    d[u, p] = nt(do2[p], kv[keys[u], width + p * 128 : width + (p + 1) * 128])
            for u in range(parts):
                for p in range(pairs):
                    e = jnp.exp(s[u, p] - wide(lse2[p]))
                    ds[u, p] = (e * (d[u, p] - wide(dlt2[p]))).astype(BF)
            for p in range(pairs):
                more = [nn(ds[u, p], kv[keys[u], p * 128 : (p + 1) * 128]) for u in range(parts)]
                acc[p] = acc[p] + functools.reduce(jnp.add, more)

        chunks(sc[4 + 2 * i], sc[5 + 2 * i], step, wait)
        for p in range(pairs):
            dq_o[rows, p * 128 : (p + 1) * 128] = (pick(acc[p], low) * 0.125).astype(BF)
        return 0

    lax.fori_loop(0, count // QB, one, 0)
    wait(span)


def key_kernel(*refs):
    nb = 2 * SIDE + 1
    sc, span_ref, dq_ref, w_ref, lin_ref, gm_ref, gain, dstride_ref = refs[:8]
    own, sib = refs[8 : 8 + nb], refs[8 + nb : 8 + 2 * nb]
    ownp, sibp = refs[8 + 2 * nb : 8 + 3 * nb], refs[8 + 3 * nb : 8 + 4 * nb]
    gp_o, gsp_o, sums_o, kvl, q, do, stat, lse, dlt, k2, v2, dk, dv, s, d, e, ds, there, sem, sem2, sem3 = refs[8 + 4 * nb :]
    count, width = gsp_o.shape
    span = 2 * nb * count
    pairs = width // 128
    rest = q.shape[0] - span
    q[span:, :] = jnp.zeros((rest, width), BF)
    do[span:, :] = jnp.zeros((rest, width), BF)
    stat[:, span:] = jnp.zeros((stat.shape[0], rest), BF)
    there[0] = 0

    def copies(block, src=own[0], pay=ownp[0]):
        return [
            (src.at[:, pl.ds(0, width)], q.at[rows_of(block, count), :]),
            (pay.at[pl.ds(0, count), :], do.at[rows_of(block, count), :]),
        ]

    def side(block, pay=ownp[0]):
        return [(pay.at[pl.ds(count, 48), pl.ds(0, count)], stat.at[:, rows_of(block, count)])]

    local = pltpu.make_async_copy(own[SIDE].at[:, pl.ds(width, 2 * width)], kvl, sem3.at[0])
    local.start()
    sources = list(zip(window(sc, own, sib), window(sc, ownp, sibp)))
    start_copies(sc, [(block, side(block, pay)) for _, (block, pay) in sources], sem2, count)
    start_copies(sc, [(block, copies(block, src, pay)) for (block, src), (_, pay) in sources], sem, count)

    def wait(end):
        wait_until(sc, end, copies, sem, count, there)

    local.wait()
    wait_until(sc, span, side, sem2, count, there)
    there[0] = 0
    lse[...] = stat[0:8, :].astype(F32) + stat[8:16, :].astype(F32) + stat[16:24, :].astype(F32)
    dlt[...] = stat[24:32, :].astype(F32) + stat[32:40, :].astype(F32) + stat[40:48, :].astype(F32)
    low = lax.broadcasted_iota(jnp.int32, (QB, 128), 1) < 64

    def one(i, _):
        rows = pl.ds(pl.multiple_of(i * QB, QB), QB)
        for p in range(pairs):
            k2[p] = halves(kvl[rows, p * 128 : (p + 1) * 128], low) * jnp.asarray(0.125, BF)
            v2[p] = halves(kvl[rows, width + p * 128 : width + (p + 1) * 128], low)
            dk[p] = jnp.zeros_like(dk[p])
            dv[p] = jnp.zeros_like(dv[p])
        lo, hi = span_ref[rows, 2:3], span_ref[rows, 3:4]

        def step(n, parts):
            start = sc[4 + 2 * i] + n * KB
            queries = [pl.ds(pl.multiple_of(start + u * KB, 128), KB) for u in range(parts)]
            for u in range(parts):
                for p in range(pairs):
                    lanes = slice(p * 128, (p + 1) * 128)
                    s[u, p] = nt(k2[p], q[queries[u], lanes])
                    d[u, p] = nt(v2[p], do[queries[u], lanes])
            for u in range(parts):
                bias = in_range(lo, hi, start + u * KB)
                for p in range(pairs):
                    for h in range(2):
                        part = slice(h * QB, (h + 1) * QB)
                        head = slice(2 * p + h, 2 * p + h + 1)
                        grown = jnp.exp(s[u, p, part] + (bias - lse[head, queries[u]]))
                        e[u, p, part] = grown.astype(BF)
                        ds[u, p, part] = (grown * (d[u, p, part] - dlt[head, queries[u]])).astype(BF)
            for p in range(pairs):
                lanes = slice(p * 128, (p + 1) * 128)
                dv[p] = dv[p] + functools.reduce(jnp.add, [nn(e[u, p], do[queries[u], lanes]) for u in range(parts)])
                dk[p] = dk[p] + functools.reduce(jnp.add, [nn(ds[u, p], q[queries[u], lanes]) for u in range(parts)])

        chunks(sc[4 + 2 * i], sc[5 + 2 * i], step, wait)
        for p in range(pairs):
            gp_o[rows, width + p * 128 : width + (p + 1) * 128] = (pick(dk[p], low) * 0.125).astype(BF)
            gp_o[rows, 2 * width + p * 128 : 2 * width + (p + 1) * 128] = pick(dv[p], low).astype(BF)
        return 0

    lax.fori_loop(0, count // QB, one, 0)
    wait(span)
    gp_o[:, :width] = dq_ref[...]
    grad = nt(gp_o[...], w_ref[...])
    xhat, rstd = norm_parts(lin_ref[...])
    total = gm_ref[...] + norm_back(grad, xhat, rstd, vector(gain))
    gsp_o[...] = (total * dstride_ref[...]).astype(BF)
    sums_o[0:1, :] = colsum(grad * xhat)
    sums_o[1:2, :] = colsum(grad)
    sums_o[2:3, :] = colsum(gp_o[:, :width].astype(F32))
    sums_o[3:4, :] = colsum(gp_o[:, 2 * width :].astype(F32))
    sums_o[4:8, :] = jnp.zeros((4, width), F32)


def pieces(x, n):
    out = []
    for _ in range(n):
        part = x.astype(BF)
        out.append(part)
        x = x - part.astype(F32)
    return out


def mlp_kernel(
    core, ctx, lin, dy, lse, wo, w1, w2, bo, b1, b2, gain_ref, shift,
    out_o, keep_o, send_o, gm_o, pay_o, dlt_o, sums_o, out_acc, gmi_acc, roles, sem,
):
    count, width = lin.shape
    ff = w1.shape[1]

    copies = []

    def give(role, at, size, value):
        cols = slice(at, at + size)
        roles[role, :, cols] = value
        number = len(copies)
        source = roles.at[role, :, pl.ds(at, size)]
        here = pltpu.make_async_copy(source, keep_o.at[:, pl.ds(at, size)], sem.at[number])
        there = pltpu.make_async_copy(source, send_o.at[:, pl.ds(at, size)], sem.at[number])
        copies.append(here)

        @pl.when(core[0] == role)
        def _():
            here.start()

        @pl.when(core[0] != role)
        def _():
            there.start()

        return roles.at[role, :, cols]

    context = ctx[...]
    ctx_b = context.astype(BF)
    for role in range(2):
        give(role, ff + 2 * width, width // 2, ctx_b[:, role * width // 2 : (role + 1) * width // 2])
    give(0, ff, width, dy[...])
    middle = lin[...] + nn(ctx_b, wo[...]) + vector(bo)
    xhat, rstd = norm_parts(middle)
    gain = vector(gain_ref)
    mi = give(1, ff, width, (xhat * gain + vector(shift)).astype(BF))
    grad_out = dy[...].astype(F32)
    sums_o[7:8, :] = colsum(grad_out)
    for f in range(ff // width):
        cols = slice(f * width, (f + 1) * width)
        act, dact = gelu_pair(nn(mi[...], w1[:, cols]) + vector(b1.at[cols]))
        act = give(0, f * width, width, act.astype(BF))
        ghp = (nt(dy[...], w2[cols, :]) * dact).astype(BF)
        ghp_ref = give(1, f * width, width, ghp)
        sums_o[3 + f : 4 + f, :] = colsum(ghp.astype(F32))
        more = nn(act[...], w2[cols, :])
        gmore = nt(ghp_ref[...], w1[:, cols])
        if f == 0:
            out_acc[...] = middle + vector(b2) + more
            gmi_acc[...] = gmore
        else:
            out_acc[...] = out_acc[...] + more
            gmi_acc[...] = gmi_acc[...] + gmore
    out_o[...] = out_acc[...].astype(BF)
    gmi = gmi_acc[...]
    sums_o[1:2, :] = colsum(gmi * xhat)
    sums_o[2:3, :] = colsum(gmi)
    grad_middle = grad_out + norm_back(gmi, xhat, rstd, gain)
    gm_o[...] = grad_middle
    branch = grad_middle.astype(BF)
    for role in range(2):
        give(role, ff + width, width, branch)
    sums_o[0:1, :] = colsum(branch.astype(F32))
    gctx = nt(branch, wo[...]).astype(BF)
    pay_o[:count, :] = gctx
    prod = pieces(gctx.astype(F32) * context, 3)
    head = width // HEADS

    def is_head(shape, feature, number):
        feature, number = (lax.broadcasted_iota(jnp.int32, shape, n) for n in (feature, number))
        return jnp.where(feature // head == number, 1.0, 0.0).astype(BF)

    onehot, onehot_t = is_head((width, 128), 0, 1), is_head((16, width), 1, 0)
    eye = lax.broadcasted_iota(jnp.int32, (16, 128), 0) == lax.broadcasted_iota(jnp.int32, (16, 128), 1)
    eye = jnp.where(eye, 1.0, 0.0).astype(BF)
    dlt_o[...] = nn(prod[0], onehot) + nn(prod[1], onehot) + nn(prod[2], onehot)
    across = nt(onehot_t, prod[0]) + nt(onehot_t, prod[1]) + nt(onehot_t, prod[2])
    pay_o[count:, :] = jnp.zeros((48, width), BF)
    lse_t = [nt(eye, part)[:8].astype(BF) for part in pieces(lse[...], 3)]
    pay_o[count : count + 24, :count] = jnp.concatenate(lse_t, axis=0)
    pay_o[count + 24 : count + 48, :count] = jnp.concatenate(pieces(across[:8], 3), axis=0)
    for copy in copies:
        copy.wait()


def by_lanes(out, value):
    for n in range(out.shape[0]):
        out[n, : value.shape[0], :] = value[:, n * 128 : (n + 1) * 128].astype(BF)


def mlp_weights_kernel(core, big, small, branch, ctx, big2, small2, branch2, ctx2, *rest):
    out_o = rest[-1]
    last = pl.program_id(0) == pl.num_programs(0) - 1

    @pl.when(jnp.logical_not(last) & (core[0] == 0))
    def _():
        by_lanes(out_o, tn(big[...], small[...]) + tn(big2[...], small2[...]))

    @pl.when(jnp.logical_not(last) & (core[0] != 0))
    def _():
        by_lanes(out_o, tn(small[...], big[...]) + tn(small2[...], big2[...]))

    @pl.when(last)
    def _():
        by_lanes(out_o, tn(ctx[...], branch[...]) + tn(ctx2[...], branch2[...]))


def last_weights_kernel(core, ain, gp, columns, gsp, ain2, gp2, columns2, gsp2, out_o):
    @pl.when(core[0] == 0)
    def _():
        by_lanes(out_o, tn(ain[...], gp[...]) + tn(ain2[...], gp2[...]))

    @pl.when(core[0] != 0)
    def _():
        by_lanes(out_o, tn(columns[...], gsp[...]) + tn(columns2[...], gsp2[...]))


def stem_back_kernel(gsp, left, right, vw, dstem, x, pack, sums1, sums2, _, gpre, ends_o, g, gext, gup, stem):
    count, width = gsp.shape
    ext = gext.shape[0]
    inner = slice(PAD, PAD + count)
    even, odd = slice(0, width), slice(width, 2 * width)
    g[...] = jnp.zeros_like(g)
    g[inner, :] = gsp[...].astype(F32)
    g[PAD - 1 : PAD, :] = left[...].astype(F32)
    g[PAD + count : PAD + count + 1, :] = right[...].astype(F32)
    gext[...] = g[:ext, :].astype(BF)
    gup[...] = (g[1 : ext + 1, :] * pack[:, 1:2]).astype(BF)
    gpre[:, even] = (nt(gext[...], vw[width : 2 * width, :]) * dstem[:, even]).astype(BF)
    grad_odd = nt(gext[...], vw[2 * width :, :]) + nt(gup[...], vw[:width, :])
    gpre[:, odd] = (grad_odd * dstem[:, odd]).astype(BF)
    taps = tn(x[inner, : 3 * SLOT], gpre[inner, even]) + tn(x[inner, SLOT:], gpre[inner, odd])
    mels = (stem.shape[0] - 16) // 3
    for t in range(3):
        stem[t * mels : (t + 1) * mels, :] = taps[t * SLOT : t * SLOT + mels, :]
    stem_sum = colsum(gpre[inner, even].astype(F32)) + colsum(gpre[inner, odd].astype(F32))
    stride_sum = colsum(gsp[...].astype(F32))
    rows = [stem_sum, stride_sum, sums2[0:4, :], sums1[...], jnp.zeros((2, width), F32)]
    stem[3 * mels :, :] = jnp.concatenate(rows, axis=0)
    by_lanes(ends_o, stem[...])


def mel_kernel(gpre, sw, pack, mel_o, wbig, gx):
    count = mel_o.shape[0] // 2
    mels = mel_o.shape[1]
    inner = slice(PAD, PAD + count)
    taps_of(wbig, sw)
    gx[...] = nt(gpre[...], wbig[...])
    on_even = gx[inner, SLOT : 2 * SLOT] + pack[inner, 0:1] * gx[PAD - 1 : PAD + count - 1, 3 * SLOT :]
    on_odd = gx[inner, 2 * SLOT : 3 * SLOT] + pack[inner, 1:2] * gx[PAD + 1 : PAD + count + 1, :SLOT]
    mel_o[pl.ds(0, count, stride=2), :] = on_even[:, :mels]
    mel_o[pl.ds(1, count, stride=2), :] = on_odd[:, :mels]


def summed(parts):
    total = parts[0].astype(F32)
    for n in range(1, parts.shape[0]):
        total = total + parts[n].astype(F32)
    return total.astype(BF)


def sum_kernel(parts, _, out_o):
    out_o[...] = summed(parts)


def spread_kernel(parts, _, out_o):
    total = summed(parts)
    for n in range(out_o.shape[0]):
        out_o[n] = total


def unpack_kernel(core, mine, theirs, _a, _b, _c, attn_o, stride_o, stem_o, *rest):
    vectors, ends = rest[:-1], rest[-1]
    rows, width = stride_o.shape
    lanes = width // 128
    chips, each, _ = mine.shape
    share = rows * lanes // chips
    few = each - share

    def put(first, second):
        for chip in range(chips):
            at = chip * share
            while at < (chip + 1) * share:
                block, row = divmod(at, width)
                run = min((chip + 1) * share, (block + 1) * width) - at
                b, n = divmod(block, lanes)
                source = slice(at - chip * share, at - chip * share + run)
                attn_o[row : row + run, b * width + n * 128 : b * width + (n + 1) * 128] = first[chip, source, :].astype(F32)
                stride_o[b * width + row : b * width + row + run, n * 128 : (n + 1) * 128] = second[chip, source, :].astype(F32)
                at += run
            n, row = divmod(chip * few, ends.shape[0])
            total = first[chip, share:, :].astype(F32) + second[chip, share:, :].astype(F32)
            ends[row : row + few, n * 128 : (n + 1) * 128] = total

    @pl.when(core[0] == 0)
    def _():
        put(mine, theirs)

    @pl.when(core[0] != 0)
    def _():
        put(theirs, mine)

    mels = stem_o.shape[0]
    stem_o[...] = ends[:mels, :]
    row = mels
    for out in vectors:
        for n in range(out.shape[0] // width):
            out[n * width : (n + 1) * width] = ends[row + n : row + n + 1, :].reshape(width)
        row += out.shape[0] // width


def move(block, distance):
    count = lax.axis_size("frames")
    return lax.ppermute(block, "frames", [(d, (d + distance) % count) for d in range(count)])


def swap(block):
    count = lax.axis_size("frames")
    return lax.ppermute(block, "frames", [(d, d ^ 1) for d in range(count)])


def cost(us):
    return pl.CostEstimate(flops=int(us * 1.1e9), bytes_accessed=int(us * 2e6), transcendentals=0)


def call(kernel, outs, args, scratch=(), specs=None, limit=56, us=10, out_specs=None):
    vmem = pl.BlockSpec(memory_space=pltpu.VMEM)
    return pl.pallas_call(
        kernel,
        out_shape=[jax.ShapeDtypeStruct(s, d) for s, d in outs],
        in_specs=specs if specs is not None else [vmem] * len(args),
        out_specs=out_specs if out_specs is not None else [vmem] * len(outs),
        scratch_shapes=list(scratch),
        compiler_params=pltpu.CompilerParams(vmem_limit_bytes=limit * MIB),
        cost_estimate=cost(us),
    )(*args)


def chip_groups():
    chips = lax.axis_size("frames") // 2
    return [[2 * n + core for n in range(chips)] for core in range(2)]


def scatter(both):
    chips = lax.axis_size("frames") // 2
    parts = both.reshape(chips, both.shape[0] // chips, 128)
    return lax.all_to_all(parts, "frames", 0, 0, axis_index_groups=chip_groups(), tiled=True)


def unlanes(x):
    return jnp.concatenate([x[n] for n in range(x.shape[0])], axis=1)


def local(
    mel_frames, clip_lengths, valid_keys, stem_weight, stem_bias, stride_weight, stride_bias, attn_gain, attn_shift,
    attn_weight, query_bias, value_bias, output_weight, output_bias, mlp_gain, mlp_shift, hidden_weight, hidden_bias,
    return_weight, return_bias, cotangent,
):
    count, width = cotangent.shape
    ff = hidden_weight.shape[1]
    mels = mel_frames.shape[1]
    devices = lax.axis_size("frames")
    device = lax.axis_index("frames")
    core = device % 2
    nb = 2 * SIDE + 1
    ext = count + 2 * PAD
    base = (device - core - 2 * SIDE) * count

    left, right = move(mel_frames[-2:], 1), move(mel_frames[:2], -1)

    smem = pl.BlockSpec(memory_space=pltpu.SMEM)
    vmem = pl.BlockSpec(memory_space=pltpu.VMEM)
    hbm = pl.BlockSpec(memory_space=pl.ANY)
    whole = pltpu.VMEM((count, 128), jnp.int32)
    spans, pack, table, key_plan, query_plan = pl.pallas_call(
        functools.partial(tables_kernel, total=devices * count),
        out_shape=[
            jax.ShapeDtypeStruct(s, d)
            for s, d in (
                ((count, 128), jnp.int32), ((ext, 128), F32), ((count, width), F32), ((16,), jnp.int32), ((16,), jnp.int32)
            )
        ],
        in_specs=[smem] * 3,
        out_specs=[vmem] * 3 + [smem] * 2,
        scratch_shapes=[whole] * 3,
        cost_estimate=cost(4),
    )(device[None].astype(jnp.int32), clip_lengths, valid_keys)

    x, columns, dstem, dstride, layer_in, attn_in = call(
        stem_kernel,
        [
            ((ext, 4 * SLOT), BF), ((count, 3 * width), BF), ((ext, 2 * width), F32), ((count, width), F32), ((count, width), F32),
            ((count, width), BF),
        ],
        (
            mel_frames, left, right, stem_weight, stem_bias, stride_weight, stride_bias, attn_gain, attn_shift, pack, table,
        ),
        [pltpu.VMEM((2 * ext + 16, SLOT), F32), pltpu.VMEM((4 * SLOT, 2 * width), BF), pltpu.VMEM((ext, width), F32)],
        us=7,
    )

    joint = jnp.concatenate([query_bias.astype(F32), jnp.zeros((width,), F32), value_bias.astype(F32)])

    def project(block):
        return (nn(block, attn_weight) + joint).astype(BF)

    def after(value, *others):
        return lax.optimization_barrier((value, *others))[0]

    def gather(block, pair):
        own, sib = {0: project(block)}, {0: project(pair)}
        ends = block, block
        done = [own[0], sib[0]]
        for k in range(1, SIDE + 1):
            ends = move(ends[0], 2), move(ends[1], -2)
            if k == 1:
                ends = after(ends[0], *done), after(ends[1], *done)
            here, there = dict(zip((-k, k), ends)), {n: swap(b) for n, b in zip((-k, k), ends)}
            for n in (-k, k):
                own[n] = project(after(here[n], *(done if k == SIDE else there.values())))
            for n in (-k, k):
                sib[n] = project(after(there[n], own[-k], own[k]))
            done += [v[n] for v in (own, sib) for n in (-k, k)]
        order = range(-SIDE, SIDE + 1)
        return [own[n] for n in order], [sib[n] for n in order]

    pair_in = swap(attn_in)
    own, sib = gather(attn_in, pair_in)
    pair_columns = lax.ppermute(columns, "frames", [(d, d + 1) for d in range(0, devices, 2)])
    reach = 2 * nb * count + KB
    pairs = width // 128
    sems = pltpu.SemaphoreType.DMA((2 * nb, 2))
    count_of = pltpu.SMEM((1,), jnp.int32)

    stacked = pltpu.VMEM((pairs, 2 * QB, 128), BF)
    summed = pltpu.VMEM((pairs, 2 * QB, 128), F32)
    score = pltpu.VMEM((2, pairs, 2 * QB, KB), F32)
    weight = pltpu.VMEM((2, pairs, 2 * QB, KB), BF)
    one_sem = pltpu.SemaphoreType.DMA((1,))
    local_query = pltpu.VMEM((count, width), BF)

    ctx, lse = call(
        forward_kernel,
        [((count, width), F32), ((count, 128), F32)],
        (key_plan, spans, *own, *sib),
        [
            local_query, pltpu.VMEM((reach, 2 * width), BF), stacked, summed, summed, summed, summed, score, weight, count_of,
            sems, one_sem,
        ],
        [smem, vmem] + [hbm] * (2 * nb),
        us=15,
    )

    core1 = core[None].astype(jnp.int32)
    bundle = ff + 2 * width + width // 2
    layer_out, keep, send, grad_middle, pay, dlt, sums1 = call(
        mlp_kernel,
        [
            ((count, width), BF), ((count, bundle), BF), ((count, bundle), BF), ((count, width), F32), ((count + 48, width), BF),
            ((count, 128), F32), ((8, width), F32),
        ],
        (
            core1, ctx, layer_in, cotangent, lse, output_weight, hidden_weight, return_weight, output_bias, hidden_bias, return_bias,
            mlp_gain, mlp_shift,
        ),
        [
            pltpu.VMEM((count, width), F32), pltpu.VMEM((count, width), F32), pltpu.VMEM((2, count, bundle), BF),
            pltpu.SemaphoreType.DMA((2 * (ff // width) + 6,)),
        ],
        [smem] + [vmem] * 12,
        out_specs=[vmem, hbm, hbm] + [vmem] * 4,
        us=11,
    )

    travel = {-k: move(pay, 2 * k) for k in (1, -1, 2, -2)}
    travel[0] = pay
    got = swap(send)

    (grad_query,) = call(
        query_kernel,
        [((count, width), BF)],
        (key_plan, spans, pay, lse, dlt, *own, *sib),
        [
            local_query, pltpu.VMEM((reach, 2 * width), BF), stacked, stacked, summed, summed, summed, score, score, weight,
            count_of, sems, one_sem,
        ],
        [smem] + [vmem] * 4 + [hbm] * (2 * nb),
        us=15,
    )
    rows = ff + width // 2
    blocks = ff // width

    def at(n):
        return pl.BlockSpec((count, width), lambda i, core: (0, n))

    def each(i, core):
        return (0, jnp.minimum(i, blocks - 1))

    bundle_specs = [
        pl.BlockSpec((count, width), each), at(blocks), at(blocks + 1),
        pl.BlockSpec((count, width // 2), lambda i, core: (0, 2 * (blocks + 2))),
    ]
    mlp_both = pl.pallas_call(
        mlp_weights_kernel,
        out_shape=jax.ShapeDtypeStruct((pairs, rows, 128), BF),
        grid_spec=pltpu.PrefetchScalarGridSpec(
            num_scalar_prefetch=1,
            grid=(blocks + 1,),
            in_specs=bundle_specs * 2 + [hbm] * 5,
            out_specs=pl.BlockSpec((pairs, width, 128), lambda i, core: (0, i, 0)),
        ),
        compiler_params=pltpu.CompilerParams(vmem_limit_bytes=40 * MIB),
        cost_estimate=cost(5),
    )(core1, keep, keep, keep, keep, got, got, got, got, grad_query, *(travel[k] for k in (-2, -1, 1, 2))).reshape(-1, 128)

    sib_pay = {k: swap(travel[k]) for k in travel}
    own_pay, sib_pay = ([v[k] for k in range(-SIDE, SIDE + 1)] for v in (travel, sib_pay))

    grad_projected, gsp, sums2 = call(
        key_kernel,
        [((count, 3 * width), BF), ((count, width), BF), ((8, width), F32)],
        (
            query_plan, spans, grad_query, attn_weight, layer_in, grad_middle, attn_gain,
            dstride, *own, *sib, *own_pay, *sib_pay,
        ),
        [
            pltpu.VMEM((count, 2 * width), BF), pltpu.VMEM((reach, width), BF), pltpu.VMEM((reach, width), BF),
            pltpu.VMEM((48, reach), BF), pltpu.VMEM((8, reach), F32), pltpu.VMEM((8, reach), F32), stacked, stacked, summed, summed, score, score, weight,
            weight, count_of, sems, pltpu.SemaphoreType.DMA((2 * nb, 1)),
            one_sem,
        ],
        [smem] + [vmem] * 7 + [hbm] * (4 * nb),
        us=18,
    )
    left, right = move(gsp[-1:], 1), move(gsp[:1], -1)

    def to_core(n, block):
        return lax.ppermute(block, "frames", [(d + 1 - n, d + n) for d in range(0, devices, 2)])

    def whole_block(i, core):
        return (0, 0)

    def column_block(i, core):
        return (0, i)

    last_specs = [pl.BlockSpec((count, width), m) for m in (whole_block, column_block, column_block, whole_block)]
    both = pl.pallas_call(
        last_weights_kernel,
        out_shape=jax.ShapeDtypeStruct((3 * pairs, width, 128), BF),
        grid_spec=pltpu.PrefetchScalarGridSpec(
            num_scalar_prefetch=1,
            grid=(3,),
            in_specs=last_specs * 2,
            out_specs=pl.BlockSpec((pairs, width, 128), lambda i, core: (i, 0, 0)),
        ),
        compiler_params=pltpu.CompilerParams(vmem_limit_bytes=40 * MIB),
        cost_estimate=cost(3),
    )(core1, attn_in, grad_projected, columns, gsp, pair_in, to_core(0, grad_projected), pair_columns, to_core(1, gsp))
    mlp_parts = scatter(mlp_both)
    (mlp_share,) = call(
        sum_kernel, [(mlp_parts.shape[1:], BF)], (mlp_parts, both), specs=[vmem, hbm], us=3
    )

    gpre, ends = call(
        stem_back_kernel,
        [((ext, 2 * width), BF), ((pairs, 3 * mels + 16, 128), BF)],
        (gsp, left, right, stride_weight, dstem, x, pack, sums1, sums2, both),
        [
            pltpu.VMEM((ext + 8, width), F32), pltpu.VMEM((ext, width), BF), pltpu.VMEM((ext, width), BF),
            pltpu.VMEM((3 * mels + 16, width), F32),
        ],
        [vmem] * 9 + [hbm],
        us=4,
    )
    chips = devices // 2
    both = jnp.concatenate([both.reshape(chips, -1, 128), ends.reshape(chips, -1, 128)], axis=1)

    (mel_grad,) = call(
        mel_kernel,
        [((2 * count, mels), F32)],
        (gpre, stem_weight, pack),
        [pltpu.VMEM((4 * SLOT, 2 * width), BF), pltpu.VMEM((ext, 4 * SLOT), F32)],
        us=3,
    )

    parts = scatter(both.reshape(-1, 128))
    (spread,) = call(spread_kernel, [(parts.shape, BF)], (parts, mel_grad), specs=[vmem, hbm], us=3)
    mine = lax.all_to_all(spread, "frames", 0, 0, axis_index_groups=chip_groups(), tiled=True)

    every = lax.all_gather(mlp_share, "frames", axis=0, tiled=False)
    every = every.reshape(chips, 2, -1, 128)
    first, second = (every[:, n].reshape(pairs, rows, 128) for n in range(2))
    grad_return_weight = unlanes(first[:, :ff]).astype(F32)
    grad_hidden_weight = jnp.concatenate(
        [unlanes(second[:, b * width : (b + 1) * width]) for b in range(ff // width)], axis=1
    ).astype(F32)
    half = slice(ff, ff + width // 2)
    grad_output_weight = jnp.concatenate([unlanes(first[:, half]), unlanes(second[:, half])], axis=0).astype(F32)

    sizes = [width] * 9 + [ff, width]
    grad_attn_weight, grad_stride_weight, grad_stem_weight, *bias = call(
        unpack_kernel,
        [((width, 3 * width), F32), ((3 * width, width), F32), ((3 * mels, width), F32)] + [((n,), F32) for n in sizes],
        (core1, mine, swap(mine), grad_return_weight, grad_hidden_weight, grad_output_weight),
        [pltpu.VMEM((3 * mels + 16, width), F32)],
        [smem, vmem, vmem] + [hbm] * 3,
        us=6,
    )
    return (
        layer_out, mel_grad, grad_stem_weight, bias[0], grad_stride_weight, bias[1], bias[2], bias[3], grad_attn_weight,
        bias[4], bias[5], grad_output_weight, bias[6], bias[7], bias[8], grad_hidden_weight, bias[9],
        grad_return_weight, bias[10],
    )


def solution(mesh):
    split = P("frames", None)
    in_specs = (split,) + (P(),) * 19 + (split,)
    out_specs = (split, split) + (P(),) * 17
    return jax.shard_map(local, mesh=mesh, in_specs=in_specs, out_specs=out_specs, check_vma=False)
```

```python
import functools
import math

import jax
import jax.numpy as jnp
from jax import lax
from jax.experimental import pallas as pl
from jax.experimental.pallas import tpu as pltpu
from jax.sharding import PartitionSpec as P

HEADS = 8
SIDE = 2
QB = 128
KB = 256
PAD = 16
SLOT = 128
NEG = -1e30
BF = jnp.bfloat16
F32 = jnp.float32
MIB = 1 << 20


def nn(a, b):
    return lax.dot_general(a, b, (((1,), (0,)), ((), ())), preferred_element_type=F32)


def nt(a, b):
    return lax.dot_general(a, b, (((1,), (1,)), ((), ())), preferred_element_type=F32)


def tn(a, b):
    return lax.dot_general(a, b, (((0,), (0,)), ((), ())), preferred_element_type=F32)


def gelu_pair(x):
    bell = jnp.exp(-0.5 * x * x)
    t = 1.0 / (1.0 + 0.2316419 * jnp.abs(x))
    poly = 0.127414796 + t * (-0.142248368 + t * (0.7107068705 + t * (-0.7265760135 + t * 0.5307027145)))
    tail = bell * t * poly
    phi = jnp.where(x >= 0, 1.0 - tail, tail)
    return x * phi, phi + 0.3989422804 * x * bell


def norm_parts(x):
    center = jnp.mean(x, axis=-1, keepdims=True)
    centered = x - center
    rstd = lax.rsqrt(jnp.mean(centered * centered, axis=-1, keepdims=True) + 1e-05)
    return centered * rstd, rstd


def norm_back(grad, xhat, rstd, gain):
    inner = grad * gain
    m1 = jnp.mean(inner, axis=-1, keepdims=True)
    m2 = jnp.mean(inner * xhat, axis=-1, keepdims=True)
    return rstd * (inner - m1 - xhat * m2)


def vector(ref):
    return ref[...].astype(F32).reshape(1, -1)


def colsum(x):
    return jnp.sum(x, axis=0, keepdims=True)


def halves(x, low):
    zero = jnp.zeros_like(x)
    return jnp.concatenate([jnp.where(low, x, zero), jnp.where(low, zero, x)], axis=0)


def pick(x, low):
    return jnp.where(low, x[:QB], x[QB:])


def wide(x):
    return jnp.concatenate([x, x], axis=1)


def tall(x):
    return jnp.concatenate([x, x], axis=0)


def tables_kernel(device, lengths, valids, spans_o, pack_o, table_o, keys_o, queries_o, start_s, length_s, valid_s, *, total):
    count, width = table_o.shape
    base = (device[0] - device[0] % 2 - 2 * SIDE) * count
    first = device[0] * count
    token = first + lax.broadcasted_iota(jnp.int32, (count, 128), 0)
    row = lax.broadcasted_iota(jnp.int32, pack_o.shape, 0) + lax.broadcasted_iota(jnp.int32, pack_o.shape, 1) - PAD
    here = (row >= 0) & (row <= count) & (first + row < total)
    pack_o[...] = jnp.where(here, 1.0, 0.0)
    keys_o[0] = queries_o[0] = device[0] % 2

    def clip(c, start):
        length = lengths[c]
        valid = jnp.minimum(valids[c], length)
        end = start + length

        @pl.when((start < first + count) & (end > first))
        def _():
            inside = (token >= start) & (token < end)
            start_s[...] = jnp.where(inside, start, start_s[...])
            length_s[...] = jnp.where(inside, length, length_s[...])
            valid_s[...] = jnp.where(inside, valid, valid_s[...])
            for n in range(count // QB):
                at = first + n * QB

                @pl.when((start <= at) & (at < end))
                def _():
                    keys_o[4 + 2 * n] = queries_o[4 + 2 * n] = ((start - base) >> 7) << 7

                @pl.when((start < at + QB) & (at + QB <= end))
                def _():
                    keys_o[5 + 2 * n] = start + valid - base
                    queries_o[5 + 2 * n] = end - base

        @pl.when((start >= first) & (start <= first + count))
        def _():
            pack_o[...] = jnp.where(first + row == start, 0.0, pack_o[...])

        return end

    lax.fori_loop(0, lengths.shape[0], clip, 0)
    for plan in (keys_o, queries_o):
        low, high = plan[4], 0
        for n in range(count // QB):
            steps = (plan[5 + 2 * n] - plan[4 + 2 * n] + KB - 1) // KB
            plan[5 + 2 * n] = steps
            low = jnp.minimum(low, plan[4 + 2 * n])
            high = jnp.maximum(high, plan[4 + 2 * n] + steps * KB)
        plan[1], plan[2] = low, high
    lane = lax.broadcasted_iota(jnp.int32, (count, 128), 1)
    key_lo = start_s[...] - base
    position = token - start_s[...]
    is_key = position < valid_s[...]
    query_lo = jnp.where(is_key, key_lo, 1 << 20)
    query_hi = jnp.where(is_key, key_lo + length_s[...], 0)
    first_two = jnp.where(lane == 0, key_lo, key_lo + valid_s[...])
    spans_o[...] = jnp.where(lane < 2, first_two, jnp.where(lane == 2, query_lo, query_hi))
    half = width // 2
    number = lax.broadcasted_iota(jnp.int32, (1, half), 1).astype(F32)
    rates = jnp.exp(number * (-math.log(10000.0) / (half - 1)))
    angles = wide(position.astype(F32)) * rates
    table_o[:, :half] = jnp.sin(angles)
    table_o[:, half:] = jnp.cos(angles)


def taps_of(wbig, sw):
    mels, width = sw.shape[0] // 3, sw.shape[1]
    wbig[...] = jnp.zeros_like(wbig)
    for t in range(3):
        tap = sw[t * mels : (t + 1) * mels, :]
        wbig[t * SLOT : t * SLOT + mels, :width] = tap
        wbig[(t + 1) * SLOT : (t + 1) * SLOT + mels, width:] = tap


def stem_kernel(
    mel, left, right, sw, sbias, vw, vbias, gain, shift, pack, table,
    x_o, cols_o, dstem_o, dstride_o, lin_o, ain_o, m, wbig, shifted,
):
    count, width = lin_o.shape
    frames, mels = mel.shape
    ext = x_o.shape[0]
    taps_of(wbig, sw)
    top = 2 * PAD + 8
    m[...] = jnp.zeros_like(m)
    m[top : top + frames, :mels] = mel[...].astype(F32)
    m[top - 2 : top, :mels] = left[...].astype(F32)
    m[top + frames : top + frames + 2, :mels] = right[...].astype(F32)
    opn, opn_next = pack[:, 0:1], pack[:, 1:2]
    x_o[:, :SLOT] = (m[pl.ds(7, ext, stride=2), :] * opn).astype(BF)
    x_o[:, SLOT : 2 * SLOT] = m[pl.ds(8, ext, stride=2), :].astype(BF)
    x_o[:, 2 * SLOT : 3 * SLOT] = m[pl.ds(9, ext, stride=2), :].astype(BF)
    x_o[:, 3 * SLOT :] = (m[pl.ds(10, ext, stride=2), :] * opn_next).astype(BF)
    inner = slice(PAD, PAD + count)
    even, odd = slice(0, width), slice(width, 2 * width)
    act, dact = gelu_pair(nn(x_o[...], wbig[:, even]) + vector(sbias))
    dstem_o[:, even] = dact
    cols_o[:, width : 2 * width] = act[inner].astype(BF)
    act, dact = gelu_pair(nn(x_o[...], wbig[:, odd]) + vector(sbias))
    dstem_o[:, odd] = dact
    cols_o[:, 2 * width :] = act[inner].astype(BF)
    shifted[...] = act
    cols_o[:, :width] = (shifted[PAD - 1 : PAD + count - 1, :] * pack[inner, 0:1]).astype(BF)
    pre = nn(cols_o[...], vw[...]) + vector(vbias)
    act2, dact2 = gelu_pair(pre)
    dstride_o[...] = dact2
    lin = act2 + table[...]
    lin_o[...] = lin
    xhat, _ = norm_parts(lin)
    ain_o[...] = (xhat * vector(gain) + vector(shift)).astype(BF)


def needed(sc, block, count):
    return (block * count < sc[2]) & ((block + 1) * count > sc[1])


def start_copies(sc, pairs, sem, count):
    for block, copies in pairs:
        @pl.when(needed(sc, block, count))
        def _():
            for m, (src, dst) in enumerate(copies):
                pltpu.make_async_copy(src, dst, sem.at[block, m]).start()


def wait_until(sc, end, copies, sem, count, there):
    def one(block, _):
        @pl.when(needed(sc, block, count))
        def _():
            for m, (src, dst) in enumerate(copies(block)):
                pltpu.make_async_copy(src, dst, sem.at[block, m]).wait()

        return 0

    upto = jnp.minimum((end + count - 1) // count, 2 * (2 * SIDE + 1))
    lax.fori_loop(there[0], upto, one, 0)
    there[0] = jnp.maximum(there[0], upto)


def window(sc, own, sib):
    core = sc[0]
    out = []
    for k in range(2 * SIDE + 1):
        out += [(2 * k + core, own[k]), (2 * k + 1 - core, sib[k])]
    return out


def rows_of(block, count):
    return pl.ds(pl.multiple_of(block * count, count), count)


def in_range(lo, hi, start):
    col = start + lax.broadcasted_iota(jnp.int32, (QB, KB), 1)
    return jnp.where((col >= lo) & (col < hi), 0.0, NEG)


def chunks(first, steps, step, wait):
    def two(n, _):
        wait(first + (2 * n + 2) * KB)
        step(2 * n, 2)
        return 0

    lax.fori_loop(0, steps // 2, two, 0)

    @pl.when(steps % 2 == 1)
    def _():
        wait(first + steps * KB)
        step(steps - 1, 1)


def layer_kernel(*refs):
    nb = 2 * SIDE + 1
    sc, span_ref = refs[:2]
    own, sib = refs[2 : 2 + nb], refs[2 + nb : 2 + 2 * nb]
    at = 2 + 2 * nb
    fetched, vectors, outs = refs[at : at + 5], refs[at + 5 : at + 10], refs[at + 10 : at + 18]
    lse_o = outs[0]
    scratch = refs[at + 18 :]
    ctx_o, local_ref, kv, q2, acc, peak, total, scale, s, e, there, sem, sem2 = scratch[:13]
    held, mlp_scratch = scratch[13:18], scratch[18:]
    count, width = ctx_o.shape
    late = [pltpu.make_async_copy(src, dst, sem2.at[1 + n]) for n, (src, dst) in enumerate(zip(fetched, held))]
    span = 2 * nb * count
    pairs = width // 128
    kv[span:, :] = jnp.zeros((kv.shape[0] - span, 2 * width), BF)
    there[0] = 0

    def copies(block, src=own[0]):
        return [(src.at[:, pl.ds(width, 2 * width)], kv.at[rows_of(block, count), :])]

    local = pltpu.make_async_copy(own[SIDE].at[:, pl.ds(0, width)], local_ref, sem2.at[0])
    local.start()
    start_copies(sc, [(block, copies(block, src)) for block, src in window(sc, own, sib)], sem, count)
    for copy in late:
        copy.start()
    local.wait()

    def wait(end):
        wait_until(sc, end, copies, sem, count, there)

    low = lax.broadcasted_iota(jnp.int32, (QB, 128), 1) < 64
    lanes = lax.broadcasted_iota(jnp.int32, (QB, 128), 1)

    def one(i, _):
        rows = pl.ds(pl.multiple_of(i * QB, QB), QB)
        for p in range(pairs):
            q2[p] = halves(local_ref[rows, p * 128 : (p + 1) * 128], low) * jnp.asarray(0.125, BF)
            acc[p] = jnp.zeros_like(acc[p])
            peak[p] = jnp.full_like(peak[p], NEG)
            total[p] = jnp.zeros_like(total[p])
        lo, hi = span_ref[rows, 0:1], span_ref[rows, 1:2]

        def step(n, parts):
            start = sc[4 + 2 * i] + n * KB
            keys = [pl.ds(pl.multiple_of(start + u * KB, 128), KB) for u in range(parts)]
            for u in range(parts):
                bias = tall(in_range(lo, hi, start + u * KB))
                for p in range(pairs):
                    s[u, p] = nt(q2[p], kv[keys[u], p * 128 : (p + 1) * 128]) + bias
            for p in range(pairs):
                best = functools.reduce(jnp.maximum, [s[u, p] for u in range(parts)])
                old = peak[p]
                top = jnp.maximum(old, jnp.max(best, axis=1, keepdims=True))
                peak[p] = top
                scale[p] = jnp.exp(old - top)
            for p in range(pairs):
                total[p] = scale[p] * total[p]
                for u in range(parts):
                    grown = jnp.exp(s[u, p] - wide(peak[p]))
                    e[u, p] = grown.astype(BF)
                    total[p] = total[p] + (grown[:, :128] + grown[:, 128:])
            for p in range(pairs):
                value = [kv[keys[u], width + p * 128 : width + (p + 1) * 128] for u in range(parts)]
                acc[p] = scale[p] * acc[p] + functools.reduce(jnp.add, [nn(e[u, p], value[u]) for u in range(parts)])

        chunks(sc[4 + 2 * i], sc[5 + 2 * i], step, wait)
        lse = jnp.zeros((QB, 128), F32)
        for p in range(pairs):
            row_total = jnp.sum(total[p], axis=1, keepdims=True)
            ctx_o[rows, p * 128 : (p + 1) * 128] = pick(acc[p] / row_total, low)
            both = peak[p] + jnp.log(row_total)
            lse = jnp.where(lanes == 2 * p, both[:QB], lse)
            lse = jnp.where(lanes == 2 * p + 1, both[QB:], lse)
        lse_o[rows, :] = lse
        return 0

    lax.fori_loop(0, count // QB, one, 0)
    wait(span)
    for copy in late:
        copy.wait()
    mlp(sc, ctx_o, lse_o, *held, *vectors, *outs[1:], *mlp_scratch)


def query_kernel(*refs):
    nb = 2 * SIDE + 1
    sc, span_ref, pay_ref, lse_ref, dlt_ref = refs[:5]
    own, sib = refs[5 : 5 + nb], refs[5 + nb : 5 + 2 * nb]
    dq_o, local_ref, kv, q2, do2, acc, lse2, dlt2, s, d, ds, there, sem, sem2 = refs[7 + 2 * nb :]
    count, width = dq_o.shape
    span = 2 * nb * count
    pairs = width // 128
    kv[span:, :] = jnp.zeros((kv.shape[0] - span, 2 * width), BF)
    there[0] = 0

    def copies(block, src=own[0]):
        return [(src.at[:, pl.ds(width, 2 * width)], kv.at[rows_of(block, count), :])]

    local = pltpu.make_async_copy(own[SIDE].at[:, pl.ds(0, width)], local_ref, sem2.at[0])
    local.start()
    start_copies(sc, [(block, copies(block, src)) for block, src in window(sc, own, sib)], sem, count)
    local.wait()

    def wait(end):
        wait_until(sc, end, copies, sem, count, there)

    low = lax.broadcasted_iota(jnp.int32, (QB, 128), 1) < 64

    def one(i, _):
        rows = pl.ds(pl.multiple_of(i * QB, QB), QB)
        lse, dlt = lse_ref[rows, :], dlt_ref[rows, :]
        for p in range(pairs):
            q2[p] = halves(local_ref[rows, p * 128 : (p + 1) * 128], low) * jnp.asarray(0.125, BF)
            do2[p] = halves(pay_ref[rows, p * 128 : (p + 1) * 128], low)
            acc[p] = jnp.zeros_like(acc[p])
            for h in range(2):
                part = pl.ds(h * QB, QB)
                lse2[p, part, :] = jnp.broadcast_to(lse[:, 2 * p + h : 2 * p + h + 1], (QB, 128))
                dlt2[p, part, :] = jnp.broadcast_to(dlt[:, 2 * p + h : 2 * p + h + 1], (QB, 128))
        lo, hi = span_ref[rows, 0:1], span_ref[rows, 1:2]

        def step(n, parts):
            start = sc[4 + 2 * i] + n * KB
            keys = [pl.ds(pl.multiple_of(start + u * KB, 128), KB) for u in range(parts)]
            for u in range(parts):
                bias = tall(in_range(lo, hi, start + u * KB))
                for p in range(pairs):
                    s[u, p] = nt(q2[p], kv[keys[u], p * 128 : (p + 1) * 128]) + bias
                    d[u, p] = nt(do2[p], kv[keys[u], width + p * 128 : width + (p + 1) * 128])
            for u in range(parts):
                for p in range(pairs):
                    e = jnp.exp(s[u, p] - wide(lse2[p]))
                    ds[u, p] = (e * (d[u, p] - wide(dlt2[p]))).astype(BF)
            for p in range(pairs):
                more = [nn(ds[u, p], kv[keys[u], p * 128 : (p + 1) * 128]) for u in range(parts)]
                acc[p] = acc[p] + functools.reduce(jnp.add, more)

        chunks(sc[4 + 2 * i], sc[5 + 2 * i], step, wait)
        for p in range(pairs):
            dq_o[rows, p * 128 : (p + 1) * 128] = (pick(acc[p], low) * 0.125).astype(BF)
        return 0

    lax.fori_loop(0, count // QB, one, 0)
    wait(span)


def key_kernel(*refs):
    nb = 2 * SIDE + 1
    sc, span_ref, dq_ref, w_ref, lin_ref, gm_ref, gain, dstride_ref = refs[:8]
    own, sib = refs[8 : 8 + nb], refs[8 + nb : 8 + 2 * nb]
    ownp, sibp = refs[8 + 2 * nb : 8 + 3 * nb], refs[8 + 3 * nb : 8 + 4 * nb]
    gp_o, gsp_o, sums_o, kvl, q, do, stat, lse, dlt, k2, v2, dk, dv, s, d, e, ds, there, sem, sem2, sem3 = refs[9 + 4 * nb :]
    count, width = gsp_o.shape
    span = 2 * nb * count
    pairs = width // 128
    rest = q.shape[0] - span
    q[span:, :] = jnp.zeros((rest, width), BF)
    do[span:, :] = jnp.zeros((rest, width), BF)
    stat[:, span:] = jnp.zeros((stat.shape[0], rest), BF)
    there[0] = 0

    def copies(block, src=own[0], pay=ownp[0]):
        return [
            (src.at[:, pl.ds(0, width)], q.at[rows_of(block, count), :]),
            (pay.at[pl.ds(0, count), :], do.at[rows_of(block, count), :]),
        ]

    def side(block, pay=ownp[0]):
        return [(pay.at[pl.ds(count, 48), pl.ds(0, count)], stat.at[:, rows_of(block, count)])]

    local = pltpu.make_async_copy(own[SIDE].at[:, pl.ds(width, 2 * width)], kvl, sem3.at[0])
    local.start()
    sources = list(zip(window(sc, own, sib), window(sc, ownp, sibp)))
    start_copies(sc, [(block, side(block, pay)) for _, (block, pay) in sources], sem2, count)
    start_copies(sc, [(block, copies(block, src, pay)) for (block, src), (_, pay) in sources], sem, count)

    def wait(end):
        wait_until(sc, end, copies, sem, count, there)

    local.wait()
    wait_until(sc, span, side, sem2, count, there)
    there[0] = 0
    lse[...] = stat[0:8, :].astype(F32) + stat[8:16, :].astype(F32) + stat[16:24, :].astype(F32)
    dlt[...] = stat[24:32, :].astype(F32) + stat[32:40, :].astype(F32) + stat[40:48, :].astype(F32)
    low = lax.broadcasted_iota(jnp.int32, (QB, 128), 1) < 64

    def one(i, _):
        rows = pl.ds(pl.multiple_of(i * QB, QB), QB)
        for p in range(pairs):
            k2[p] = halves(kvl[rows, p * 128 : (p + 1) * 128], low) * jnp.asarray(0.125, BF)
            v2[p] = halves(kvl[rows, width + p * 128 : width + (p + 1) * 128], low)
            dk[p] = jnp.zeros_like(dk[p])
            dv[p] = jnp.zeros_like(dv[p])
        lo, hi = span_ref[rows, 2:3], span_ref[rows, 3:4]

        def step(n, parts):
            start = sc[4 + 2 * i] + n * KB
            queries = [pl.ds(pl.multiple_of(start + u * KB, 128), KB) for u in range(parts)]
            for u in range(parts):
                for p in range(pairs):
                    lanes = slice(p * 128, (p + 1) * 128)
                    s[u, p] = nt(k2[p], q[queries[u], lanes])
                    d[u, p] = nt(v2[p], do[queries[u], lanes])
            for u in range(parts):
                bias = in_range(lo, hi, start + u * KB)
                for p in range(pairs):
                    for h in range(2):
                        part = slice(h * QB, (h + 1) * QB)
                        head = slice(2 * p + h, 2 * p + h + 1)
                        grown = jnp.exp(s[u, p, part] + (bias - lse[head, queries[u]]))
                        e[u, p, part] = grown.astype(BF)
                        ds[u, p, part] = (grown * (d[u, p, part] - dlt[head, queries[u]])).astype(BF)
            for p in range(pairs):
                lanes = slice(p * 128, (p + 1) * 128)
                dv[p] = dv[p] + functools.reduce(jnp.add, [nn(e[u, p], do[queries[u], lanes]) for u in range(parts)])
                dk[p] = dk[p] + functools.reduce(jnp.add, [nn(ds[u, p], q[queries[u], lanes]) for u in range(parts)])

        chunks(sc[4 + 2 * i], sc[5 + 2 * i], step, wait)
        for p in range(pairs):
            gp_o[rows, width + p * 128 : width + (p + 1) * 128] = (pick(dk[p], low) * 0.125).astype(BF)
            gp_o[rows, 2 * width + p * 128 : 2 * width + (p + 1) * 128] = pick(dv[p], low).astype(BF)
        return 0

    lax.fori_loop(0, count // QB, one, 0)
    wait(span)
    gp_o[:, :width] = dq_ref[...]
    grad = nt(gp_o[...], w_ref[...])
    xhat, rstd = norm_parts(lin_ref[...])
    total = gm_ref[...] + norm_back(grad, xhat, rstd, vector(gain))
    gsp_o[...] = (total * dstride_ref[...]).astype(BF)
    sums_o[0:1, :] = colsum(grad * xhat)
    sums_o[1:2, :] = colsum(grad)
    sums_o[2:3, :] = colsum(gp_o[:, :width].astype(F32))
    sums_o[3:4, :] = colsum(gp_o[:, 2 * width :].astype(F32))
    sums_o[4:8, :] = jnp.zeros((4, width), F32)


def pieces(x, n):
    out = []
    for _ in range(n):
        part = x.astype(BF)
        out.append(part)
        x = x - part.astype(F32)
    return out


def mlp(
    core, ctx, lse, lin, dy, wo, w1, w2, bo, b1, b2, gain_ref, shift,
    out_o, keep_o, send_o, gm_o, pay_o, dlt_o, sums_o, out_acc, gmi_acc, roles, sem,
):
    count, width = lin.shape
    ff = w1.shape[1]

    copies = []

    def give(role, at, size, value):
        cols = slice(at, at + size)
        roles[role, :, cols] = value
        number = len(copies)
        source = roles.at[role, :, pl.ds(at, size)]
        here = pltpu.make_async_copy(source, keep_o.at[:, pl.ds(at, size)], sem.at[number])
        there = pltpu.make_async_copy(source, send_o.at[:, pl.ds(at, size)], sem.at[number])
        copies.append(here)

        @pl.when(core[0] == role)
        def _():
            here.start()

        @pl.when(core[0] != role)
        def _():
            there.start()

        return roles.at[role, :, cols]

    context = ctx[...]
    ctx_b = context.astype(BF)
    for role in range(2):
        give(role, ff + 2 * width, width // 2, ctx_b[:, role * width // 2 : (role + 1) * width // 2])
    give(0, ff, width, dy[...])
    middle = lin[...] + nn(ctx_b, wo[...]) + vector(bo)
    xhat, rstd = norm_parts(middle)
    gain = vector(gain_ref)
    mi = give(1, ff, width, (xhat * gain + vector(shift)).astype(BF))
    grad_out = dy[...].astype(F32)
    sums_o[7:8, :] = colsum(grad_out)
    for f in range(ff // width):
        cols = slice(f * width, (f + 1) * width)
        act, dact = gelu_pair(nn(mi[...], w1[:, cols]) + vector(b1.at[cols]))
        act = give(0, f * width, width, act.astype(BF))
        ghp = (nt(dy[...], w2[cols, :]) * dact).astype(BF)
        ghp_ref = give(1, f * width, width, ghp)
        sums_o[3 + f : 4 + f, :] = colsum(ghp.astype(F32))
        more = nn(act[...], w2[cols, :])
        gmore = nt(ghp_ref[...], w1[:, cols])
        if f == 0:
            out_acc[...] = middle + vector(b2) + more
            gmi_acc[...] = gmore
        else:
            out_acc[...] = out_acc[...] + more
            gmi_acc[...] = gmi_acc[...] + gmore
    out_o[...] = out_acc[...].astype(BF)
    gmi = gmi_acc[...]
    sums_o[1:2, :] = colsum(gmi * xhat)
    sums_o[2:3, :] = colsum(gmi)
    grad_middle = grad_out + norm_back(gmi, xhat, rstd, gain)
    gm_o[...] = grad_middle
    branch = grad_middle.astype(BF)
    for role in range(2):
        give(role, ff + width, width, branch)
    sums_o[0:1, :] = colsum(branch.astype(F32))
    gctx = nt(branch, wo[...]).astype(BF)
    pay_o[:count, :] = gctx
    prod = pieces(gctx.astype(F32) * context, 3)
    head = width // HEADS

    def is_head(shape, feature, number):
        feature, number = (lax.broadcasted_iota(jnp.int32, shape, n) for n in (feature, number))
        return jnp.where(feature // head == number, 1.0, 0.0).astype(BF)

    onehot, onehot_t = is_head((width, 128), 0, 1), is_head((16, width), 1, 0)
    eye = lax.broadcasted_iota(jnp.int32, (16, 128), 0) == lax.broadcasted_iota(jnp.int32, (16, 128), 1)
    eye = jnp.where(eye, 1.0, 0.0).astype(BF)
    dlt_o[...] = nn(prod[0], onehot) + nn(prod[1], onehot) + nn(prod[2], onehot)
    across = nt(onehot_t, prod[0]) + nt(onehot_t, prod[1]) + nt(onehot_t, prod[2])
    pay_o[count:, :] = jnp.zeros((48, width), BF)
    lse_t = [nt(eye, part)[:8].astype(BF) for part in pieces(lse[...], 3)]
    pay_o[count : count + 24, :count] = jnp.concatenate(lse_t, axis=0)
    pay_o[count + 24 : count + 48, :count] = jnp.concatenate(pieces(across[:8], 3), axis=0)
    for copy in copies:
        copy.wait()


def put_tiles(out, block, value):
    groups = out.shape[0]
    for n in range(value.shape[1] // 128):
        tile = block * (value.shape[1] // 128) + n
        each = (out.shape[2] - 16) // 16
        rows = pl.ds(pl.multiple_of(tile % each * 16, 16), 16)
        out[:, tile // each, rows, :] = value[:, n * 128 : (n + 1) * 128].astype(BF).reshape(groups, 16, 128)


def put_last(out, value):
    lanes = value.shape[1] // 128
    for row in range(value.shape[0] // 16):
        for n in range(lanes):
            chip = row * lanes + n
            tile = value[row * 16 : (row + 1) * 16, n * 128 : (n + 1) * 128]
            out[chip // 2, chip % 2, out.shape[2] - 16 :, :] = tile.astype(BF)


def mlp_weights_kernel(core, big, small, branch, ctx, big2, small2, branch2, ctx2, *rest):
    out_o = rest[-1]
    step = pl.program_id(0)
    last = step == pl.num_programs(0) - 1

    @pl.when(jnp.logical_not(last) & (core[0] == 0))
    def _():
        put_tiles(out_o, step, tn(big[...], small[...]) + tn(big2[...], small2[...]))

    @pl.when(jnp.logical_not(last) & (core[0] != 0))
    def _():
        put_tiles(out_o, step, tn(small[...], big[...]) + tn(small2[...], big2[...]))

    @pl.when(last)
    def _():
        put_last(out_o, tn(ctx[...], branch[...]) + tn(ctx2[...], branch2[...]))


def last_weights_kernel(core, ain, gp, columns, gsp, ain2, gp2, columns2, gsp2, out_o):
    step = pl.program_id(0)

    @pl.when(core[0] == 0)
    def _():
        put_tiles(out_o, step, tn(ain[...], gp[...]) + tn(ain2[...], gp2[...]))

    @pl.when(core[0] != 0)
    def _():
        put_tiles(out_o, step, tn(columns[...], gsp[...]) + tn(columns2[...], gsp2[...]))


def stem_back_kernel(gsp, left, right, vw, dstem, x, pack, sums1, sums2, rows_in, gpre, rows_o, g, gext, gup, stem, tiles, sem):
    count, width = gsp.shape
    ext = gext.shape[0]
    inner = slice(PAD, PAD + count)
    even, odd = slice(0, width), slice(width, 2 * width)
    g[...] = jnp.zeros_like(g)
    g[inner, :] = gsp[...].astype(F32)
    g[PAD - 1 : PAD, :] = left[...].astype(F32)
    g[PAD + count : PAD + count + 1, :] = right[...].astype(F32)
    gext[...] = g[:ext, :].astype(BF)
    gup[...] = (g[1 : ext + 1, :] * pack[:, 1:2]).astype(BF)
    gpre[:, even] = (nt(gext[...], vw[width : 2 * width, :]) * dstem[:, even]).astype(BF)
    grad_odd = nt(gext[...], vw[2 * width :, :]) + nt(gup[...], vw[:width, :])
    gpre[:, odd] = (grad_odd * dstem[:, odd]).astype(BF)
    taps = tn(x[inner, : 3 * SLOT], gpre[inner, even]) + tn(x[inner, SLOT:], gpre[inner, odd])
    mels = (stem.shape[0] - 16) // 3
    for t in range(3):
        stem[t * mels : (t + 1) * mels, :] = taps[t * SLOT : t * SLOT + mels, :]
    stem_sum = colsum(gpre[inner, even].astype(F32)) + colsum(gpre[inner, odd].astype(F32))
    stride_sum = colsum(gsp[...].astype(F32))
    rows = [stem_sum, stride_sum, sums2[0:4, :], sums1[...], jnp.zeros((2, width), F32)]
    stem[3 * mels :, :] = jnp.concatenate(rows, axis=0)
    put_last(tiles, stem[...])
    share = rows_o.shape[2]
    copy = pltpu.make_async_copy(tiles, rows_o.at[:, :, pl.ds(share - 16, 16), :], sem.at[0])
    copy.start()
    copy.wait()


def mel_kernel(gpre, sw, pack, mel_o, wbig, gx):
    count = mel_o.shape[0] // 2
    mels = mel_o.shape[1]
    inner = slice(PAD, PAD + count)
    taps_of(wbig, sw)
    gx[...] = nt(gpre[...], wbig[...])
    on_even = gx[inner, SLOT : 2 * SLOT] + pack[inner, 0:1] * gx[PAD - 1 : PAD + count - 1, 3 * SLOT :]
    on_odd = gx[inner, 2 * SLOT : 3 * SLOT] + pack[inner, 1:2] * gx[PAD + 1 : PAD + count + 1, :SLOT]
    mel_o[pl.ds(0, count, stride=2), :] = on_even[:, :mels]
    mel_o[pl.ds(1, count, stride=2), :] = on_odd[:, :mels]


def summed(parts):
    def more(n, total):
        return total + parts[n].astype(F32)

    return lax.fori_loop(1, parts.shape[0], more, parts[0].astype(F32)).astype(BF)


def spread_kernel(parts, *rest):
    out_o = rest[-1]
    total = summed(parts)

    def put(n, _):
        out_o[n] = total
        return 0

    lax.fori_loop(0, out_o.shape[0], put, 0)


def both_halves(core, mine, theirs, group, part, rows):
    a, b = mine[group, part, rows, :].astype(F32), theirs[group, part, rows, :].astype(F32)
    return jnp.where(core[0] == 0, a, b), jnp.where(core[0] == 0, b, a)


def unpack_mlp_kernel(core, mine, theirs, return_o, hidden_o, output_o):
    width = return_o.shape[1]
    lanes = width // 128
    each = (mine.shape[2] - 16) // 16

    def one(group, _):
        for tile in range(2 * each):
            rows = slice(tile % each * 16, tile % each * 16 + 16)
            first, second = both_halves(core, mine, theirs, group, tile // each, rows)
            block, n = divmod(tile, lanes)
            here = pl.ds(pl.multiple_of(block * width + group * 16, 16), 16)
            return_o[here, n * 128 : (n + 1) * 128] = first
            here = pl.ds(pl.multiple_of(group * 16, 16), 16)
            hidden_o[here, block * width + n * 128 : block * width + (n + 1) * 128] = second
        return 0

    lax.fori_loop(0, width // 16, one, 0)
    half = width // 2

    def last(row, _):
        for n in range(lanes):
            chip = slice(each * 16, each * 16 + 16)
            first, second = both_halves(core, mine, theirs, row * (lanes // 2) + n // 2, n % 2, chip)
            output_o[pl.ds(pl.multiple_of(row * 16, 16), 16), n * 128 : (n + 1) * 128] = first
            output_o[pl.ds(pl.multiple_of(half + row * 16, 16), 16), n * 128 : (n + 1) * 128] = second
        return 0

    lax.fori_loop(0, half // 16, last, 0)


def unpack_kernel(core, mine, theirs, attn_o, stride_o, stem_o, *rest):
    vectors, ends = rest[:-1], rest[-1]
    width = stride_o.shape[1]
    lanes = width // 128
    each = (mine.shape[2] - 16) // 16

    def one(group, _):
        at = group * 16
        for tile in range(2 * each):
            rows = slice(tile % each * 16, tile % each * 16 + 16)
            first, second = both_halves(core, mine, theirs, group, tile // each, rows)
            attn_o[pl.ds(pl.multiple_of(at, 16), 16), tile * 128 : (tile + 1) * 128] = first
            block, n = divmod(tile, lanes)
            stride_o[pl.ds(pl.multiple_of(block * width + at, 16), 16), n * 128 : (n + 1) * 128] = second
        return 0

    lax.fori_loop(0, mine.shape[0], one, 0)
    last = slice(each * 16, each * 16 + 16)
    for row in range(ends.shape[0] // 16):
        for n in range(lanes):
            chip = row * lanes + n
            first, second = both_halves(core, mine, theirs, chip // 2, chip % 2, last)
            ends[row * 16 : row * 16 + 16, n * 128 : (n + 1) * 128] = first + second
    mels = stem_o.shape[0]
    stem_o[...] = ends[:mels, :]
    row = mels
    for out in vectors:
        for n in range(out.shape[0] // width):
            out[n * width : (n + 1) * width] = ends[row + n : row + n + 1, :].reshape(width)
        row += out.shape[0] // width


def move(block, distance):
    count = lax.axis_size("frames")
    return lax.ppermute(block, "frames", [(d, (d + distance) % count) for d in range(count)])


def swap(block):
    count = lax.axis_size("frames")
    return lax.ppermute(block, "frames", [(d, d ^ 1) for d in range(count)])


def cost(us):
    return pl.CostEstimate(flops=int(us * 1.1e9), bytes_accessed=int(us * 2e6), transcendentals=0)


def call(kernel, outs, args, scratch=(), specs=None, limit=56, us=10, out_specs=None):
    vmem = pl.BlockSpec(memory_space=pltpu.VMEM)
    return pl.pallas_call(
        kernel,
        out_shape=[jax.ShapeDtypeStruct(s, d) for s, d in outs],
        in_specs=specs if specs is not None else [vmem] * len(args),
        out_specs=out_specs if out_specs is not None else [vmem] * len(outs),
        scratch_shapes=list(scratch),
        compiler_params=pltpu.CompilerParams(vmem_limit_bytes=limit * MIB),
        cost_estimate=cost(us),
    )(*args)


def chip_groups():
    chips = lax.axis_size("frames") // 2
    return [[2 * n + core for n in range(chips)] for core in range(2)]


def follow(value, other):
    hbm = pl.BlockSpec(memory_space=pl.ANY)
    return pl.pallas_call(
        lambda value_in, other_in, value_out: None,
        out_shape=jax.ShapeDtypeStruct(value.shape, value.dtype),
        in_specs=[hbm, hbm],
        out_specs=hbm,
        input_output_aliases={0: 0},
        cost_estimate=cost(1),
    )(value, other)


def over_chips(block):
    parts = block.reshape((-1,) + block.shape[2:])
    return lax.all_to_all(parts, "frames", 0, 0, axis_index_groups=chip_groups(), tiled=True)


def local(
    mel_frames, clip_lengths, valid_keys, stem_weight, stem_bias, stride_weight, stride_bias, attn_gain, attn_shift,
    attn_weight, query_bias, value_bias, output_weight, output_bias, mlp_gain, mlp_shift, hidden_weight, hidden_bias,
    return_weight, return_bias, cotangent,
):
    count, width = cotangent.shape
    ff = hidden_weight.shape[1]
    mels = mel_frames.shape[1]
    devices = lax.axis_size("frames")
    device = lax.axis_index("frames")
    core = device % 2
    nb = 2 * SIDE + 1
    ext = count + 2 * PAD
    base = (device - core - 2 * SIDE) * count

    left, right = move(mel_frames[-2:], 1), move(mel_frames[:2], -1)

    smem = pl.BlockSpec(memory_space=pltpu.SMEM)
    vmem = pl.BlockSpec(memory_space=pltpu.VMEM)
    hbm = pl.BlockSpec(memory_space=pl.ANY)
    whole = pltpu.VMEM((count, 128), jnp.int32)
    spans, pack, table, key_plan, query_plan = pl.pallas_call(
        functools.partial(tables_kernel, total=devices * count),
        out_shape=[
            jax.ShapeDtypeStruct(s, d)
            for s, d in (
                ((count, 128), jnp.int32), ((ext, 128), F32), ((count, width), F32), ((16,), jnp.int32), ((16,), jnp.int32)
            )
        ],
        in_specs=[smem] * 3,
        out_specs=[vmem] * 3 + [smem] * 2,
        scratch_shapes=[whole] * 3,
        cost_estimate=cost(4),
    )(device[None].astype(jnp.int32), clip_lengths, valid_keys)

    x, columns, dstem, dstride, layer_in, attn_in = call(
        stem_kernel,
        [
            ((ext, 4 * SLOT), BF), ((count, 3 * width), BF), ((ext, 2 * width), F32), ((count, width), F32), ((count, width), F32),
            ((count, width), BF),
        ],
        (
            mel_frames, left, right, stem_weight, stem_bias, stride_weight, stride_bias, attn_gain, attn_shift, pack, table,
        ),
        [pltpu.VMEM((2 * ext + 16, SLOT), F32), pltpu.VMEM((4 * SLOT, 2 * width), BF), pltpu.VMEM((ext, width), F32)],
        us=7,
    )

    joint = jnp.concatenate([query_bias.astype(F32), jnp.zeros((width,), F32), value_bias.astype(F32)])

    def project(block):
        return (nn(block, attn_weight) + joint).astype(BF)

    def after(value, *others):
        return lax.optimization_barrier((value, *others))[0]

    def gather(block, pair):
        own, sib = {0: project(block)}, {0: project(pair)}
        ends = block, block
        done = [own[0], sib[0]]
        for k in range(1, SIDE + 1):
            ends = move(ends[0], 2), move(ends[1], -2)
            if k == 1:
                ends = after(ends[0], *done), after(ends[1], *done)
            here, there = dict(zip((-k, k), ends)), {n: swap(b) for n, b in zip((-k, k), ends)}
            for n in (-k, k):
                own[n] = project(after(here[n], *(done if k == SIDE else there.values())))
            for n in (-k, k):
                sib[n] = project(after(there[n], own[-k], own[k]))
            done += [v[n] for v in (own, sib) for n in (-k, k)]
        order = range(-SIDE, SIDE + 1)
        return [own[n] for n in order], [sib[n] for n in order]

    pair_in = swap(attn_in)
    own, sib = gather(attn_in, pair_in)
    pair_columns = lax.ppermute(columns, "frames", [(d, d + 1) for d in range(0, devices, 2)])
    reach = 2 * nb * count + KB
    pairs = width // 128
    sems = pltpu.SemaphoreType.DMA((2 * nb, 2))
    count_of = pltpu.SMEM((1,), jnp.int32)

    stacked = pltpu.VMEM((pairs, 2 * QB, 128), BF)
    summed = pltpu.VMEM((pairs, 2 * QB, 128), F32)
    score = pltpu.VMEM((2, pairs, 2 * QB, KB), F32)
    weight = pltpu.VMEM((2, pairs, 2 * QB, KB), BF)
    one_sem = pltpu.SemaphoreType.DMA((1,))
    local_query = pltpu.VMEM((count, width), BF)

    core1 = core[None].astype(jnp.int32)
    bundle = ff + 2 * width + width // 2
    block_f32 = pltpu.VMEM((count, width), F32)
    lse, layer_out, keep, send, grad_middle, pay, dlt, sums1 = call(
        layer_kernel,
        [
            ((count, 128), F32), ((count, width), BF), ((count, bundle), BF), ((count, bundle), BF), ((count, width), F32),
            ((count + 48, width), BF), ((count, 128), F32), ((8, width), F32),
        ],
        (
            key_plan, spans, *own, *sib, layer_in, cotangent, output_weight, hidden_weight, return_weight, output_bias,
            hidden_bias, return_bias, mlp_gain, mlp_shift,
        ),
        [
            block_f32, local_query, pltpu.VMEM((reach, 2 * width), BF), stacked, summed, summed, summed, summed, score, weight,
            count_of, sems, pltpu.SemaphoreType.DMA((6,)),
            block_f32, local_query, pltpu.VMEM((width, width), BF), pltpu.VMEM((width, ff), BF), pltpu.VMEM((ff, width), BF),
            block_f32, block_f32, pltpu.VMEM((2, count, bundle), BF), pltpu.SemaphoreType.DMA((2 * (ff // width) + 6,)),
        ],
        [smem, vmem] + [hbm] * (2 * nb + 5) + [vmem] * 5,
        out_specs=[vmem, vmem, hbm, hbm] + [vmem] * 4,
        us=26,
    )

    got = swap(send)
    near = {-1: move(pay, 2), 1: move(pay, -2)}

    blocks = ff // width
    groups = width // 16
    tiles = (groups, 2, 16 * (blocks * pairs // 2 + 1), 128)

    def at(n):
        return pl.BlockSpec((count, width), lambda i, core: (0, n))

    def each(i, core):
        return (0, jnp.minimum(i, blocks - 1))

    bundle_specs = [
        pl.BlockSpec((count, width), each), at(blocks), at(blocks + 1),
        pl.BlockSpec((count, width // 2), lambda i, core: (0, 2 * (blocks + 2))),
    ]
    mlp_both = pl.pallas_call(
        mlp_weights_kernel,
        out_shape=jax.ShapeDtypeStruct(tiles, BF),
        grid_spec=pltpu.PrefetchScalarGridSpec(
            num_scalar_prefetch=1,
            grid=(blocks + 1,),
            in_specs=bundle_specs * 2,
            out_specs=pl.BlockSpec(tiles, lambda i, core: (0, 0, 0, 0)),
        ),
        compiler_params=pltpu.CompilerParams(vmem_limit_bytes=40 * MIB),
        cost_estimate=cost(5.0),
    )(core1, keep, keep, keep, keep, got, got, got, got)

    near = {k: follow(b, mlp_both) for k, b in near.items()}
    far = {-2: move(near[-1], 2), 2: move(near[1], -2)}
    (grad_query,) = call(
        query_kernel,
        [((count, width), BF)],
        (key_plan, spans, pay, lse, dlt, *own, *sib, near[-1], near[1]),
        [
            local_query, pltpu.VMEM((reach, 2 * width), BF), stacked, stacked, summed, summed, summed, score, score, weight,
            count_of, sems, one_sem,
        ],
        [smem] + [vmem] * 4 + [hbm] * (2 * nb + 2),
        us=15.0,
    )
    travel = {0: pay, **near, **{k: follow(b, grad_query) for k, b in far.items()}}
    sib_pay = {k: swap(travel[k]) for k in travel}
    own_pay, sib_pay = ([v[k] for k in range(-SIDE, SIDE + 1)] for v in (travel, sib_pay))

    mlp_parts = over_chips(mlp_both)
    (mlp_spread,) = call(
        spread_kernel, [(mlp_parts.shape, BF)], (mlp_parts, grad_query), specs=[vmem, hbm], us=3.0
    )
    mlp_mine = over_chips(mlp_spread[:, None]).reshape(tiles)

    grad_projected, gsp, sums2 = call(
        key_kernel,
        [((count, 3 * width), BF), ((count, width), BF), ((8, width), F32)],
        (
            query_plan, spans, grad_query, attn_weight, layer_in, grad_middle, attn_gain,
            dstride, *own, *sib, *own_pay, *sib_pay, mlp_spread,
        ),
        [
            pltpu.VMEM((count, 2 * width), BF), pltpu.VMEM((reach, width), BF), pltpu.VMEM((reach, width), BF),
            pltpu.VMEM((48, reach), BF), pltpu.VMEM((8, reach), F32), pltpu.VMEM((8, reach), F32), stacked, stacked, summed, summed, score, score, weight,
            weight, count_of, sems, pltpu.SemaphoreType.DMA((2 * nb, 1)),
            one_sem,
        ],
        [smem] + [vmem] * 7 + [hbm] * (4 * nb + 1),
        us=18.0,
    )
    left, right = move(gsp[-1:], 1), move(gsp[:1], -1)

    def to_core(n, block):
        return lax.ppermute(block, "frames", [(d + 1 - n, d + n) for d in range(0, devices, 2)])

    gp_pair, gsp_pair = to_core(0, grad_projected), to_core(1, gsp)
    def whole_block(i, core):
        return (0, 0)

    def column_block(i, core):
        return (0, i)

    last_tiles = (groups, 2, 16 * (3 * pairs // 2 + 1), 128)
    last_specs = [pl.BlockSpec((count, width), m) for m in (whole_block, column_block, column_block, whole_block)]
    both = pl.pallas_call(
        last_weights_kernel,
        out_shape=jax.ShapeDtypeStruct(last_tiles, BF),
        grid_spec=pltpu.PrefetchScalarGridSpec(
            num_scalar_prefetch=1,
            grid=(3,),
            in_specs=last_specs * 2,
            out_specs=pl.BlockSpec(last_tiles, lambda i, core: (0, 0, 0, 0)),
        ),
        compiler_params=pltpu.CompilerParams(vmem_limit_bytes=40 * MIB),
        cost_estimate=cost(3),
    )(core1, attn_in, grad_projected, columns, gsp, pair_in, gp_pair, pair_columns, gsp_pair)
    gpre, both = pl.pallas_call(
        stem_back_kernel,
        out_shape=[jax.ShapeDtypeStruct((ext, 2 * width), BF), jax.ShapeDtypeStruct(last_tiles, BF)],
        in_specs=[vmem] * 9 + [hbm],
        out_specs=[vmem, hbm],
        scratch_shapes=[
            pltpu.VMEM((ext + 8, width), F32), pltpu.VMEM((ext, width), BF), pltpu.VMEM((ext, width), BF),
            pltpu.VMEM((3 * mels + 16, width), F32), pltpu.VMEM((groups, 2, 16, 128), BF), one_sem,
        ],
        input_output_aliases={9: 1},
        compiler_params=pltpu.CompilerParams(vmem_limit_bytes=40 * MIB),
        cost_estimate=cost(4),
    )(gsp, left, right, stride_weight, dstem, x, pack, sums1, sums2, both)

    (mel_grad,) = call(
        mel_kernel,
        [((2 * count, mels), F32)],
        (gpre, stem_weight, pack),
        [pltpu.VMEM((4 * SLOT, 2 * width), BF), pltpu.VMEM((ext, 4 * SLOT), F32)],
        us=3,
    )

    grad_return_weight, grad_hidden_weight, grad_output_weight = call(
        unpack_mlp_kernel,
        [((ff, width), F32), ((width, ff), F32), ((width, width), F32)],
        (core1, mlp_mine, swap(mlp_mine)),
        specs=[smem, vmem, vmem],
        us=5,
    )
    parts = over_chips(both)
    (spread,) = call(
        spread_kernel, [(parts.shape, BF)], (parts, mel_grad, grad_output_weight), specs=[vmem, hbm, hbm], us=3
    )
    mine = over_chips(spread[:, None]).reshape(last_tiles)
    sizes = [width] * 9 + [ff, width]
    grad_attn_weight, grad_stride_weight, grad_stem_weight, *bias = call(
        unpack_kernel,
        [((width, 3 * width), F32), ((3 * width, width), F32), ((3 * mels, width), F32)] + [((n,), F32) for n in sizes],
        (core1, mine, swap(mine)),
        [pltpu.VMEM((3 * mels + 16, width), F32)],
        [smem, vmem, vmem],
        us=6,
    )
    return (
        layer_out, mel_grad, grad_stem_weight, bias[0], grad_stride_weight, bias[1], bias[2], bias[3], grad_attn_weight,
        bias[4], bias[5], grad_output_weight, bias[6], bias[7], bias[8], grad_hidden_weight, bias[9],
        grad_return_weight, bias[10],
    )


def solution(mesh):
    split = P("frames", None)
    in_specs = (split,) + (P(),) * 19 + (split,)
    out_specs = (split, split) + (P(),) * 17
    return jax.shard_map(local, mesh=mesh, in_specs=in_specs, out_specs=out_specs, check_vma=False)
```

```python
import functools
import math

import jax
import jax.numpy as jnp
from jax import lax
from jax.experimental import pallas as pl
from jax.experimental.pallas import tpu as pltpu
from jax.sharding import PartitionSpec as P

HEADS = 8
SIDE = 2
QB = 128
KB = 256
PAD = 16
SLOT = 128
NEG = -1e30
BF = jnp.bfloat16
F32 = jnp.float32
MIB = 1 << 20


def nn(a, b):
    return lax.dot_general(a, b, (((1,), (0,)), ((), ())), preferred_element_type=F32)


def nt(a, b):
    return lax.dot_general(a, b, (((1,), (1,)), ((), ())), preferred_element_type=F32)


def tn(a, b):
    return lax.dot_general(a, b, (((0,), (0,)), ((), ())), preferred_element_type=F32)


def gelu_pair(x):
    bell = jnp.exp(-0.5 * x * x)
    t = 1.0 / (1.0 + 0.2316419 * jnp.abs(x))
    poly = 0.127414796 + t * (-0.142248368 + t * (0.7107068705 + t * (-0.7265760135 + t * 0.5307027145)))
    tail = bell * t * poly
    phi = jnp.where(x >= 0, 1.0 - tail, tail)
    return x * phi, phi + 0.3989422804 * x * bell


def norm_parts(x):
    center = jnp.mean(x, axis=-1, keepdims=True)
    centered = x - center
    rstd = lax.rsqrt(jnp.mean(centered * centered, axis=-1, keepdims=True) + 1e-05)
    return centered * rstd, rstd


def norm_back(grad, xhat, rstd, gain):
    inner = grad * gain
    m1 = jnp.mean(inner, axis=-1, keepdims=True)
    m2 = jnp.mean(inner * xhat, axis=-1, keepdims=True)
    return rstd * (inner - m1 - xhat * m2)


def vector(ref):
    return ref[...].astype(F32).reshape(1, -1)


def colsum(x):
    return jnp.sum(x, axis=0, keepdims=True)


def halves(x, low):
    zero = jnp.zeros_like(x)
    return jnp.concatenate([jnp.where(low, x, zero), jnp.where(low, zero, x)], axis=0)


def pick(x, low):
    return jnp.where(low, x[:QB], x[QB:])


def wide(x):
    return jnp.concatenate([x, x], axis=1)


def tall(x):
    return jnp.concatenate([x, x], axis=0)


def tables_kernel(device, lengths, valids, spans_o, pack_o, table_o, keys_o, queries_o, start_s, length_s, valid_s, *, total):
    count, width = table_o.shape
    base = (device[0] - device[0] % 2 - 2 * SIDE) * count
    first = device[0] * count
    token = first + lax.broadcasted_iota(jnp.int32, (count, 128), 0)
    row = lax.broadcasted_iota(jnp.int32, pack_o.shape, 0) + lax.broadcasted_iota(jnp.int32, pack_o.shape, 1) - PAD
    here = (row >= 0) & (row <= count) & (first + row < total)
    pack_o[...] = jnp.where(here, 1.0, 0.0)
    keys_o[0] = queries_o[0] = device[0] % 2

    def clip(c, start):
        length = lengths[c]
        valid = jnp.minimum(valids[c], length)
        end = start + length

        @pl.when((start < first + count) & (end > first))
        def _():
            inside = (token >= start) & (token < end)
            start_s[...] = jnp.where(inside, start, start_s[...])
            length_s[...] = jnp.where(inside, length, length_s[...])
            valid_s[...] = jnp.where(inside, valid, valid_s[...])
            for n in range(count // QB):
                at = first + n * QB

                @pl.when((start <= at) & (at < end))
                def _():
                    keys_o[4 + 2 * n] = queries_o[4 + 2 * n] = ((start - base) >> 7) << 7

                @pl.when((start < at + QB) & (at + QB <= end))
                def _():
                    keys_o[5 + 2 * n] = start + valid - base
                    queries_o[5 + 2 * n] = end - base

        @pl.when((start >= first) & (start <= first + count))
        def _():
            pack_o[...] = jnp.where(first + row == start, 0.0, pack_o[...])

        return end

    lax.fori_loop(0, lengths.shape[0], clip, 0)
    for plan in (keys_o, queries_o):
        low, high = plan[4], 0
        for n in range(count // QB):
            steps = (plan[5 + 2 * n] - plan[4 + 2 * n] + KB - 1) // KB
            plan[5 + 2 * n] = steps
            low = jnp.minimum(low, plan[4 + 2 * n])
            high = jnp.maximum(high, plan[4 + 2 * n] + steps * KB)
        plan[1], plan[2] = low, high
    lane = lax.broadcasted_iota(jnp.int32, (count, 128), 1)
    key_lo = start_s[...] - base
    position = token - start_s[...]
    is_key = position < valid_s[...]
    query_lo = jnp.where(is_key, key_lo, 1 << 20)
    query_hi = jnp.where(is_key, key_lo + length_s[...], 0)
    first_two = jnp.where(lane == 0, key_lo, key_lo + valid_s[...])
    spans_o[...] = jnp.where(lane < 2, first_two, jnp.where(lane == 2, query_lo, query_hi))
    half = width // 2
    number = lax.broadcasted_iota(jnp.int32, (1, half), 1).astype(F32)
    rates = jnp.exp(number * (-math.log(10000.0) / (half - 1)))
    angles = wide(position.astype(F32)) * rates
    table_o[:, :half] = jnp.sin(angles)
    table_o[:, half:] = jnp.cos(angles)


def taps_of(wbig, sw):
    mels, width = sw.shape[0] // 3, sw.shape[1]
    wbig[...] = jnp.zeros_like(wbig)
    for t in range(3):
        tap = sw[t * mels : (t + 1) * mels, :]
        wbig[t * SLOT : t * SLOT + mels, :width] = tap
        wbig[(t + 1) * SLOT : (t + 1) * SLOT + mels, width:] = tap


def stem_kernel(
    mel, left, right, sw, sbias, vw, vbias, gain, shift, pack, table,
    x_o, cols_o, dstem_o, dstride_o, lin_o, ain_o, m, wbig, shifted,
):
    count, width = lin_o.shape
    frames, mels = mel.shape
    ext = x_o.shape[0]
    taps_of(wbig, sw)
    top = 2 * PAD + 8
    m[...] = jnp.zeros_like(m)
    m[top : top + frames, :mels] = mel[...].astype(F32)
    m[top - 2 : top, :mels] = left[...].astype(F32)
    m[top + frames : top + frames + 2, :mels] = right[...].astype(F32)
    opn, opn_next = pack[:, 0:1], pack[:, 1:2]
    x_o[:, :SLOT] = (m[pl.ds(7, ext, stride=2), :] * opn).astype(BF)
    x_o[:, SLOT : 2 * SLOT] = m[pl.ds(8, ext, stride=2), :].astype(BF)
    x_o[:, 2 * SLOT : 3 * SLOT] = m[pl.ds(9, ext, stride=2), :].astype(BF)
    x_o[:, 3 * SLOT :] = (m[pl.ds(10, ext, stride=2), :] * opn_next).astype(BF)
    inner = slice(PAD, PAD + count)
    even, odd = slice(0, width), slice(width, 2 * width)
    act, dact = gelu_pair(nn(x_o[...], wbig[:, even]) + vector(sbias))
    dstem_o[:, even] = dact
    cols_o[:, width : 2 * width] = act[inner].astype(BF)
    act, dact = gelu_pair(nn(x_o[...], wbig[:, odd]) + vector(sbias))
    dstem_o[:, odd] = dact
    cols_o[:, 2 * width :] = act[inner].astype(BF)
    shifted[...] = act
    cols_o[:, :width] = (shifted[PAD - 1 : PAD + count - 1, :] * pack[inner, 0:1]).astype(BF)
    pre = nn(cols_o[...], vw[...]) + vector(vbias)
    act2, dact2 = gelu_pair(pre)
    dstride_o[...] = dact2
    lin = act2 + table[...]
    lin_o[...] = lin
    xhat, _ = norm_parts(lin)
    ain_o[...] = (xhat * vector(gain) + vector(shift)).astype(BF)


def needed(sc, block, count):
    return (block * count < sc[2]) & ((block + 1) * count > sc[1])


def start_copies(sc, pairs, sem, count, begun, upto):
    for block, copies in pairs:

        @pl.when(needed(sc, block, count) & (block >= begun[0]) & (block < upto))
        def _():
            for m, (src, dst) in enumerate(copies):
                pltpu.make_async_copy(src, dst, sem.at[block, m]).start()

    begun[0] = jnp.maximum(begun[0], upto)


def wait_until(sc, end, copies, sem, count, there, ahead=None):
    def one(block, _):
        @pl.when(needed(sc, block, count))
        def _():
            for m, (src, dst) in enumerate(copies(block)):
                pltpu.make_async_copy(src, dst, sem.at[block, m]).wait()

        return 0

    upto = jnp.minimum((end + count - 1) // count, 2 * (2 * SIDE + 1))
    if ahead is not None:

        @pl.when(upto > there[0])
        def _():
            ahead(upto + 2)

    lax.fori_loop(there[0], upto, one, 0)
    there[0] = jnp.maximum(there[0], upto)


def window(sc, own, sib):
    core = sc[0]
    out = []
    for k in range(2 * SIDE + 1):
        out += [(2 * k + core, own[k]), (2 * k + 1 - core, sib[k])]
    return out


def rows_of(block, count):
    return pl.ds(pl.multiple_of(block * count, count), count)


def in_range(lo, hi, start):
    col = start + lax.broadcasted_iota(jnp.int32, (QB, KB), 1)
    return jnp.where((col >= lo) & (col < hi), 0.0, NEG)


def chunks(first, steps, step, wait):
    def two(n, _):
        wait(first + (2 * n + 2) * KB)
        step(2 * n, 2)
        return 0

    lax.fori_loop(0, steps // 2, two, 0)

    @pl.when(steps % 2 == 1)
    def _():
        wait(first + steps * KB)
        step(steps - 1, 1)


def layer_kernel(*refs):
    nb = 2 * SIDE + 1
    sc, span_ref = refs[:2]
    own, sib = refs[2 : 2 + nb], refs[2 + nb : 2 + 2 * nb]
    at = 2 + 2 * nb
    fetched, vectors, outs = refs[at : at + 5], refs[at + 5 : at + 10], refs[at + 10 : at + 18]
    lse_o = outs[0]
    scratch = refs[at + 18 :]
    ctx_o, local_ref, kv, q2, acc, peak, total, scale, s, e, there, begun, sem, sem2 = scratch[:14]
    held, mlp_scratch = scratch[14:19], scratch[19:]
    count, width = ctx_o.shape
    late = [pltpu.make_async_copy(src, dst, sem2.at[1 + n]) for n, (src, dst) in enumerate(zip(fetched, held))]
    span = 2 * nb * count
    pairs = width // 128
    kv[span:, :] = jnp.zeros((kv.shape[0] - span, 2 * width), BF)
    there[0] = 0

    def copies(block, src=own[0]):
        return [(src.at[:, pl.ds(width, 2 * width)], kv.at[rows_of(block, count), :])]

    local = pltpu.make_async_copy(own[SIDE].at[:, pl.ds(0, width)], local_ref, sem2.at[0])
    local.start()
    begun[0] = 0
    sources = [(block, copies(block, src)) for block, src in window(sc, own, sib)]

    def ahead(upto):
        start_copies(sc, sources, sem, count, begun, upto)

    ahead(sc[1] // count + 3)
    for copy in late:
        copy.start()
    local.wait()

    def wait(end):
        wait_until(sc, end, copies, sem, count, there, ahead)

    low = lax.broadcasted_iota(jnp.int32, (QB, 128), 1) < 64
    lanes = lax.broadcasted_iota(jnp.int32, (QB, 128), 1)

    def one(i, _):
        rows = pl.ds(pl.multiple_of(i * QB, QB), QB)
        for p in range(pairs):
            q2[p] = halves(local_ref[rows, p * 128 : (p + 1) * 128], low) * jnp.asarray(0.125, BF)
            acc[p] = jnp.zeros_like(acc[p])
            peak[p] = jnp.full_like(peak[p], NEG)
            total[p] = jnp.zeros_like(total[p])
        lo, hi = span_ref[rows, 0:1], span_ref[rows, 1:2]

        def step(n, parts):
            start = sc[4 + 2 * i] + n * KB
            keys = [pl.ds(pl.multiple_of(start + u * KB, 128), KB) for u in range(parts)]
            for u in range(parts):
                bias = tall(in_range(lo, hi, start + u * KB))
                for p in range(pairs):
                    s[u, p] = nt(q2[p], kv[keys[u], p * 128 : (p + 1) * 128]) + bias
            for p in range(pairs):
                best = functools.reduce(jnp.maximum, [s[u, p] for u in range(parts)])
                old = peak[p]
                top = jnp.maximum(old, jnp.max(best, axis=1, keepdims=True))
                peak[p] = top
                scale[p] = jnp.exp(old - top)
            for p in range(pairs):
                total[p] = scale[p] * total[p]
                for u in range(parts):
                    grown = jnp.exp(s[u, p] - wide(peak[p]))
                    e[u, p] = grown.astype(BF)
                    total[p] = total[p] + (grown[:, :128] + grown[:, 128:])
            for p in range(pairs):
                value = [kv[keys[u], width + p * 128 : width + (p + 1) * 128] for u in range(parts)]
                acc[p] = scale[p] * acc[p] + functools.reduce(jnp.add, [nn(e[u, p], value[u]) for u in range(parts)])

        chunks(sc[4 + 2 * i], sc[5 + 2 * i], step, wait)
        lse = jnp.zeros((QB, 128), F32)
        for p in range(pairs):
            row_total = jnp.sum(total[p], axis=1, keepdims=True)
            ctx_o[rows, p * 128 : (p + 1) * 128] = pick(acc[p] / row_total, low)
            both = peak[p] + jnp.log(row_total)
            lse = jnp.where(lanes == 2 * p, both[:QB], lse)
            lse = jnp.where(lanes == 2 * p + 1, both[QB:], lse)
        lse_o[rows, :] = lse
        return 0

    lax.fori_loop(0, count // QB, one, 0)
    wait(span)
    for copy in late:
        copy.wait()
    mlp(sc, ctx_o, lse_o, *held, *vectors, *outs[1:], *mlp_scratch)


def query_kernel(*refs):
    nb = 2 * SIDE + 1
    sc, span_ref, pay_ref, lse_ref, dlt_ref = refs[:5]
    own, sib = refs[5 : 5 + nb], refs[5 + nb : 5 + 2 * nb]
    dq_o, local_ref, kv, q2, do2, acc, lse2, dlt2, s, d, ds, there, begun, sem, sem2 = refs[7 + 2 * nb :]
    count, width = dq_o.shape
    span = 2 * nb * count
    pairs = width // 128
    kv[span:, :] = jnp.zeros((kv.shape[0] - span, 2 * width), BF)
    there[0] = 0

    def copies(block, src=own[0]):
        return [(src.at[:, pl.ds(width, 2 * width)], kv.at[rows_of(block, count), :])]

    local = pltpu.make_async_copy(own[SIDE].at[:, pl.ds(0, width)], local_ref, sem2.at[0])
    local.start()
    begun[0] = 0
    sources = [(block, copies(block, src)) for block, src in window(sc, own, sib)]

    def ahead(upto):
        start_copies(sc, sources, sem, count, begun, upto)

    ahead(sc[1] // count + 3)
    local.wait()

    def wait(end):
        wait_until(sc, end, copies, sem, count, there, ahead)

    low = lax.broadcasted_iota(jnp.int32, (QB, 128), 1) < 64

    def one(i, _):
        rows = pl.ds(pl.multiple_of(i * QB, QB), QB)
        lse, dlt = lse_ref[rows, :], dlt_ref[rows, :]
        for p in range(pairs):
            q2[p] = halves(local_ref[rows, p * 128 : (p + 1) * 128], low) * jnp.asarray(0.125, BF)
            do2[p] = halves(pay_ref[rows, p * 128 : (p + 1) * 128], low)
            acc[p] = jnp.zeros_like(acc[p])
            for h in range(2):
                part = pl.ds(h * QB, QB)
                lse2[p, part, :] = jnp.broadcast_to(lse[:, 2 * p + h : 2 * p + h + 1], (QB, 128))
                dlt2[p, part, :] = jnp.broadcast_to(dlt[:, 2 * p + h : 2 * p + h + 1], (QB, 128))
        lo, hi = span_ref[rows, 0:1], span_ref[rows, 1:2]

        def step(n, parts):
            start = sc[4 + 2 * i] + n * KB
            keys = [pl.ds(pl.multiple_of(start + u * KB, 128), KB) for u in range(parts)]
            for u in range(parts):
                bias = tall(in_range(lo, hi, start + u * KB))
                for p in range(pairs):
                    s[u, p] = nt(q2[p], kv[keys[u], p * 128 : (p + 1) * 128]) + bias
                    d[u, p] = nt(do2[p], kv[keys[u], width + p * 128 : width + (p + 1) * 128])
            for u in range(parts):
                for p in range(pairs):
                    e = jnp.exp(s[u, p] - wide(lse2[p]))
                    ds[u, p] = (e * (d[u, p] - wide(dlt2[p]))).astype(BF)
            for p in range(pairs):
                more = [nn(ds[u, p], kv[keys[u], p * 128 : (p + 1) * 128]) for u in range(parts)]
                acc[p] = acc[p] + functools.reduce(jnp.add, more)

        chunks(sc[4 + 2 * i], sc[5 + 2 * i], step, wait)
        for p in range(pairs):
            dq_o[rows, p * 128 : (p + 1) * 128] = (pick(acc[p], low) * 0.125).astype(BF)
        return 0

    lax.fori_loop(0, count // QB, one, 0)
    wait(span)


def key_kernel(*refs):
    nb = 2 * SIDE + 1
    sc, span_ref, dq_ref, w_ref, lin_ref, gm_ref, gain, dstride_ref = refs[:8]
    own, sib = refs[8 : 8 + nb], refs[8 + nb : 8 + 2 * nb]
    ownp, sibp = refs[8 + 2 * nb : 8 + 3 * nb], refs[8 + 3 * nb : 8 + 4 * nb]
    gp_o, gsp_o, sums_o, kvl, q, do, stat, lse, dlt, k2, v2, dk, dv, s, d, e, ds, there, begun, sem, sem2, sem3 = refs[9 + 4 * nb :]
    count, width = gsp_o.shape
    span = 2 * nb * count
    pairs = width // 128
    rest = q.shape[0] - span
    q[span:, :] = jnp.zeros((rest, width), BF)
    do[span:, :] = jnp.zeros((rest, width), BF)
    stat[:, span:] = jnp.zeros((stat.shape[0], rest), BF)
    there[0] = 0

    def copies(block, src=own[0], pay=ownp[0]):
        return [
            (src.at[:, pl.ds(0, width)], q.at[rows_of(block, count), :]),
            (pay.at[pl.ds(0, count), :], do.at[rows_of(block, count), :]),
        ]

    def side(block, pay=ownp[0]):
        return [(pay.at[pl.ds(count, 48), pl.ds(0, count)], stat.at[:, rows_of(block, count)])]

    local = pltpu.make_async_copy(own[SIDE].at[:, pl.ds(width, 2 * width)], kvl, sem3.at[0])
    local.start()
    pairs_of = list(zip(window(sc, own, sib), window(sc, ownp, sibp)))
    begun[0] = 0
    start_copies(sc, [(block, side(block, pay)) for _, (block, pay) in pairs_of], sem2, count, begun, 2 * nb)
    begun[0] = 0
    sources = [(block, copies(block, src, pay)) for (block, src), (_, pay) in pairs_of]

    def ahead(upto):
        start_copies(sc, sources, sem, count, begun, upto)

    ahead(sc[1] // count + 3)

    def wait(end):
        wait_until(sc, end, copies, sem, count, there, ahead)

    local.wait()
    wait_until(sc, span, side, sem2, count, there)
    there[0] = 0
    lse[...] = stat[0:8, :].astype(F32) + stat[8:16, :].astype(F32) + stat[16:24, :].astype(F32)
    dlt[...] = stat[24:32, :].astype(F32) + stat[32:40, :].astype(F32) + stat[40:48, :].astype(F32)
    low = lax.broadcasted_iota(jnp.int32, (QB, 128), 1) < 64

    def one(i, _):
        rows = pl.ds(pl.multiple_of(i * QB, QB), QB)
        for p in range(pairs):
            k2[p] = halves(kvl[rows, p * 128 : (p + 1) * 128], low) * jnp.asarray(0.125, BF)
            v2[p] = halves(kvl[rows, width + p * 128 : width + (p + 1) * 128], low)
            dk[p] = jnp.zeros_like(dk[p])
            dv[p] = jnp.zeros_like(dv[p])
        lo, hi = span_ref[rows, 2:3], span_ref[rows, 3:4]

        def step(n, parts):
            start = sc[4 + 2 * i] + n * KB
            queries = [pl.ds(pl.multiple_of(start + u * KB, 128), KB) for u in range(parts)]
            for u in range(parts):
                for p in range(pairs):
                    lanes = slice(p * 128, (p + 1) * 128)
                    s[u, p] = nt(k2[p], q[queries[u], lanes])
                    d[u, p] = nt(v2[p], do[queries[u], lanes])
            for u in range(parts):
                bias = in_range(lo, hi, start + u * KB)
                for p in range(pairs):
                    for h in range(2):
                        part = slice(h * QB, (h + 1) * QB)
                        head = slice(2 * p + h, 2 * p + h + 1)
                        grown = jnp.exp(s[u, p, part] + (bias - lse[head, queries[u]]))
                        e[u, p, part] = grown.astype(BF)
                        ds[u, p, part] = (grown * (d[u, p, part] - dlt[head, queries[u]])).astype(BF)
            for p in range(pairs):
                lanes = slice(p * 128, (p + 1) * 128)
                dv[p] = dv[p] + functools.reduce(jnp.add, [nn(e[u, p], do[queries[u], lanes]) for u in range(parts)])
                dk[p] = dk[p] + functools.reduce(jnp.add, [nn(ds[u, p], q[queries[u], lanes]) for u in range(parts)])

        chunks(sc[4 + 2 * i], sc[5 + 2 * i], step, wait)
        for p in range(pairs):
            gp_o[rows, width + p * 128 : width + (p + 1) * 128] = (pick(dk[p], low) * 0.125).astype(BF)
            gp_o[rows, 2 * width + p * 128 : 2 * width + (p + 1) * 128] = pick(dv[p], low).astype(BF)
        return 0

    lax.fori_loop(0, count // QB, one, 0)
    wait(span)
    gp_o[:, :width] = dq_ref[...]
    grad = nt(gp_o[...], w_ref[...])
    xhat, rstd = norm_parts(lin_ref[...])
    total = gm_ref[...] + norm_back(grad, xhat, rstd, vector(gain))
    gsp_o[...] = (total * dstride_ref[...]).astype(BF)
    sums_o[0:1, :] = colsum(grad * xhat)
    sums_o[1:2, :] = colsum(grad)
    sums_o[2:3, :] = colsum(gp_o[:, :width].astype(F32))
    sums_o[3:4, :] = colsum(gp_o[:, 2 * width :].astype(F32))
    sums_o[4:8, :] = jnp.zeros((4, width), F32)


def pieces(x, n):
    out = []
    for _ in range(n):
        part = x.astype(BF)
        out.append(part)
        x = x - part.astype(F32)
    return out


def mlp(
    core, ctx, lse, lin, dy, wo, w1, w2, bo, b1, b2, gain_ref, shift,
    out_o, keep_o, send_o, gm_o, pay_o, dlt_o, sums_o, out_acc, gmi_acc, roles, sem,
):
    count, width = lin.shape
    ff = w1.shape[1]

    copies = []

    def give(role, at, size, value):
        cols = slice(at, at + size)
        roles[role, :, cols] = value
        number = len(copies)
        source = roles.at[role, :, pl.ds(at, size)]
        here = pltpu.make_async_copy(source, keep_o.at[:, pl.ds(at, size)], sem.at[number])
        there = pltpu.make_async_copy(source, send_o.at[:, pl.ds(at, size)], sem.at[number])
        copies.append(here)

        @pl.when(core[0] == role)
        def _():
            here.start()

        @pl.when(core[0] != role)
        def _():
            there.start()

        return roles.at[role, :, cols]

    context = ctx[...]
    ctx_b = context.astype(BF)
    for role in range(2):
        give(role, ff + 2 * width, width // 2, ctx_b[:, role * width // 2 : (role + 1) * width // 2])
    give(0, ff, width, dy[...])
    middle = lin[...] + nn(ctx_b, wo[...]) + vector(bo)
    xhat, rstd = norm_parts(middle)
    gain = vector(gain_ref)
    mi = give(1, ff, width, (xhat * gain + vector(shift)).astype(BF))
    grad_out = dy[...].astype(F32)
    sums_o[7:8, :] = colsum(grad_out)
    for f in range(ff // width):
        cols = slice(f * width, (f + 1) * width)
        act, dact = gelu_pair(nn(mi[...], w1[:, cols]) + vector(b1.at[cols]))
        act = give(0, f * width, width, act.astype(BF))
        ghp = (nt(dy[...], w2[cols, :]) * dact).astype(BF)
        ghp_ref = give(1, f * width, width, ghp)
        sums_o[3 + f : 4 + f, :] = colsum(ghp.astype(F32))
        more = nn(act[...], w2[cols, :])
        gmore = nt(ghp_ref[...], w1[:, cols])
        if f == 0:
            out_acc[...] = middle + vector(b2) + more
            gmi_acc[...] = gmore
        else:
            out_acc[...] = out_acc[...] + more
            gmi_acc[...] = gmi_acc[...] + gmore
    out_o[...] = out_acc[...].astype(BF)
    gmi = gmi_acc[...]
    sums_o[1:2, :] = colsum(gmi * xhat)
    sums_o[2:3, :] = colsum(gmi)
    grad_middle = grad_out + norm_back(gmi, xhat, rstd, gain)
    gm_o[...] = grad_middle
    branch = grad_middle.astype(BF)
    for role in range(2):
        give(role, ff + width, width, branch)
    sums_o[0:1, :] = colsum(branch.astype(F32))
    gctx = nt(branch, wo[...]).astype(BF)
    pay_o[:count, :] = gctx
    prod = pieces(gctx.astype(F32) * context, 3)
    head = width // HEADS

    def is_head(shape, feature, number):
        feature, number = (lax.broadcasted_iota(jnp.int32, shape, n) for n in (feature, number))
        return jnp.where(feature // head == number, 1.0, 0.0).astype(BF)

    onehot, onehot_t = is_head((width, 128), 0, 1), is_head((16, width), 1, 0)
    eye = lax.broadcasted_iota(jnp.int32, (16, 128), 0) == lax.broadcasted_iota(jnp.int32, (16, 128), 1)
    eye = jnp.where(eye, 1.0, 0.0).astype(BF)
    dlt_o[...] = nn(prod[0], onehot) + nn(prod[1], onehot) + nn(prod[2], onehot)
    across = nt(onehot_t, prod[0]) + nt(onehot_t, prod[1]) + nt(onehot_t, prod[2])
    pay_o[count:, :] = jnp.zeros((48, width), BF)
    lse_t = [nt(eye, part)[:8].astype(BF) for part in pieces(lse[...], 3)]
    pay_o[count : count + 24, :count] = jnp.concatenate(lse_t, axis=0)
    pay_o[count + 24 : count + 48, :count] = jnp.concatenate(pieces(across[:8], 3), axis=0)
    for copy in copies:
        copy.wait()


def put_tiles(out, block, value):
    groups = out.shape[0]
    for n in range(value.shape[1] // 128):
        tile = block * (value.shape[1] // 128) + n
        each = (out.shape[2] - 16) // 16
        rows = pl.ds(pl.multiple_of(tile % each * 16, 16), 16)
        out[:, tile // each, rows, :] = value[:, n * 128 : (n + 1) * 128].astype(BF).reshape(groups, 16, 128)


def put_last(out, value):
    lanes = value.shape[1] // 128
    for row in range(value.shape[0] // 16):
        for n in range(lanes):
            chip = row * lanes + n
            tile = value[row * 16 : (row + 1) * 16, n * 128 : (n + 1) * 128]
            out[chip // 2, chip % 2, out.shape[2] - 16 :, :] = tile.astype(BF)


def mlp_weights_kernel(core, big, small, branch, ctx, big2, small2, branch2, ctx2, *rest):
    out_o = rest[-1]
    step = pl.program_id(0)
    last = step == pl.num_programs(0) - 1

    @pl.when(jnp.logical_not(last) & (core[0] == 0))
    def _():
        put_tiles(out_o, step, tn(big[...], small[...]) + tn(big2[...], small2[...]))

    @pl.when(jnp.logical_not(last) & (core[0] != 0))
    def _():
        put_tiles(out_o, step, tn(small[...], big[...]) + tn(small2[...], big2[...]))

    @pl.when(last)
    def _():
        put_last(out_o, tn(ctx[...], branch[...]) + tn(ctx2[...], branch2[...]))


def last_weights_kernel(core, ain, gp, columns, gsp, ain2, gp2, columns2, gsp2, out_o):
    step = pl.program_id(0)

    @pl.when(core[0] == 0)
    def _():
        put_tiles(out_o, step, tn(ain[...], gp[...]) + tn(ain2[...], gp2[...]))

    @pl.when(core[0] != 0)
    def _():
        put_tiles(out_o, step, tn(columns[...], gsp[...]) + tn(columns2[...], gsp2[...]))


def stem_back_kernel(gsp, left, right, vw, dstem, x, pack, sums1, sums2, rows_in, gpre, rows_o, g, gext, gup, stem, tiles, sem):
    count, width = gsp.shape
    ext = gext.shape[0]
    inner = slice(PAD, PAD + count)
    even, odd = slice(0, width), slice(width, 2 * width)
    g[...] = jnp.zeros_like(g)
    g[inner, :] = gsp[...].astype(F32)
    g[PAD - 1 : PAD, :] = left[...].astype(F32)
    g[PAD + count : PAD + count + 1, :] = right[...].astype(F32)
    gext[...] = g[:ext, :].astype(BF)
    gup[...] = (g[1 : ext + 1, :] * pack[:, 1:2]).astype(BF)
    gpre[:, even] = (nt(gext[...], vw[width : 2 * width, :]) * dstem[:, even]).astype(BF)
    grad_odd = nt(gext[...], vw[2 * width :, :]) + nt(gup[...], vw[:width, :])
    gpre[:, odd] = (grad_odd * dstem[:, odd]).astype(BF)
    taps = tn(x[inner, : 3 * SLOT], gpre[inner, even]) + tn(x[inner, SLOT:], gpre[inner, odd])
    mels = (stem.shape[0] - 16) // 3
    for t in range(3):
        stem[t * mels : (t + 1) * mels, :] = taps[t * SLOT : t * SLOT + mels, :]
    stem_sum = colsum(gpre[inner, even].astype(F32)) + colsum(gpre[inner, odd].astype(F32))
    stride_sum = colsum(gsp[...].astype(F32))
    rows = [stem_sum, stride_sum, sums2[0:4, :], sums1[...], jnp.zeros((2, width), F32)]
    stem[3 * mels :, :] = jnp.concatenate(rows, axis=0)
    put_last(tiles, stem[...])
    share = rows_o.shape[2]
    copy = pltpu.make_async_copy(tiles, rows_o.at[:, :, pl.ds(share - 16, 16), :], sem.at[0])
    copy.start()
    copy.wait()


def mel_kernel(gpre, sw, pack, mel_o, wbig, gx):
    count = mel_o.shape[0] // 2
    mels = mel_o.shape[1]
    inner = slice(PAD, PAD + count)
    taps_of(wbig, sw)
    gx[...] = nt(gpre[...], wbig[...])
    on_even = gx[inner, SLOT : 2 * SLOT] + pack[inner, 0:1] * gx[PAD - 1 : PAD + count - 1, 3 * SLOT :]
    on_odd = gx[inner, 2 * SLOT : 3 * SLOT] + pack[inner, 1:2] * gx[PAD + 1 : PAD + count + 1, :SLOT]
    mel_o[pl.ds(0, count, stride=2), :] = on_even[:, :mels]
    mel_o[pl.ds(1, count, stride=2), :] = on_odd[:, :mels]


def summed(parts):
    def more(n, total):
        return total + parts[n].astype(F32)

    return lax.fori_loop(1, parts.shape[0], more, parts[0].astype(F32)).astype(BF)


def spread_kernel(parts, *rest):
    out_o = rest[-1]
    total = summed(parts)

    def put(n, _):
        out_o[n] = total
        return 0

    lax.fori_loop(0, out_o.shape[0], put, 0)


def both_halves(core, mine, theirs, group, part, rows):
    a, b = mine[group, part, rows, :].astype(F32), theirs[group, part, rows, :].astype(F32)
    return jnp.where(core[0] == 0, a, b), jnp.where(core[0] == 0, b, a)


def unpack_mlp_kernel(core, mine, theirs, return_o, hidden_o, output_o):
    width = return_o.shape[1]
    lanes = width // 128
    each = (mine.shape[2] - 16) // 16

    def one(group, _):
        for tile in range(2 * each):
            rows = slice(tile % each * 16, tile % each * 16 + 16)
            first, second = both_halves(core, mine, theirs, group, tile // each, rows)
            block, n = divmod(tile, lanes)
            here = pl.ds(pl.multiple_of(block * width + group * 16, 16), 16)
            return_o[here, n * 128 : (n + 1) * 128] = first
            here = pl.ds(pl.multiple_of(group * 16, 16), 16)
            hidden_o[here, block * width + n * 128 : block * width + (n + 1) * 128] = second
        return 0

    lax.fori_loop(0, width // 16, one, 0)
    half = width // 2

    def last(row, _):
        for n in range(lanes):
            chip = slice(each * 16, each * 16 + 16)
            first, second = both_halves(core, mine, theirs, row * (lanes // 2) + n // 2, n % 2, chip)
            output_o[pl.ds(pl.multiple_of(row * 16, 16), 16), n * 128 : (n + 1) * 128] = first
            output_o[pl.ds(pl.multiple_of(half + row * 16, 16), 16), n * 128 : (n + 1) * 128] = second
        return 0

    lax.fori_loop(0, half // 16, last, 0)


def unpack_kernel(core, mine, theirs, attn_o, stride_o, stem_o, *rest):
    vectors, ends = rest[:-1], rest[-1]
    width = stride_o.shape[1]
    lanes = width // 128
    each = (mine.shape[2] - 16) // 16

    def run(first_of, second_of):
        def one(group, _):
            at = group * 16
            for tile in range(2 * each):
                rows = slice(tile % each * 16, tile % each * 16 + 16)
                first = first_of[group, tile // each, rows, :].astype(F32)
                second = second_of[group, tile // each, rows, :].astype(F32)
                attn_o[pl.ds(pl.multiple_of(at, 16), 16), tile * 128 : (tile + 1) * 128] = first
                block, n = divmod(tile, lanes)
                stride_o[pl.ds(pl.multiple_of(block * width + at, 16), 16), n * 128 : (n + 1) * 128] = second
            return 0

        lax.fori_loop(0, mine.shape[0], one, 0)

    @pl.when(core[0] == 0)
    def _():
        run(mine, theirs)

    @pl.when(core[0] != 0)
    def _():
        run(theirs, mine)

    last = slice(each * 16, each * 16 + 16)
    for row in range(ends.shape[0] // 16):
        for n in range(lanes):
            chip = row * lanes + n
            first, second = both_halves(core, mine, theirs, chip // 2, chip % 2, last)
            ends[row * 16 : row * 16 + 16, n * 128 : (n + 1) * 128] = first + second
    mels = stem_o.shape[0]
    stem_o[...] = ends[:mels, :]
    row = mels
    for out in vectors:
        for n in range(out.shape[0] // width):
            out[n * width : (n + 1) * width] = ends[row + n : row + n + 1, :].reshape(width)
        row += out.shape[0] // width


def move(block, distance):
    count = lax.axis_size("frames")
    return lax.ppermute(block, "frames", [(d, (d + distance) % count) for d in range(count)])


def swap(block):
    count = lax.axis_size("frames")
    return lax.ppermute(block, "frames", [(d, d ^ 1) for d in range(count)])


def cost(us):
    return pl.CostEstimate(flops=int(us * 1.1e9), bytes_accessed=int(us * 2e6), transcendentals=0)


def call(kernel, outs, args, scratch=(), specs=None, limit=56, us=10, out_specs=None):
    vmem = pl.BlockSpec(memory_space=pltpu.VMEM)
    return pl.pallas_call(
        kernel,
        out_shape=[jax.ShapeDtypeStruct(s, d) for s, d in outs],
        in_specs=specs if specs is not None else [vmem] * len(args),
        out_specs=out_specs if out_specs is not None else [vmem] * len(outs),
        scratch_shapes=list(scratch),
        compiler_params=pltpu.CompilerParams(vmem_limit_bytes=limit * MIB),
        cost_estimate=cost(us),
    )(*args)


def chip_groups():
    chips = lax.axis_size("frames") // 2
    return [[2 * n + core for n in range(chips)] for core in range(2)]


def follow(value, other):
    hbm = pl.BlockSpec(memory_space=pl.ANY)
    return pl.pallas_call(
        lambda value_in, other_in, value_out: None,
        out_shape=jax.ShapeDtypeStruct(value.shape, value.dtype),
        in_specs=[hbm, hbm],
        out_specs=hbm,
        input_output_aliases={0: 0},
        cost_estimate=cost(1),
    )(value, other)


def over_chips(block):
    parts = block.reshape((-1,) + block.shape[2:])
    return lax.all_to_all(parts, "frames", 0, 0, axis_index_groups=chip_groups(), tiled=True)


def local(
    mel_frames, clip_lengths, valid_keys, stem_weight, stem_bias, stride_weight, stride_bias, attn_gain, attn_shift,
    attn_weight, query_bias, value_bias, output_weight, output_bias, mlp_gain, mlp_shift, hidden_weight, hidden_bias,
    return_weight, return_bias, cotangent,
):
    count, width = cotangent.shape
    ff = hidden_weight.shape[1]
    mels = mel_frames.shape[1]
    devices = lax.axis_size("frames")
    device = lax.axis_index("frames")
    core = device % 2
    nb = 2 * SIDE + 1
    ext = count + 2 * PAD
    base = (device - core - 2 * SIDE) * count

    left, right = move(mel_frames[-2:], 1), move(mel_frames[:2], -1)

    smem = pl.BlockSpec(memory_space=pltpu.SMEM)
    vmem = pl.BlockSpec(memory_space=pltpu.VMEM)
    hbm = pl.BlockSpec(memory_space=pl.ANY)
    whole = pltpu.VMEM((count, 128), jnp.int32)
    spans, pack, table, key_plan, query_plan = pl.pallas_call(
        functools.partial(tables_kernel, total=devices * count),
        out_shape=[
            jax.ShapeDtypeStruct(s, d)
            for s, d in (
                ((count, 128), jnp.int32), ((ext, 128), F32), ((count, width), F32), ((16,), jnp.int32), ((16,), jnp.int32)
            )
        ],
        in_specs=[smem] * 3,
        out_specs=[vmem] * 3 + [smem] * 2,
        scratch_shapes=[whole] * 3,
        cost_estimate=cost(4),
    )(device[None].astype(jnp.int32), clip_lengths, valid_keys)

    x, columns, dstem, dstride, layer_in, attn_in = call(
        stem_kernel,
        [
            ((ext, 4 * SLOT), BF), ((count, 3 * width), BF), ((ext, 2 * width), F32), ((count, width), F32), ((count, width), F32),
            ((count, width), BF),
        ],
        (
            mel_frames, left, right, stem_weight, stem_bias, stride_weight, stride_bias, attn_gain, attn_shift, pack, table,
        ),
        [pltpu.VMEM((2 * ext + 16, SLOT), F32), pltpu.VMEM((4 * SLOT, 2 * width), BF), pltpu.VMEM((ext, width), F32)],
        us=7,
        limit=24,
    )

    joint = jnp.concatenate([query_bias.astype(F32), jnp.zeros((width,), F32), value_bias.astype(F32)])

    def project(block):
        return (nn(block, attn_weight) + joint).astype(BF)

    def after(value, *others):
        return lax.optimization_barrier((value, *others))[0]

    def gather(block, pair):
        own, sib = {0: project(block)}, {0: project(pair)}
        ends = block, block
        done = [own[0], sib[0]]
        for k in range(1, SIDE + 1):
            ends = move(ends[0], 2), move(ends[1], -2)
            if k == 1:
                ends = after(ends[0], *done), after(ends[1], *done)
            here, there = dict(zip((-k, k), ends)), {n: swap(b) for n, b in zip((-k, k), ends)}
            for n in (-k, k):
                own[n] = project(after(here[n], *(done if k == SIDE else there.values())))
            for n in (-k, k):
                sib[n] = project(after(there[n], own[-k], own[k]))
            done += [v[n] for v in (own, sib) for n in (-k, k)]
        order = range(-SIDE, SIDE + 1)
        return [own[n] for n in order], [sib[n] for n in order]

    pair_in = swap(attn_in)
    own, sib = gather(attn_in, pair_in)
    pair_columns = lax.ppermute(columns, "frames", [(d, d + 1) for d in range(0, devices, 2)])
    reach = 2 * nb * count + KB
    pairs = width // 128
    sems = pltpu.SemaphoreType.DMA((2 * nb, 2))
    count_of = pltpu.SMEM((1,), jnp.int32)

    stacked = pltpu.VMEM((pairs, 2 * QB, 128), BF)
    summed = pltpu.VMEM((pairs, 2 * QB, 128), F32)
    score = pltpu.VMEM((2, pairs, 2 * QB, KB), F32)
    weight = pltpu.VMEM((2, pairs, 2 * QB, KB), BF)
    one_sem = pltpu.SemaphoreType.DMA((1,))
    local_query = pltpu.VMEM((count, width), BF)

    core1 = core[None].astype(jnp.int32)
    bundle = ff + 2 * width + width // 2
    block_f32 = pltpu.VMEM((count, width), F32)
    lse, layer_out, keep, send, grad_middle, pay, dlt, sums1 = call(
        layer_kernel,
        [
            ((count, 128), F32), ((count, width), BF), ((count, bundle), BF), ((count, bundle), BF), ((count, width), F32),
            ((count + 48, width), BF), ((count, 128), F32), ((8, width), F32),
        ],
        (
            key_plan, spans, *own, *sib, layer_in, cotangent, output_weight, hidden_weight, return_weight, output_bias,
            hidden_bias, return_bias, mlp_gain, mlp_shift,
        ),
        [
            block_f32, local_query, pltpu.VMEM((reach, 2 * width), BF), stacked, summed, summed, summed, summed, score, weight,
            count_of, count_of, sems, pltpu.SemaphoreType.DMA((6,)),
            block_f32, local_query, pltpu.VMEM((width, width), BF), pltpu.VMEM((width, ff), BF), pltpu.VMEM((ff, width), BF),
            block_f32, block_f32, pltpu.VMEM((2, count, bundle), BF), pltpu.SemaphoreType.DMA((2 * (ff // width) + 6,)),
        ],
        [smem, vmem] + [hbm] * (2 * nb + 5) + [vmem] * 5,
        out_specs=[vmem, vmem, hbm, hbm] + [vmem] * 4,
        us=26,
    )

    got = swap(send)
    near = {-1: move(pay, 2), 1: move(pay, -2)}

    blocks = ff // width
    groups = width // 16
    tiles = (groups, 2, 16 * (blocks * pairs // 2 + 1), 128)

    def at(n):
        return pl.BlockSpec((count, width), lambda i, core: (0, n))

    def each(i, core):
        return (0, jnp.minimum(i, blocks - 1))

    bundle_specs = [
        pl.BlockSpec((count, width), each), at(blocks), at(blocks + 1),
        pl.BlockSpec((count, width // 2), lambda i, core: (0, 2 * (blocks + 2))),
    ]
    mlp_both = pl.pallas_call(
        mlp_weights_kernel,
        out_shape=jax.ShapeDtypeStruct(tiles, BF),
        grid_spec=pltpu.PrefetchScalarGridSpec(
            num_scalar_prefetch=1,
            grid=(blocks + 1,),
            in_specs=bundle_specs * 2,
            out_specs=pl.BlockSpec(tiles, lambda i, core: (0, 0, 0, 0)),
        ),
        compiler_params=pltpu.CompilerParams(vmem_limit_bytes=20 * MIB),
        cost_estimate=cost(5.0),
    )(core1, keep, keep, keep, keep, got, got, got, got)

    near = {k: follow(b, mlp_both) for k, b in near.items()}
    far = {-2: move(near[-1], 2), 2: move(near[1], -2)}
    (grad_query,) = call(
        query_kernel,
        [((count, width), BF)],
        (key_plan, spans, pay, lse, dlt, *own, *sib, near[-1], near[1]),
        [
            local_query, pltpu.VMEM((reach, 2 * width), BF), stacked, stacked, summed, summed, summed, score, score, weight,
            count_of, count_of, sems, one_sem,
        ],
        [smem] + [vmem] * 4 + [hbm] * (2 * nb + 2),
        us=15,
        limit=56,
    )
    travel = {0: pay, **near, **{k: follow(b, grad_query) for k, b in far.items()}}
    sib_pay = {k: swap(travel[k]) for k in travel}
    own_pay, sib_pay = ([v[k] for k in range(-SIDE, SIDE + 1)] for v in (travel, sib_pay))

    mlp_parts = over_chips(mlp_both)
    (mlp_spread,) = call(
        spread_kernel, [(mlp_parts.shape, BF)], (mlp_parts, grad_query), specs=[vmem, hbm], us=3, limit=12
    )
    mlp_mine = over_chips(mlp_spread[:, None]).reshape(tiles)

    grad_projected, gsp, sums2 = call(
        key_kernel,
        [((count, 3 * width), BF), ((count, width), BF), ((8, width), F32)],
        (
            query_plan, spans, grad_query, attn_weight, layer_in, grad_middle, attn_gain,
            dstride, *own, *sib, *own_pay, *sib_pay, mlp_spread,
        ),
        [
            pltpu.VMEM((count, 2 * width), BF), pltpu.VMEM((reach, width), BF), pltpu.VMEM((reach, width), BF),
            pltpu.VMEM((48, reach), BF), pltpu.VMEM((8, reach), F32), pltpu.VMEM((8, reach), F32), stacked, stacked, summed, summed, score, score, weight,
            weight, count_of, count_of, sems, pltpu.SemaphoreType.DMA((2 * nb, 1)),
            one_sem,
        ],
        [smem] + [vmem] * 7 + [hbm] * (4 * nb + 1),
        us=18,
        limit=56,
    )
    left, right = move(gsp[-1:], 1), move(gsp[:1], -1)

    gp_pair, gsp_pair = swap(grad_projected), swap(gsp)
    def whole_block(i, core):
        return (0, 0)

    def column_block(i, core):
        return (0, i)

    last_tiles = (groups, 2, 16 * (3 * pairs // 2 + 1), 128)
    last_specs = [pl.BlockSpec((count, width), m) for m in (whole_block, column_block, column_block, whole_block)]
    both = pl.pallas_call(
        last_weights_kernel,
        out_shape=jax.ShapeDtypeStruct(last_tiles, BF),
        grid_spec=pltpu.PrefetchScalarGridSpec(
            num_scalar_prefetch=1,
            grid=(3,),
            in_specs=last_specs * 2,
            out_specs=pl.BlockSpec(last_tiles, lambda i, core: (0, 0, 0, 0)),
        ),
        compiler_params=pltpu.CompilerParams(vmem_limit_bytes=20 * MIB),
        cost_estimate=cost(3),
    )(core1, attn_in, grad_projected, columns, gsp, pair_in, gp_pair, pair_columns, gsp_pair)
    gpre, both = pl.pallas_call(
        stem_back_kernel,
        out_shape=[jax.ShapeDtypeStruct((ext, 2 * width), BF), jax.ShapeDtypeStruct(last_tiles, BF)],
        in_specs=[vmem] * 9 + [hbm],
        out_specs=[vmem, hbm],
        scratch_shapes=[
            pltpu.VMEM((ext + 8, width), F32), pltpu.VMEM((ext, width), BF), pltpu.VMEM((ext, width), BF),
            pltpu.VMEM((3 * mels + 16, width), F32), pltpu.VMEM((groups, 2, 16, 128), BF), one_sem,
        ],
        input_output_aliases={9: 1},
        compiler_params=pltpu.CompilerParams(vmem_limit_bytes=20 * MIB),
        cost_estimate=cost(4),
    )(gsp, left, right, stride_weight, dstem, x, pack, sums1, sums2, both)

    (mel_grad,) = call(
        mel_kernel,
        [((2 * count, mels), F32)],
        (gpre, stem_weight, pack),
        [pltpu.VMEM((4 * SLOT, 2 * width), BF), pltpu.VMEM((ext, 4 * SLOT), F32)],
        us=3,
        limit=16,
    )

    grad_return_weight, grad_hidden_weight, grad_output_weight = call(
        unpack_mlp_kernel,
        [((ff, width), F32), ((width, ff), F32), ((width, width), F32)],
        (core1, mlp_mine, swap(mlp_mine)),
        specs=[smem, vmem, vmem],
        us=5,
        limit=24,
    )
    parts = over_chips(both)
    (spread,) = call(
        spread_kernel, [(parts.shape, BF)], (parts, mel_grad, grad_output_weight), specs=[vmem, hbm, hbm], us=3, limit=12
    )
    mine = over_chips(spread[:, None]).reshape(last_tiles)
    sizes = [width] * 9 + [ff, width]
    grad_attn_weight, grad_stride_weight, grad_stem_weight, *bias = call(
        unpack_kernel,
        [((width, 3 * width), F32), ((3 * width, width), F32), ((3 * mels, width), F32)] + [((n,), F32) for n in sizes],
        (core1, mine, swap(mine)),
        [pltpu.VMEM((3 * mels + 16, width), F32)],
        [smem, vmem, vmem],
        us=6,
        limit=22,
    )
    return (
        layer_out, mel_grad, grad_stem_weight, bias[0], grad_stride_weight, bias[1], bias[2], bias[3], grad_attn_weight,
        bias[4], bias[5], grad_output_weight, bias[6], bias[7], bias[8], grad_hidden_weight, bias[9],
        grad_return_weight, bias[10],
    )


def solution(mesh):
    split = P("frames", None)
    in_specs = (split,) + (P(),) * 19 + (split,)
    out_specs = (split, split) + (P(),) * 17
    return jax.shard_map(local, mesh=mesh, in_specs=in_specs, out_specs=out_specs, check_vma=False)
```

```python
import functools
import math

import jax
import jax.numpy as jnp
from jax import lax
from jax.experimental import pallas as pl
from jax.experimental.pallas import tpu as pltpu
from jax.sharding import PartitionSpec as P

HEADS = 8
SIDE = 2
QB = 128
KB = 256
PAD = 16
SLOT = 128
NEG = -1e30
BF = jnp.bfloat16
F32 = jnp.float32
MIB = 1 << 20


def nn(a, b):
    return lax.dot_general(a, b, (((1,), (0,)), ((), ())), preferred_element_type=F32)


def nt(a, b):
    return lax.dot_general(a, b, (((1,), (1,)), ((), ())), preferred_element_type=F32)


def tn(a, b):
    return lax.dot_general(a, b, (((0,), (0,)), ((), ())), preferred_element_type=F32)


def gelu_pair(x):
    bell = jnp.exp(-0.5 * x * x)
    t = 1.0 / (1.0 + 0.2316419 * jnp.abs(x))
    poly = 0.127414796 + t * (-0.142248368 + t * (0.7107068705 + t * (-0.7265760135 + t * 0.5307027145)))
    tail = bell * t * poly
    phi = jnp.where(x >= 0, 1.0 - tail, tail)
    return x * phi, phi + 0.3989422804 * x * bell


def norm_parts(x):
    center = jnp.mean(x, axis=-1, keepdims=True)
    centered = x - center
    rstd = lax.rsqrt(jnp.mean(centered * centered, axis=-1, keepdims=True) + 1e-05)
    return centered * rstd, rstd


def norm_back(grad, xhat, rstd, gain):
    inner = grad * gain
    m1 = jnp.mean(inner, axis=-1, keepdims=True)
    m2 = jnp.mean(inner * xhat, axis=-1, keepdims=True)
    return rstd * (inner - m1 - xhat * m2)


def vector(ref):
    return ref[...].astype(F32).reshape(1, -1)


def colsum(x):
    return jnp.sum(x, axis=0, keepdims=True)


def halves(x, low):
    zero = jnp.zeros_like(x)
    return jnp.concatenate([jnp.where(low, x, zero), jnp.where(low, zero, x)], axis=0)


def pick(x, low):
    return jnp.where(low, x[:QB], x[QB:])


def wide(x):
    return jnp.concatenate([x, x], axis=1)


def tall(x):
    return jnp.concatenate([x, x], axis=0)


def tables_kernel(device, lengths, valids, spans_o, pack_o, table_o, keys_o, queries_o, start_s, length_s, valid_s, *, total):
    count, width = table_o.shape
    base = (device[0] - device[0] % 2 - 2 * SIDE) * count
    first = device[0] * count
    token = first + lax.broadcasted_iota(jnp.int32, (count, 128), 0)
    row = lax.broadcasted_iota(jnp.int32, pack_o.shape, 0) + lax.broadcasted_iota(jnp.int32, pack_o.shape, 1) - PAD
    here = (row >= 0) & (row <= count) & (first + row < total)
    pack_o[...] = jnp.where(here, 1.0, 0.0)
    keys_o[0] = queries_o[0] = device[0] % 2

    def clip(c, start):
        length = lengths[c]
        valid = jnp.minimum(valids[c], length)
        end = start + length

        @pl.when((start < first + count) & (end > first))
        def _():
            inside = (token >= start) & (token < end)
            start_s[...] = jnp.where(inside, start, start_s[...])
            length_s[...] = jnp.where(inside, length, length_s[...])
            valid_s[...] = jnp.where(inside, valid, valid_s[...])
            for n in range(count // QB):
                at = first + n * QB

                @pl.when((start <= at) & (at < end))
                def _():
                    keys_o[4 + 2 * n] = queries_o[4 + 2 * n] = ((start - base) >> 7) << 7

                @pl.when((start < at + QB) & (at + QB <= end))
                def _():
                    keys_o[5 + 2 * n] = start + valid - base
                    queries_o[5 + 2 * n] = end - base

        @pl.when((start >= first) & (start <= first + count))
        def _():
            pack_o[...] = jnp.where(first + row == start, 0.0, pack_o[...])

        return end

    lax.fori_loop(0, lengths.shape[0], clip, 0)
    for plan in (keys_o, queries_o):
        low, high = plan[4], 0
        for n in range(count // QB):
            steps = (plan[5 + 2 * n] - plan[4 + 2 * n] + KB - 1) // KB
            plan[5 + 2 * n] = steps
            low = jnp.minimum(low, plan[4 + 2 * n])
            high = jnp.maximum(high, plan[4 + 2 * n] + steps * KB)
        plan[1], plan[2] = low, high
    lane = lax.broadcasted_iota(jnp.int32, (count, 128), 1)
    key_lo = start_s[...] - base
    position = token - start_s[...]
    is_key = position < valid_s[...]
    query_lo = jnp.where(is_key, key_lo, 1 << 20)
    query_hi = jnp.where(is_key, key_lo + length_s[...], 0)
    first_two = jnp.where(lane == 0, key_lo, key_lo + valid_s[...])
    spans_o[...] = jnp.where(lane < 2, first_two, jnp.where(lane == 2, query_lo, query_hi))
    half = width // 2
    number = lax.broadcasted_iota(jnp.int32, (1, half), 1).astype(F32)
    rates = jnp.exp(number * (-math.log(10000.0) / (half - 1)))
    angles = wide(position.astype(F32)) * rates
    table_o[:, :half] = jnp.sin(angles)
    table_o[:, half:] = jnp.cos(angles)


def taps_of(wbig, sw):
    mels, width = sw.shape[0] // 3, sw.shape[1]
    wbig[...] = jnp.zeros_like(wbig)
    for t in range(3):
        tap = sw[t * mels : (t + 1) * mels, :]
        wbig[t * SLOT : t * SLOT + mels, :width] = tap
        wbig[(t + 1) * SLOT : (t + 1) * SLOT + mels, width:] = tap


def stem_kernel(
    mel, left, right, sw, sbias, vw, vbias, gain, shift, pack, table,
    x_o, cols_o, dstem_o, dstride_o, lin_o, ain_o, m, wbig, shifted,
):
    count, width = lin_o.shape
    frames, mels = mel.shape
    ext = x_o.shape[0]
    taps_of(wbig, sw)
    top = 2 * PAD + 8
    m[...] = jnp.zeros_like(m)
    m[top : top + frames, :mels] = mel[...].astype(F32)
    m[top - 2 : top, :mels] = left[...].astype(F32)
    m[top + frames : top + frames + 2, :mels] = right[...].astype(F32)
    opn, opn_next = pack[:, 0:1], pack[:, 1:2]
    x_o[:, :SLOT] = (m[pl.ds(7, ext, stride=2), :] * opn).astype(BF)
    x_o[:, SLOT : 2 * SLOT] = m[pl.ds(8, ext, stride=2), :].astype(BF)
    x_o[:, 2 * SLOT : 3 * SLOT] = m[pl.ds(9, ext, stride=2), :].astype(BF)
    x_o[:, 3 * SLOT :] = (m[pl.ds(10, ext, stride=2), :] * opn_next).astype(BF)
    inner = slice(PAD, PAD + count)
    even, odd = slice(0, width), slice(width, 2 * width)
    act, dact = gelu_pair(nn(x_o[...], wbig[:, even]) + vector(sbias))
    dstem_o[:, even] = dact
    cols_o[:, width : 2 * width] = act[inner].astype(BF)
    act, dact = gelu_pair(nn(x_o[...], wbig[:, odd]) + vector(sbias))
    dstem_o[:, odd] = dact
    cols_o[:, 2 * width :] = act[inner].astype(BF)
    shifted[...] = act
    cols_o[:, :width] = (shifted[PAD - 1 : PAD + count - 1, :] * pack[inner, 0:1]).astype(BF)
    pre = nn(cols_o[...], vw[...]) + vector(vbias)
    act2, dact2 = gelu_pair(pre)
    dstride_o[...] = dact2
    lin = act2 + table[...]
    lin_o[...] = lin
    xhat, _ = norm_parts(lin)
    ain_o[...] = (xhat * vector(gain) + vector(shift)).astype(BF)


def needed(sc, block, count):
    return (block * count < sc[2]) & ((block + 1) * count > sc[1])


def start_copies(sc, pairs, sem, count, begun, upto):
    for block, copies in pairs:

        @pl.when(needed(sc, block, count) & (block >= begun[0]) & (block < upto))
        def _():
            for m, (src, dst) in enumerate(copies):
                pltpu.make_async_copy(src, dst, sem.at[block, m]).start()

    begun[0] = jnp.maximum(begun[0], upto)


def wait_until(sc, end, copies, sem, count, there, ahead=None):
    def one(block, _):
        @pl.when(needed(sc, block, count))
        def _():
            for m, (src, dst) in enumerate(copies(block)):
                pltpu.make_async_copy(src, dst, sem.at[block, m]).wait()

        return 0

    upto = jnp.minimum((end + count - 1) // count, 2 * (2 * SIDE + 1))
    if ahead is not None:

        @pl.when(upto > there[0])
        def _():
            ahead(upto + 2)

    lax.fori_loop(there[0], upto, one, 0)
    there[0] = jnp.maximum(there[0], upto)


def window(sc, own, sib):
    core = sc[0]
    out = []
    for k in range(2 * SIDE + 1):
        out += [(2 * k + core, own[k]), (2 * k + 1 - core, sib[k])]
    return out


def rows_of(block, count):
    return pl.ds(pl.multiple_of(block * count, count), count)


def in_range(lo, hi, start):
    col = start + lax.broadcasted_iota(jnp.int32, (QB, KB), 1)
    return jnp.where((col >= lo) & (col < hi), 0.0, NEG)


def chunks(first, steps, step, wait):
    def two(n, _):
        wait(first + (2 * n + 2) * KB)
        step(2 * n, 2)
        return 0

    lax.fori_loop(0, steps // 2, two, 0)

    @pl.when(steps % 2 == 1)
    def _():
        wait(first + steps * KB)
        step(steps - 1, 1)


def layer_kernel(*refs):
    nb = 2 * SIDE + 1
    sc, span_ref = refs[:2]
    own, sib = refs[2 : 2 + nb], refs[2 + nb : 2 + 2 * nb]
    at = 2 + 2 * nb
    fetched, vectors, outs = refs[at : at + 5], refs[at + 5 : at + 10], refs[at + 10 : at + 18]
    lse_o = outs[0]
    scratch = refs[at + 18 :]
    ctx_o, local_ref, kv, q2, acc, peak, total, scale, s, e, there, begun, sem, sem2 = scratch[:14]
    held, mlp_scratch = scratch[14:19], scratch[19:]
    count, width = ctx_o.shape
    late = [pltpu.make_async_copy(src, dst, sem2.at[1 + n]) for n, (src, dst) in enumerate(zip(fetched, held))]
    span = 2 * nb * count
    pairs = width // 128
    kv[span:, :] = jnp.zeros((kv.shape[0] - span, 2 * width), BF)
    there[0] = 0

    def copies(block, src=own[0]):
        return [(src.at[:, pl.ds(width, 2 * width)], kv.at[rows_of(block, count), :])]

    local = pltpu.make_async_copy(own[SIDE].at[:, pl.ds(0, width)], local_ref, sem2.at[0])
    local.start()
    begun[0] = 0
    sources = [(block, copies(block, src)) for block, src in window(sc, own, sib)]

    def ahead(upto):
        start_copies(sc, sources, sem, count, begun, upto)

    ahead(sc[1] // count + 3)
    for copy in late:
        copy.start()
    local.wait()

    def wait(end):
        wait_until(sc, end, copies, sem, count, there, ahead)

    low = lax.broadcasted_iota(jnp.int32, (QB, 128), 1) < 64
    lanes = lax.broadcasted_iota(jnp.int32, (QB, 128), 1)

    def one(i, _):
        rows = pl.ds(pl.multiple_of(i * QB, QB), QB)
        for p in range(pairs):
            q2[p] = halves(local_ref[rows, p * 128 : (p + 1) * 128], low) * jnp.asarray(0.125, BF)
            acc[p] = jnp.zeros_like(acc[p])
            peak[p] = jnp.full_like(peak[p], NEG)
            total[p] = jnp.zeros_like(total[p])
        lo, hi = span_ref[rows, 0:1], span_ref[rows, 1:2]

        def step(n, parts):
            start = sc[4 + 2 * i] + n * KB
            keys = [pl.ds(pl.multiple_of(start + u * KB, 128), KB) for u in range(parts)]
            for u in range(parts):
                bias = tall(in_range(lo, hi, start + u * KB))
                for p in range(pairs):
                    s[u, p] = nt(q2[p], kv[keys[u], p * 128 : (p + 1) * 128]) + bias
            for p in range(pairs):
                best = functools.reduce(jnp.maximum, [s[u, p] for u in range(parts)])
                old = peak[p]
                top = jnp.maximum(old, jnp.max(best, axis=1, keepdims=True))
                peak[p] = top
                scale[p] = jnp.exp(old - top)
            for p in range(pairs):
                total[p] = scale[p] * total[p]
                for u in range(parts):
                    grown = jnp.exp(s[u, p] - wide(peak[p]))
                    e[u, p] = grown.astype(BF)
                    total[p] = total[p] + (grown[:, :128] + grown[:, 128:])
            for p in range(pairs):
                value = [kv[keys[u], width + p * 128 : width + (p + 1) * 128] for u in range(parts)]
                acc[p] = scale[p] * acc[p] + functools.reduce(jnp.add, [nn(e[u, p], value[u]) for u in range(parts)])

        chunks(sc[4 + 2 * i], sc[5 + 2 * i], step, wait)
        lse = jnp.zeros((QB, 128), F32)
        for p in range(pairs):
            row_total = jnp.sum(total[p], axis=1, keepdims=True)
            ctx_o[rows, p * 128 : (p + 1) * 128] = pick(acc[p] / row_total, low)
            both = peak[p] + jnp.log(row_total)
            lse = jnp.where(lanes == 2 * p, both[:QB], lse)
            lse = jnp.where(lanes == 2 * p + 1, both[QB:], lse)
        lse_o[rows, :] = lse
        return 0

    lax.fori_loop(0, count // QB, one, 0)
    wait(span)
    for copy in late:
        copy.wait()
    mlp(sc, ctx_o, lse_o, *held, *vectors, *outs[1:], *mlp_scratch)


def query_kernel(*refs):
    nb = 2 * SIDE + 1
    sc, span_ref, pay_ref, lse_ref, dlt_ref = refs[:5]
    own, sib = refs[5 : 5 + nb], refs[5 + nb : 5 + 2 * nb]
    dq_o, mark, local_ref, kv, q2, do2, acc, lse2, dlt2, s, d, ds, there, begun, sem, sem2 = refs[5 + 2 * nb :]
    mark[...] = jnp.zeros_like(mark)
    count, width = dq_o.shape
    span = 2 * nb * count
    pairs = width // 128
    kv[span:, :] = jnp.zeros((kv.shape[0] - span, 2 * width), BF)
    there[0] = 0

    def copies(block, src=own[0]):
        return [(src.at[:, pl.ds(width, 2 * width)], kv.at[rows_of(block, count), :])]

    local = pltpu.make_async_copy(own[SIDE].at[:, pl.ds(0, width)], local_ref, sem2.at[0])
    local.start()
    begun[0] = 0
    sources = [(block, copies(block, src)) for block, src in window(sc, own, sib)]

    def ahead(upto):
        start_copies(sc, sources, sem, count, begun, upto)

    ahead(sc[1] // count + 3)
    local.wait()

    def wait(end):
        wait_until(sc, end, copies, sem, count, there, ahead)

    low = lax.broadcasted_iota(jnp.int32, (QB, 128), 1) < 64

    def one(i, _):
        rows = pl.ds(pl.multiple_of(i * QB, QB), QB)
        lse, dlt = lse_ref[rows, :], dlt_ref[rows, :]
        for p in range(pairs):
            q2[p] = halves(local_ref[rows, p * 128 : (p + 1) * 128], low) * jnp.asarray(0.125, BF)
            do2[p] = halves(pay_ref[rows, p * 128 : (p + 1) * 128], low)
            acc[p] = jnp.zeros_like(acc[p])
            for h in range(2):
                part = pl.ds(h * QB, QB)
                lse2[p, part, :] = jnp.broadcast_to(lse[:, 2 * p + h : 2 * p + h + 1], (QB, 128))
                dlt2[p, part, :] = jnp.broadcast_to(dlt[:, 2 * p + h : 2 * p + h + 1], (QB, 128))
        lo, hi = span_ref[rows, 0:1], span_ref[rows, 1:2]

        def step(n, parts):
            start = sc[4 + 2 * i] + n * KB
            keys = [pl.ds(pl.multiple_of(start + u * KB, 128), KB) for u in range(parts)]
            for u in range(parts):
                bias = tall(in_range(lo, hi, start + u * KB))
                for p in range(pairs):
                    s[u, p] = nt(q2[p], kv[keys[u], p * 128 : (p + 1) * 128]) + bias
                    d[u, p] = nt(do2[p], kv[keys[u], width + p * 128 : width + (p + 1) * 128])
            for u in range(parts):
                for p in range(pairs):
                    e = jnp.exp(s[u, p] - wide(lse2[p]))
                    ds[u, p] = (e * (d[u, p] - wide(dlt2[p]))).astype(BF)
            for p in range(pairs):
                more = [nn(ds[u, p], kv[keys[u], p * 128 : (p + 1) * 128]) for u in range(parts)]
                acc[p] = acc[p] + functools.reduce(jnp.add, more)

        chunks(sc[4 + 2 * i], sc[5 + 2 * i], step, wait)
        for p in range(pairs):
            dq_o[rows, p * 128 : (p + 1) * 128] = (pick(acc[p], low) * 0.125).astype(BF)
        return 0

    lax.fori_loop(0, count // QB, one, 0)
    wait(span)


def key_kernel(*refs):
    nb = 2 * SIDE + 1
    sc, span_ref, dq_ref, w_ref, lin_ref, gm_ref, gain, dstride_ref = refs[:8]
    own, sib = refs[8 : 8 + nb], refs[8 + nb : 8 + 2 * nb]
    ownp, sibp = refs[8 + 2 * nb : 8 + 3 * nb], refs[8 + 3 * nb : 8 + 4 * nb]
    gp_o, gsp_o, sums_o, kvl, q, do, stat, lse, dlt, k2, v2, dk, dv, s, d, e, ds, there, begun, sem, sem2, sem3 = refs[8 + 4 * nb :]
    count, width = gsp_o.shape
    span = 2 * nb * count
    pairs = width // 128
    rest = q.shape[0] - span
    q[span:, :] = jnp.zeros((rest, width), BF)
    do[span:, :] = jnp.zeros((rest, width), BF)
    stat[:, span:] = jnp.zeros((stat.shape[0], rest), BF)
    there[0] = 0

    def copies(block, src=own[0], pay=ownp[0]):
        return [
            (src.at[:, pl.ds(0, width)], q.at[rows_of(block, count), :]),
            (pay.at[pl.ds(0, count), :], do.at[rows_of(block, count), :]),
        ]

    def side(block, pay=ownp[0]):
        return [(pay.at[pl.ds(count, 48), pl.ds(0, count)], stat.at[:, rows_of(block, count)])]

    local = pltpu.make_async_copy(own[SIDE].at[:, pl.ds(width, 2 * width)], kvl, sem3.at[0])
    local.start()
    pairs_of = list(zip(window(sc, own, sib), window(sc, ownp, sibp)))
    begun[0] = 0
    start_copies(sc, [(block, side(block, pay)) for _, (block, pay) in pairs_of], sem2, count, begun, 2 * nb)
    begun[0] = 0
    sources = [(block, copies(block, src, pay)) for (block, src), (_, pay) in pairs_of]

    def ahead(upto):
        start_copies(sc, sources, sem, count, begun, upto)

    ahead(sc[1] // count + 3)

    def wait(end):
        wait_until(sc, end, copies, sem, count, there, ahead)

    local.wait()
    wait_until(sc, span, side, sem2, count, there)
    there[0] = 0
    lse[...] = stat[0:8, :].astype(F32) + stat[8:16, :].astype(F32) + stat[16:24, :].astype(F32)
    dlt[...] = stat[24:32, :].astype(F32) + stat[32:40, :].astype(F32) + stat[40:48, :].astype(F32)
    low = lax.broadcasted_iota(jnp.int32, (QB, 128), 1) < 64

    def one(i, _):
        rows = pl.ds(pl.multiple_of(i * QB, QB), QB)
        for p in range(pairs):
            k2[p] = halves(kvl[rows, p * 128 : (p + 1) * 128], low) * jnp.asarray(0.125, BF)
            v2[p] = halves(kvl[rows, width + p * 128 : width + (p + 1) * 128], low)
            dk[p] = jnp.zeros_like(dk[p])
            dv[p] = jnp.zeros_like(dv[p])
        lo, hi = span_ref[rows, 2:3], span_ref[rows, 3:4]

        def step(n, parts):
            start = sc[4 + 2 * i] + n * KB
            queries = [pl.ds(pl.multiple_of(start + u * KB, 128), KB) for u in range(parts)]
            for u in range(parts):
                for p in range(pairs):
                    lanes = slice(p * 128, (p + 1) * 128)
                    s[u, p] = nt(k2[p], q[queries[u], lanes])
                    d[u, p] = nt(v2[p], do[queries[u], lanes])
            for u in range(parts):
                bias = in_range(lo, hi, start + u * KB)
                for p in range(pairs):
                    for h in range(2):
                        part = slice(h * QB, (h + 1) * QB)
                        head = slice(2 * p + h, 2 * p + h + 1)
                        grown = jnp.exp(s[u, p, part] + (bias - lse[head, queries[u]]))
                        e[u, p, part] = grown.astype(BF)
                        ds[u, p, part] = (grown * (d[u, p, part] - dlt[head, queries[u]])).astype(BF)
            for p in range(pairs):
                lanes = slice(p * 128, (p + 1) * 128)
                dv[p] = dv[p] + functools.reduce(jnp.add, [nn(e[u, p], do[queries[u], lanes]) for u in range(parts)])
                dk[p] = dk[p] + functools.reduce(jnp.add, [nn(ds[u, p], q[queries[u], lanes]) for u in range(parts)])

        chunks(sc[4 + 2 * i], sc[5 + 2 * i], step, wait)
        for p in range(pairs):
            gp_o[rows, width + p * 128 : width + (p + 1) * 128] = (pick(dk[p], low) * 0.125).astype(BF)
            gp_o[rows, 2 * width + p * 128 : 2 * width + (p + 1) * 128] = pick(dv[p], low).astype(BF)
        return 0

    lax.fori_loop(0, count // QB, one, 0)
    wait(span)
    gp_o[:, :width] = dq_ref[...]
    grad = nt(gp_o[...], w_ref[...])
    xhat, rstd = norm_parts(lin_ref[...])
    total = gm_ref[...] + norm_back(grad, xhat, rstd, vector(gain))
    gsp_o[...] = (total * dstride_ref[...]).astype(BF)
    sums_o[0:1, :] = colsum(grad * xhat)
    sums_o[1:2, :] = colsum(grad)
    sums_o[2:3, :] = colsum(gp_o[:, :width].astype(F32))
    sums_o[3:4, :] = colsum(gp_o[:, 2 * width :].astype(F32))
    sums_o[4:8, :] = jnp.zeros((4, width), F32)


def pieces(x, n):
    out = []
    for _ in range(n):
        part = x.astype(BF)
        out.append(part)
        x = x - part.astype(F32)
    return out


def mlp(
    core, ctx, lse, lin, dy, wo, w1, w2, bo, b1, b2, gain_ref, shift,
    out_o, keep_o, send_o, gm_o, pay_o, dlt_o, sums_o, out_acc, gmi_acc, roles, sem,
):
    count, width = lin.shape
    ff = w1.shape[1]

    copies = []

    def give(role, at, size, value):
        cols = slice(at, at + size)
        roles[role, :, cols] = value
        number = len(copies)
        source = roles.at[role, :, pl.ds(at, size)]
        here = pltpu.make_async_copy(source, keep_o.at[:, pl.ds(at, size)], sem.at[number])
        there = pltpu.make_async_copy(source, send_o.at[:, pl.ds(at, size)], sem.at[number])
        copies.append(here)

        @pl.when(core[0] == role)
        def _():
            here.start()

        @pl.when(core[0] != role)
        def _():
            there.start()

        return roles.at[role, :, cols]

    context = ctx[...]
    ctx_b = context.astype(BF)
    for role in range(2):
        give(role, ff + 2 * width, width // 2, ctx_b[:, role * width // 2 : (role + 1) * width // 2])
    give(0, ff, width, dy[...])
    middle = lin[...] + nn(ctx_b, wo[...]) + vector(bo)
    xhat, rstd = norm_parts(middle)
    gain = vector(gain_ref)
    mi = give(1, ff, width, (xhat * gain + vector(shift)).astype(BF))
    grad_out = dy[...].astype(F32)
    sums_o[7:8, :] = colsum(grad_out)
    for f in range(ff // width):
        cols = slice(f * width, (f + 1) * width)
        act, dact = gelu_pair(nn(mi[...], w1[:, cols]) + vector(b1.at[cols]))
        act = give(0, f * width, width, act.astype(BF))
        ghp = (nt(dy[...], w2[cols, :]) * dact).astype(BF)
        ghp_ref = give(1, f * width, width, ghp)
        sums_o[3 + f : 4 + f, :] = colsum(ghp.astype(F32))
        more = nn(act[...], w2[cols, :])
        gmore = nt(ghp_ref[...], w1[:, cols])
        if f == 0:
            out_acc[...] = middle + vector(b2) + more
            gmi_acc[...] = gmore
        else:
            out_acc[...] = out_acc[...] + more
            gmi_acc[...] = gmi_acc[...] + gmore
    out_o[...] = out_acc[...].astype(BF)
    gmi = gmi_acc[...]
    sums_o[1:2, :] = colsum(gmi * xhat)
    sums_o[2:3, :] = colsum(gmi)
    grad_middle = grad_out + norm_back(gmi, xhat, rstd, gain)
    gm_o[...] = grad_middle
    branch = grad_middle.astype(BF)
    for role in range(2):
        give(role, ff + width, width, branch)
    sums_o[0:1, :] = colsum(branch.astype(F32))
    gctx = nt(branch, wo[...]).astype(BF)
    pay_o[:count, :] = gctx
    prod = pieces(gctx.astype(F32) * context, 3)
    head = width // HEADS

    def is_head(shape, feature, number):
        feature, number = (lax.broadcasted_iota(jnp.int32, shape, n) for n in (feature, number))
        return jnp.where(feature // head == number, 1.0, 0.0).astype(BF)

    onehot, onehot_t = is_head((width, 128), 0, 1), is_head((16, width), 1, 0)
    eye = lax.broadcasted_iota(jnp.int32, (16, 128), 0) == lax.broadcasted_iota(jnp.int32, (16, 128), 1)
    eye = jnp.where(eye, 1.0, 0.0).astype(BF)
    dlt_o[...] = nn(prod[0], onehot) + nn(prod[1], onehot) + nn(prod[2], onehot)
    across = nt(onehot_t, prod[0]) + nt(onehot_t, prod[1]) + nt(onehot_t, prod[2])
    pay_o[count:, :] = jnp.zeros((48, width), BF)
    lse_t = [nt(eye, part)[:8].astype(BF) for part in pieces(lse[...], 3)]
    pay_o[count : count + 24, :count] = jnp.concatenate(lse_t, axis=0)
    pay_o[count + 24 : count + 48, :count] = jnp.concatenate(pieces(across[:8], 3), axis=0)
    for copy in copies:
        copy.wait()


def put_tiles(out, block, value):
    groups = out.shape[0]
    for n in range(value.shape[1] // 128):
        tile = block * (value.shape[1] // 128) + n
        each = (out.shape[2] - 16) // 16
        rows = pl.ds(pl.multiple_of(tile % each * 16, 16), 16)
        out[:, tile // each, rows, :] = value[:, n * 128 : (n + 1) * 128].astype(BF).reshape(groups, 16, 128)


def put_last(out, value):
    lanes = value.shape[1] // 128
    for row in range(value.shape[0] // 16):
        for n in range(lanes):
            chip = row * lanes + n
            tile = value[row * 16 : (row + 1) * 16, n * 128 : (n + 1) * 128]
            out[chip // 2, chip % 2, out.shape[2] - 16 :, :] = tile.astype(BF)


def mlp_weights_kernel(core, big, small, branch, ctx, big2, small2, branch2, ctx2, *rest):
    out_o = rest[-1]
    step = pl.program_id(0)
    last = step == pl.num_programs(0) - 1

    @pl.when(jnp.logical_not(last) & (core[0] == 0))
    def _():
        put_tiles(out_o, step, tn(big[...], small[...]) + tn(big2[...], small2[...]))

    @pl.when(jnp.logical_not(last) & (core[0] != 0))
    def _():
        put_tiles(out_o, step, tn(small[...], big[...]) + tn(small2[...], big2[...]))

    @pl.when(last)
    def _():
        put_last(out_o, tn(ctx[...], branch[...]) + tn(ctx2[...], branch2[...]))


def last_weights_kernel(core, ain, gp, columns, gsp, ain2, gp2, columns2, gsp2, out_o):
    step = pl.program_id(0)

    @pl.when(core[0] == 0)
    def _():
        put_tiles(out_o, step, tn(ain[...], gp[...]) + tn(ain2[...], gp2[...]))

    @pl.when(core[0] != 0)
    def _():
        put_tiles(out_o, step, tn(columns[...], gsp[...]) + tn(columns2[...], gsp2[...]))


def stem_back_kernel(gsp, left, right, vw, dstem, x, pack, sums1, sums2, rows_in, gpre, rows_o, g, gext, gup, stem, tiles, sem):
    count, width = gsp.shape
    ext = gext.shape[0]
    inner = slice(PAD, PAD + count)
    even, odd = slice(0, width), slice(width, 2 * width)
    g[...] = jnp.zeros_like(g)
    g[inner, :] = gsp[...].astype(F32)
    g[PAD - 1 : PAD, :] = left[...].astype(F32)
    g[PAD + count : PAD + count + 1, :] = right[...].astype(F32)
    gext[...] = g[:ext, :].astype(BF)
    gup[...] = (g[1 : ext + 1, :] * pack[:, 1:2]).astype(BF)
    gpre[:, even] = (nt(gext[...], vw[width : 2 * width, :]) * dstem[:, even]).astype(BF)
    grad_odd = nt(gext[...], vw[2 * width :, :]) + nt(gup[...], vw[:width, :])
    gpre[:, odd] = (grad_odd * dstem[:, odd]).astype(BF)
    taps = tn(x[inner, : 3 * SLOT], gpre[inner, even]) + tn(x[inner, SLOT:], gpre[inner, odd])
    mels = (stem.shape[0] - 16) // 3
    for t in range(3):
        stem[t * mels : (t + 1) * mels, :] = taps[t * SLOT : t * SLOT + mels, :]
    stem_sum = colsum(gpre[inner, even].astype(F32)) + colsum(gpre[inner, odd].astype(F32))
    stride_sum = colsum(gsp[...].astype(F32))
    rows = [stem_sum, stride_sum, sums2[0:4, :], sums1[...], jnp.zeros((2, width), F32)]
    stem[3 * mels :, :] = jnp.concatenate(rows, axis=0)
    put_last(tiles, stem[...])
    share = rows_o.shape[2]
    copy = pltpu.make_async_copy(tiles, rows_o.at[:, :, pl.ds(share - 16, 16), :], sem.at[0])
    copy.start()
    copy.wait()


def mel_kernel(gpre, sw, pack, mel_o, wbig, gx):
    count = mel_o.shape[0] // 2
    mels = mel_o.shape[1]
    inner = slice(PAD, PAD + count)
    taps_of(wbig, sw)
    gx[...] = nt(gpre[...], wbig[...])
    on_even = gx[inner, SLOT : 2 * SLOT] + pack[inner, 0:1] * gx[PAD - 1 : PAD + count - 1, 3 * SLOT :]
    on_odd = gx[inner, 2 * SLOT : 3 * SLOT] + pack[inner, 1:2] * gx[PAD + 1 : PAD + count + 1, :SLOT]
    mel_o[pl.ds(0, count, stride=2), :] = on_even[:, :mels]
    mel_o[pl.ds(1, count, stride=2), :] = on_odd[:, :mels]


def summed(parts):
    def more(n, total):
        return total + parts[n].astype(F32)

    return lax.fori_loop(1, parts.shape[0], more, parts[0].astype(F32)).astype(BF)


def spread_kernel(parts, *rest):
    out_o = rest[-1]
    total = summed(parts)

    def put(n, _):
        out_o[n] = total
        return 0

    lax.fori_loop(0, out_o.shape[0], put, 0)


def both_halves(core, mine, theirs, group, part, rows):
    a, b = mine[group, part, rows, :].astype(F32), theirs[group, part, rows, :].astype(F32)
    return jnp.where(core[0] == 0, a, b), jnp.where(core[0] == 0, b, a)


def unpack_mlp_kernel(core, mine, theirs, return_o, hidden_o, output_o):
    width = return_o.shape[1]
    lanes = width // 128
    each = (mine.shape[2] - 16) // 16

    def one(group, _):
        for tile in range(2 * each):
            rows = slice(tile % each * 16, tile % each * 16 + 16)
            first, second = both_halves(core, mine, theirs, group, tile // each, rows)
            block, n = divmod(tile, lanes)
            here = pl.ds(pl.multiple_of(block * width + group * 16, 16), 16)
            return_o[here, n * 128 : (n + 1) * 128] = first
            here = pl.ds(pl.multiple_of(group * 16, 16), 16)
            hidden_o[here, block * width + n * 128 : block * width + (n + 1) * 128] = second
        return 0

    lax.fori_loop(0, width // 16, one, 0)
    half = width // 2

    def last(row, _):
        for n in range(lanes):
            chip = slice(each * 16, each * 16 + 16)
            first, second = both_halves(core, mine, theirs, row * (lanes // 2) + n // 2, n % 2, chip)
            output_o[pl.ds(pl.multiple_of(row * 16, 16), 16), n * 128 : (n + 1) * 128] = first
            output_o[pl.ds(pl.multiple_of(half + row * 16, 16), 16), n * 128 : (n + 1) * 128] = second
        return 0

    lax.fori_loop(0, half // 16, last, 0)


def unpack_kernel(core, mine, theirs, attn_o, stride_o, stem_o, *rest):
    vectors, ends = rest[:-1], rest[-1]
    width = stride_o.shape[1]
    lanes = width // 128
    each = (mine.shape[2] - 16) // 16

    def run(first_of, second_of):
        def one(group, _):
            at = group * 16
            for tile in range(2 * each):
                rows = slice(tile % each * 16, tile % each * 16 + 16)
                first = first_of[group, tile // each, rows, :].astype(F32)
                second = second_of[group, tile // each, rows, :].astype(F32)
                attn_o[pl.ds(pl.multiple_of(at, 16), 16), tile * 128 : (tile + 1) * 128] = first
                block, n = divmod(tile, lanes)
                stride_o[pl.ds(pl.multiple_of(block * width + at, 16), 16), n * 128 : (n + 1) * 128] = second
            return 0

        lax.fori_loop(0, mine.shape[0], one, 0)

    @pl.when(core[0] == 0)
    def _():
        run(mine, theirs)

    @pl.when(core[0] != 0)
    def _():
        run(theirs, mine)

    last = slice(each * 16, each * 16 + 16)
    for row in range(ends.shape[0] // 16):
        for n in range(lanes):
            chip = row * lanes + n
            first, second = both_halves(core, mine, theirs, chip // 2, chip % 2, last)
            ends[row * 16 : row * 16 + 16, n * 128 : (n + 1) * 128] = first + second
    mels = stem_o.shape[0]
    stem_o[...] = ends[:mels, :]
    row = mels
    for out in vectors:
        for n in range(out.shape[0] // width):
            out[n * width : (n + 1) * width] = ends[row + n : row + n + 1, :].reshape(width)
        row += out.shape[0] // width


def move(block, distance):
    count = lax.axis_size("frames")
    return lax.ppermute(block, "frames", [(d, (d + distance) % count) for d in range(count)])


def swap(block):
    count = lax.axis_size("frames")
    return lax.ppermute(block, "frames", [(d, d ^ 1) for d in range(count)])


def cost(us):
    return pl.CostEstimate(flops=int(us * 1.1e9), bytes_accessed=int(us * 2e6), transcendentals=0)


def call(kernel, outs, args, scratch=(), specs=None, limit=56, us=10, out_specs=None):
    vmem = pl.BlockSpec(memory_space=pltpu.VMEM)
    return pl.pallas_call(
        kernel,
        out_shape=[jax.ShapeDtypeStruct(s, d) for s, d in outs],
        in_specs=specs if specs is not None else [vmem] * len(args),
        out_specs=out_specs if out_specs is not None else [vmem] * len(outs),
        scratch_shapes=list(scratch),
        compiler_params=pltpu.CompilerParams(vmem_limit_bytes=limit * MIB),
        cost_estimate=cost(us),
    )(*args)


MARK = ((8, 128), F32)


def chip_groups():
    chips = lax.axis_size("frames") // 2
    return [[2 * n + core for n in range(chips)] for core in range(2)]


def follow(value, other):
    hbm = pl.BlockSpec(memory_space=pl.ANY)
    return pl.pallas_call(
        lambda value_in, other_in, value_out: None,
        out_shape=jax.ShapeDtypeStruct(value.shape, value.dtype),
        in_specs=[hbm, hbm],
        out_specs=hbm,
        input_output_aliases={0: 0},
        cost_estimate=cost(1),
    )(value, other)


def over_chips(block):
    parts = block.reshape((-1,) + block.shape[2:])
    return lax.all_to_all(parts, "frames", 0, 0, axis_index_groups=chip_groups(), tiled=True)


def local(
    mel_frames, clip_lengths, valid_keys, stem_weight, stem_bias, stride_weight, stride_bias, attn_gain, attn_shift,
    attn_weight, query_bias, value_bias, output_weight, output_bias, mlp_gain, mlp_shift, hidden_weight, hidden_bias,
    return_weight, return_bias, cotangent,
):
    count, width = cotangent.shape
    ff = hidden_weight.shape[1]
    mels = mel_frames.shape[1]
    devices = lax.axis_size("frames")
    device = lax.axis_index("frames")
    core = device % 2
    nb = 2 * SIDE + 1
    ext = count + 2 * PAD
    base = (device - core - 2 * SIDE) * count

    left, right = move(mel_frames[-2:], 1), move(mel_frames[:2], -1)

    smem = pl.BlockSpec(memory_space=pltpu.SMEM)
    vmem = pl.BlockSpec(memory_space=pltpu.VMEM)
    hbm = pl.BlockSpec(memory_space=pl.ANY)
    whole = pltpu.VMEM((count, 128), jnp.int32)
    spans, pack, table, key_plan, query_plan = pl.pallas_call(
        functools.partial(tables_kernel, total=devices * count),
        out_shape=[
            jax.ShapeDtypeStruct(s, d)
            for s, d in (
                ((count, 128), jnp.int32), ((ext, 128), F32), ((count, width), F32), ((16,), jnp.int32), ((16,), jnp.int32)
            )
        ],
        in_specs=[smem] * 3,
        out_specs=[vmem] * 3 + [smem] * 2,
        scratch_shapes=[whole] * 3,
        cost_estimate=cost(4),
    )(device[None].astype(jnp.int32), clip_lengths, valid_keys)

    x, columns, dstem, dstride, layer_in, attn_in = call(
        stem_kernel,
        [
            ((ext, 4 * SLOT), BF), ((count, 3 * width), BF), ((ext, 2 * width), F32), ((count, width), F32), ((count, width), F32),
            ((count, width), BF),
        ],
        (
            mel_frames, left, right, stem_weight, stem_bias, stride_weight, stride_bias, attn_gain, attn_shift, pack, table,
        ),
        [pltpu.VMEM((2 * ext + 16, SLOT), F32), pltpu.VMEM((4 * SLOT, 2 * width), BF), pltpu.VMEM((ext, width), F32)],
        us=7,
        limit=24,
    )

    joint = jnp.concatenate([query_bias.astype(F32), jnp.zeros((width,), F32), value_bias.astype(F32)])

    def project(block):
        return (nn(block, attn_weight) + joint).astype(BF)

    def after(value, *others):
        return lax.optimization_barrier((value, *others))[0]

    def gather(block, pair):
        own, sib = {0: project(block)}, {0: project(pair)}
        ends = block, block
        done = [own[0], sib[0]]
        for k in range(1, SIDE + 1):
            ends = move(ends[0], 2), move(ends[1], -2)
            if k == 1:
                ends = after(ends[0], *done), after(ends[1], *done)
            here, there = dict(zip((-k, k), ends)), {n: swap(b) for n, b in zip((-k, k), ends)}
            for n in (-k, k):
                own[n] = project(after(here[n], *(done if k == SIDE else there.values())))
            for n in (-k, k):
                sib[n] = project(after(there[n], own[-k], own[k]))
            done += [v[n] for v in (own, sib) for n in (-k, k)]
        order = range(-SIDE, SIDE + 1)
        return [own[n] for n in order], [sib[n] for n in order]

    pair_in = swap(attn_in)
    own, sib = gather(attn_in, pair_in)
    pair_columns = lax.ppermute(columns, "frames", [(d, d + 1) for d in range(0, devices, 2)])
    reach = 2 * nb * count + KB
    pairs = width // 128
    sems = pltpu.SemaphoreType.DMA((2 * nb, 2))
    count_of = pltpu.SMEM((1,), jnp.int32)

    stacked = pltpu.VMEM((pairs, 2 * QB, 128), BF)
    summed = pltpu.VMEM((pairs, 2 * QB, 128), F32)
    score = pltpu.VMEM((2, pairs, 2 * QB, KB), F32)
    weight = pltpu.VMEM((2, pairs, 2 * QB, KB), BF)
    one_sem = pltpu.SemaphoreType.DMA((1,))
    local_query = pltpu.VMEM((count, width), BF)

    core1 = core[None].astype(jnp.int32)
    bundle = ff + 2 * width + width // 2
    block_f32 = pltpu.VMEM((count, width), F32)
    lse, layer_out, keep, send, grad_middle, pay, dlt, sums1 = call(
        layer_kernel,
        [
            ((count, 128), F32), ((count, width), BF), ((count, bundle), BF), ((count, bundle), BF), ((count, width), F32),
            ((count + 48, width), BF), ((count, 128), F32), ((8, width), F32),
        ],
        (
            key_plan, spans, *own, *sib, layer_in, cotangent, output_weight, hidden_weight, return_weight, output_bias,
            hidden_bias, return_bias, mlp_gain, mlp_shift,
        ),
        [
            block_f32, local_query, pltpu.VMEM((reach, 2 * width), BF), stacked, summed, summed, summed, summed, score, weight,
            count_of, count_of, sems, pltpu.SemaphoreType.DMA((6,)),
            block_f32, local_query, pltpu.VMEM((width, width), BF), pltpu.VMEM((width, ff), BF), pltpu.VMEM((ff, width), BF),
            block_f32, block_f32, pltpu.VMEM((2, count, bundle), BF), pltpu.SemaphoreType.DMA((2 * (ff // width) + 6,)),
        ],
        [smem, vmem] + [hbm] * (2 * nb + 5) + [vmem] * 5,
        out_specs=[vmem, vmem, hbm, hbm] + [vmem] * 4,
        us=26,
    )

    got = swap(send)
    near = {-1: move(pay, 2), 1: move(pay, -2)}

    grad_query, query_mark = call(
        query_kernel,
        [((count, width), BF), MARK],
        (key_plan, spans, pay, lse, dlt, *own, *sib),
        [
            local_query, pltpu.VMEM((reach, 2 * width), BF), stacked, stacked, summed, summed, summed, score, score, weight,
            count_of, count_of, sems, one_sem,
        ],
        [smem] + [vmem] * 4 + [hbm] * (2 * nb),
        us=15,
        limit=56,
    )
    near = {k: follow(b, query_mark) for k, b in near.items()}
    far = {-2: move(near[-1], 2), 2: move(near[1], -2)}

    blocks = ff // width
    groups = width // 16
    tiles = (groups, 2, 16 * (blocks * pairs // 2 + 1), 128)

    def at(n):
        return pl.BlockSpec((count, width), lambda i, core: (0, n))

    def each(i, core):
        return (0, jnp.minimum(i, blocks - 1))

    bundle_specs = [
        pl.BlockSpec((count, width), each), at(blocks), at(blocks + 1),
        pl.BlockSpec((count, width // 2), lambda i, core: (0, 2 * (blocks + 2))),
    ]
    mlp_both = pl.pallas_call(
        mlp_weights_kernel,
        out_shape=jax.ShapeDtypeStruct(tiles, BF),
        grid_spec=pltpu.PrefetchScalarGridSpec(
            num_scalar_prefetch=1,
            grid=(blocks + 1,),
            in_specs=bundle_specs * 2 + [hbm] * 2,
            out_specs=pl.BlockSpec(tiles, lambda i, core: (0, 0, 0, 0)),
        ),
        compiler_params=pltpu.CompilerParams(vmem_limit_bytes=60 * MIB),
        cost_estimate=cost(5.0),
    )(core1, keep, keep, keep, keep, got, got, got, got, near[-1], near[1])

    travel = {0: pay, **near, **{k: follow(b, mlp_both) for k, b in far.items()}}
    sib_pay = {k: swap(travel[k]) for k in travel}
    own_pay, sib_pay = ([v[k] for k in range(-SIDE, SIDE + 1)] for v in (travel, sib_pay))

    grad_projected, gsp, sums2 = call(
        key_kernel,
        [((count, 3 * width), BF), ((count, width), BF), ((8, width), F32)],
        (
            query_plan, spans, grad_query, attn_weight, layer_in, grad_middle, attn_gain,
            dstride, *own, *sib, *own_pay, *sib_pay,
        ),
        [
            pltpu.VMEM((count, 2 * width), BF), pltpu.VMEM((reach, width), BF), pltpu.VMEM((reach, width), BF),
            pltpu.VMEM((48, reach), BF), pltpu.VMEM((8, reach), F32), pltpu.VMEM((8, reach), F32), stacked, stacked, summed, summed, score, score, weight,
            weight, count_of, count_of, sems, pltpu.SemaphoreType.DMA((2 * nb, 1)),
            one_sem,
        ],
        [smem] + [vmem] * 7 + [hbm] * (4 * nb),
        us=18,
        limit=56,
    )
    mlp_parts = over_chips(mlp_both)
    (mlp_spread,) = call(
        spread_kernel, [(mlp_parts.shape, BF)], (mlp_parts, sums2), specs=[vmem, hbm], us=3, limit=12
    )
    mlp_mine = over_chips(mlp_spread[:, None]).reshape(tiles)

    left, right = move(gsp[-1:], 1), move(gsp[:1], -1)

    gp_pair, gsp_pair = swap(grad_projected), swap(gsp)
    def whole_block(i, core):
        return (0, 0)

    def column_block(i, core):
        return (0, i)

    last_tiles = (groups, 2, 16 * (3 * pairs // 2 + 1), 128)
    last_specs = [pl.BlockSpec((count, width), m) for m in (whole_block, column_block, column_block, whole_block)]
    both = pl.pallas_call(
        last_weights_kernel,
        out_shape=jax.ShapeDtypeStruct(last_tiles, BF),
        grid_spec=pltpu.PrefetchScalarGridSpec(
            num_scalar_prefetch=1,
            grid=(3,),
            in_specs=last_specs * 2,
            out_specs=pl.BlockSpec(last_tiles, lambda i, core: (0, 0, 0, 0)),
        ),
        compiler_params=pltpu.CompilerParams(vmem_limit_bytes=20 * MIB),
        cost_estimate=cost(3),
    )(core1, attn_in, grad_projected, columns, gsp, pair_in, gp_pair, pair_columns, gsp_pair)
    gpre, both = pl.pallas_call(
        stem_back_kernel,
        out_shape=[jax.ShapeDtypeStruct((ext, 2 * width), BF), jax.ShapeDtypeStruct(last_tiles, BF)],
        in_specs=[vmem] * 9 + [hbm],
        out_specs=[vmem, hbm],
        scratch_shapes=[
            pltpu.VMEM((ext + 8, width), F32), pltpu.VMEM((ext, width), BF), pltpu.VMEM((ext, width), BF),
            pltpu.VMEM((3 * mels + 16, width), F32), pltpu.VMEM((groups, 2, 16, 128), BF), one_sem,
        ],
        input_output_aliases={9: 1},
        compiler_params=pltpu.CompilerParams(vmem_limit_bytes=20 * MIB),
        cost_estimate=cost(4),
    )(gsp, left, right, stride_weight, dstem, x, pack, sums1, sums2, both)

    (mel_grad,) = call(
        mel_kernel,
        [((2 * count, mels), F32)],
        (gpre, stem_weight, pack),
        [pltpu.VMEM((4 * SLOT, 2 * width), BF), pltpu.VMEM((ext, 4 * SLOT), F32)],
        us=3,
        limit=16,
    )

    mlp_mine = follow(mlp_mine, both)
    grad_return_weight, grad_hidden_weight, grad_output_weight = call(
        unpack_mlp_kernel,
        [((ff, width), F32), ((width, ff), F32), ((width, width), F32)],
        (core1, mlp_mine, swap(mlp_mine)),
        specs=[smem, vmem, vmem],
        us=5,
        limit=24,
    )
    parts = over_chips(both)
    (spread,) = call(
        spread_kernel, [(parts.shape, BF)], (parts, mel_grad, grad_output_weight), specs=[vmem, hbm, hbm], us=3, limit=12
    )
    mine = over_chips(spread[:, None]).reshape(last_tiles)
    sizes = [width] * 9 + [ff, width]
    grad_attn_weight, grad_stride_weight, grad_stem_weight, *bias = call(
        unpack_kernel,
        [((width, 3 * width), F32), ((3 * width, width), F32), ((3 * mels, width), F32)] + [((n,), F32) for n in sizes],
        (core1, mine, swap(mine)),
        [pltpu.VMEM((3 * mels + 16, width), F32)],
        [smem, vmem, vmem],
        us=6,
        limit=22,
    )
    return (
        layer_out, mel_grad, grad_stem_weight, bias[0], grad_stride_weight, bias[1], bias[2], bias[3], grad_attn_weight,
        bias[4], bias[5], grad_output_weight, bias[6], bias[7], bias[8], grad_hidden_weight, bias[9],
        grad_return_weight, bias[10],
    )


def solution(mesh):
    split = P("frames", None)
    in_specs = (split,) + (P(),) * 19 + (split,)
    out_specs = (split, split) + (P(),) * 17
    return jax.shard_map(local, mesh=mesh, in_specs=in_specs, out_specs=out_specs, check_vma=False)
```

```python
import functools
import math

import jax
import jax.numpy as jnp
from jax import lax
from jax.experimental import pallas as pl
from jax.experimental.pallas import tpu as pltpu
from jax.sharding import PartitionSpec as P

HEADS = 8
SIDE = 2
QB = 128
KB = 256
PAD = 16
SLOT = 128
NEG = -1e30
BF = jnp.bfloat16
F32 = jnp.float32
MIB = 1 << 20


def nn(a, b):
    return lax.dot_general(a, b, (((1,), (0,)), ((), ())), preferred_element_type=F32)


def nt(a, b):
    return lax.dot_general(a, b, (((1,), (1,)), ((), ())), preferred_element_type=F32)


def tn(a, b):
    return lax.dot_general(a, b, (((0,), (0,)), ((), ())), preferred_element_type=F32)


def gelu_pair(x):
    bell = jnp.exp(-0.5 * x * x)
    t = 1.0 / (1.0 + 0.2316419 * jnp.abs(x))
    poly = 0.127414796 + t * (-0.142248368 + t * (0.7107068705 + t * (-0.7265760135 + t * 0.5307027145)))
    tail = bell * t * poly
    phi = jnp.where(x >= 0, 1.0 - tail, tail)
    return x * phi, phi + 0.3989422804 * x * bell


def norm_parts(x):
    center = jnp.mean(x, axis=-1, keepdims=True)
    centered = x - center
    rstd = lax.rsqrt(jnp.mean(centered * centered, axis=-1, keepdims=True) + 1e-05)
    return centered * rstd, rstd


def norm_back(grad, xhat, rstd, gain):
    inner = grad * gain
    m1 = jnp.mean(inner, axis=-1, keepdims=True)
    m2 = jnp.mean(inner * xhat, axis=-1, keepdims=True)
    return rstd * (inner - m1 - xhat * m2)


def vector(ref):
    return ref[...].astype(F32).reshape(1, -1)


def colsum(x):
    return jnp.sum(x, axis=0, keepdims=True)


def halves(x, low):
    zero = jnp.zeros_like(x)
    return jnp.concatenate([jnp.where(low, x, zero), jnp.where(low, zero, x)], axis=0)


def pick(x, low):
    return jnp.where(low, x[:QB], x[QB:])


def wide(x):
    return jnp.concatenate([x, x], axis=1)


def tall(x):
    return jnp.concatenate([x, x], axis=0)


def tables_kernel(device, lengths, valids, spans_o, pack_o, table_o, keys_o, queries_o, start_s, length_s, valid_s, *, total):
    count, width = table_o.shape
    base = (device[0] - device[0] % 2 - 2 * SIDE) * count
    first = device[0] * count
    token = first + lax.broadcasted_iota(jnp.int32, (count, 128), 0)
    row = lax.broadcasted_iota(jnp.int32, pack_o.shape, 0) + lax.broadcasted_iota(jnp.int32, pack_o.shape, 1) - PAD
    here = (row >= 0) & (row <= count) & (first + row < total)
    pack_o[...] = jnp.where(here, 1.0, 0.0)
    keys_o[0] = queries_o[0] = device[0] % 2
    keys_o[3] = queries_o[3] = 1 - 2 * (device[0] // 2 % 2)

    def clip(c, start):
        length = lengths[c]
        valid = jnp.minimum(valids[c], length)
        end = start + length

        @pl.when((start < first + count) & (end > first))
        def _():
            inside = (token >= start) & (token < end)
            start_s[...] = jnp.where(inside, start, start_s[...])
            length_s[...] = jnp.where(inside, length, length_s[...])
            valid_s[...] = jnp.where(inside, valid, valid_s[...])
            for n in range(count // QB):
                at = first + n * QB

                @pl.when((start <= at) & (at < end))
                def _():
                    keys_o[4 + 2 * n] = queries_o[4 + 2 * n] = ((start - base) >> 7) << 7

                @pl.when((start < at + QB) & (at + QB <= end))
                def _():
                    keys_o[5 + 2 * n] = start + valid - base
                    queries_o[5 + 2 * n] = end - base

        @pl.when((start >= first) & (start <= first + count))
        def _():
            pack_o[...] = jnp.where(first + row == start, 0.0, pack_o[...])

        return end

    lax.fori_loop(0, lengths.shape[0], clip, 0)
    for plan in (keys_o, queries_o):
        low, high = plan[4], 0
        for n in range(count // QB):
            steps = (plan[5 + 2 * n] - plan[4 + 2 * n] + KB - 1) // KB
            plan[5 + 2 * n] = steps
            low = jnp.minimum(low, plan[4 + 2 * n])
            high = jnp.maximum(high, plan[4 + 2 * n] + steps * KB)
        plan[1], plan[2] = low, high
    lane = lax.broadcasted_iota(jnp.int32, (count, 128), 1)
    key_lo = start_s[...] - base
    position = token - start_s[...]
    is_key = position < valid_s[...]
    query_lo = jnp.where(is_key, key_lo, 1 << 20)
    query_hi = jnp.where(is_key, key_lo + length_s[...], 0)
    first_two = jnp.where(lane == 0, key_lo, key_lo + valid_s[...])
    spans_o[...] = jnp.where(lane < 2, first_two, jnp.where(lane == 2, query_lo, query_hi))
    half = width // 2
    number = lax.broadcasted_iota(jnp.int32, (1, half), 1).astype(F32)
    rates = jnp.exp(number * (-math.log(10000.0) / (half - 1)))
    angles = wide(position.astype(F32)) * rates
    table_o[:, :half] = jnp.sin(angles)
    table_o[:, half:] = jnp.cos(angles)


def taps_of(wbig, sw):
    mels, width = sw.shape[0] // 3, sw.shape[1]
    wbig[...] = jnp.zeros_like(wbig)
    for t in range(3):
        tap = sw[t * mels : (t + 1) * mels, :]
        wbig[t * SLOT : t * SLOT + mels, :width] = tap
        wbig[(t + 1) * SLOT : (t + 1) * SLOT + mels, width:] = tap


def stem_kernel(
    mel, left, right, sw, sbias, vw, vbias, gain, shift, pack, table,
    x_o, cols_o, dstem_o, dstride_o, lin_o, ain_o, m, wbig, shifted,
):
    count, width = lin_o.shape
    frames, mels = mel.shape
    ext = x_o.shape[0]
    taps_of(wbig, sw)
    top = 2 * PAD + 8
    m[...] = jnp.zeros_like(m)
    m[top : top + frames, :mels] = mel[...].astype(F32)
    m[top - 2 : top, :mels] = left[...].astype(F32)
    m[top + frames : top + frames + 2, :mels] = right[...].astype(F32)
    opn, opn_next = pack[:, 0:1], pack[:, 1:2]
    x_o[:, :SLOT] = (m[pl.ds(7, ext, stride=2), :] * opn).astype(BF)
    x_o[:, SLOT : 2 * SLOT] = m[pl.ds(8, ext, stride=2), :].astype(BF)
    x_o[:, 2 * SLOT : 3 * SLOT] = m[pl.ds(9, ext, stride=2), :].astype(BF)
    x_o[:, 3 * SLOT :] = (m[pl.ds(10, ext, stride=2), :] * opn_next).astype(BF)
    inner = slice(PAD, PAD + count)
    even, odd = slice(0, width), slice(width, 2 * width)
    act, dact = gelu_pair(nn(x_o[...], wbig[:, even]) + vector(sbias))
    dstem_o[:, even] = dact
    cols_o[:, width : 2 * width] = act[inner].astype(BF)
    act, dact = gelu_pair(nn(x_o[...], wbig[:, odd]) + vector(sbias))
    dstem_o[:, odd] = dact
    cols_o[:, 2 * width :] = act[inner].astype(BF)
    shifted[...] = act
    cols_o[:, :width] = (shifted[PAD - 1 : PAD + count - 1, :] * pack[inner, 0:1]).astype(BF)
    pre = nn(cols_o[...], vw[...]) + vector(vbias)
    act2, dact2 = gelu_pair(pre)
    dstride_o[...] = dact2
    lin = act2 + table[...]
    lin_o[...] = lin
    xhat, _ = norm_parts(lin)
    ain_o[...] = (xhat * vector(gain) + vector(shift)).astype(BF)


def needed(sc, block, count):
    return (block * count < sc[2]) & ((block + 1) * count > sc[1])


def start_copies(sc, pairs, sem, count, begun, upto):
    for block, copies in pairs:

        @pl.when(needed(sc, block, count) & (block >= begun[0]) & (block < upto))
        def _():
            for m, (src, dst) in enumerate(copies):
                pltpu.make_async_copy(src, dst, sem.at[block, m]).start()

    begun[0] = jnp.maximum(begun[0], upto)


def wait_until(sc, end, copies, sem, count, there, ahead=None):
    def one(block, _):
        @pl.when(needed(sc, block, count))
        def _():
            for m, (src, dst) in enumerate(copies(block)):
                pltpu.make_async_copy(src, dst, sem.at[block, m]).wait()

        return 0

    upto = jnp.minimum((end + count - 1) // count, 2 * (2 * SIDE + 1))
    if ahead is not None:

        @pl.when(upto > there[0])
        def _():
            ahead(upto + 2)

    lax.fori_loop(there[0], upto, one, 0)
    there[0] = jnp.maximum(there[0], upto)


def window(sc, own, sib):
    core, turn = sc[0], sc[3]
    out = []
    for k in range(2 * SIDE + 1):
        chip = SIDE + turn * (k - SIDE)
        out += [(2 * chip + core, own[k]), (2 * chip + 1 - core, sib[k])]
    return out


def rows_of(block, count):
    return pl.ds(pl.multiple_of(block * count, count), count)


def in_range(lo, hi, start):
    col = start + lax.broadcasted_iota(jnp.int32, (QB, KB), 1)
    return jnp.where((col >= lo) & (col < hi), 0.0, NEG)


def chunks(first, steps, step, wait):
    def two(n, _):
        wait(first + (2 * n + 2) * KB)
        step(2 * n, 2)
        return 0

    lax.fori_loop(0, steps // 2, two, 0)

    @pl.when(steps % 2 == 1)
    def _():
        wait(first + steps * KB)
        step(steps - 1, 1)


def layer_kernel(*refs):
    nb = 2 * SIDE + 1
    sc, span_ref = refs[:2]
    own, sib = refs[2 : 2 + nb], refs[2 + nb : 2 + 2 * nb]
    at = 2 + 2 * nb
    fetched, vectors, outs = refs[at : at + 5], refs[at + 5 : at + 10], refs[at + 10 : at + 18]
    lse_o = outs[0]
    scratch = refs[at + 18 :]
    ctx_o, local_ref, kv, q2, acc, peak, total, scale, s, e, there, begun, sem, sem2 = scratch[:14]
    held, mlp_scratch = scratch[14:19], scratch[19:]
    count, width = ctx_o.shape
    late = [pltpu.make_async_copy(src, dst, sem2.at[1 + n]) for n, (src, dst) in enumerate(zip(fetched, held))]
    span = 2 * nb * count
    pairs = width // 128
    kv[span:, :] = jnp.zeros((kv.shape[0] - span, 2 * width), BF)
    there[0] = 0

    def copies(block, src=own[0]):
        return [(src.at[:, pl.ds(width, 2 * width)], kv.at[rows_of(block, count), :])]

    local = pltpu.make_async_copy(own[SIDE].at[:, pl.ds(0, width)], local_ref, sem2.at[0])
    local.start()
    begun[0] = 0
    sources = [(block, copies(block, src)) for block, src in window(sc, own, sib)]

    def ahead(upto):
        start_copies(sc, sources, sem, count, begun, upto)

    ahead(sc[1] // count + 3)
    for copy in late:
        copy.start()
    local.wait()

    def wait(end):
        wait_until(sc, end, copies, sem, count, there, ahead)

    low = lax.broadcasted_iota(jnp.int32, (QB, 128), 1) < 64
    lanes = lax.broadcasted_iota(jnp.int32, (QB, 128), 1)

    def one(i, _):
        rows = pl.ds(pl.multiple_of(i * QB, QB), QB)
        for p in range(pairs):
            q2[p] = halves(local_ref[rows, p * 128 : (p + 1) * 128], low) * jnp.asarray(0.125, BF)
            acc[p] = jnp.zeros_like(acc[p])
            peak[p] = jnp.full_like(peak[p], NEG)
            total[p] = jnp.zeros_like(total[p])
        lo, hi = span_ref[rows, 0:1], span_ref[rows, 1:2]

        def step(n, parts):
            start = sc[4 + 2 * i] + n * KB
            keys = [pl.ds(pl.multiple_of(start + u * KB, 128), KB) for u in range(parts)]
            for u in range(parts):
                bias = tall(in_range(lo, hi, start + u * KB))
                for p in range(pairs):
                    s[u, p] = nt(q2[p], kv[keys[u], p * 128 : (p + 1) * 128]) + bias
            for p in range(pairs):
                best = functools.reduce(jnp.maximum, [s[u, p] for u in range(parts)])
                old = peak[p]
                top = jnp.maximum(old, jnp.max(best, axis=1, keepdims=True))
                peak[p] = top
                scale[p] = jnp.exp(old - top)
            for p in range(pairs):
                total[p] = scale[p] * total[p]
                for u in range(parts):
                    grown = jnp.exp(s[u, p] - wide(peak[p]))
                    e[u, p] = grown.astype(BF)
                    total[p] = total[p] + (grown[:, :128] + grown[:, 128:])
            for p in range(pairs):
                value = [kv[keys[u], width + p * 128 : width + (p + 1) * 128] for u in range(parts)]
                acc[p] = scale[p] * acc[p] + functools.reduce(jnp.add, [nn(e[u, p], value[u]) for u in range(parts)])

        chunks(sc[4 + 2 * i], sc[5 + 2 * i], step, wait)
        lse = jnp.zeros((QB, 128), F32)
        for p in range(pairs):
            row_total = jnp.sum(total[p], axis=1, keepdims=True)
            ctx_o[rows, p * 128 : (p + 1) * 128] = pick(acc[p] / row_total, low)
            both = peak[p] + jnp.log(row_total)
            lse = jnp.where(lanes == 2 * p, both[:QB], lse)
            lse = jnp.where(lanes == 2 * p + 1, both[QB:], lse)
        lse_o[rows, :] = lse
        return 0

    lax.fori_loop(0, count // QB, one, 0)
    wait(span)
    for copy in late:
        copy.wait()
    mlp(sc, ctx_o, lse_o, *held, *vectors, *outs[1:], *mlp_scratch)


def query_kernel(*refs):
    nb = 2 * SIDE + 1
    sc, span_ref, pay_ref, lse_ref, dlt_ref = refs[:5]
    own, sib = refs[5 : 5 + nb], refs[5 + nb : 5 + 2 * nb]
    dq_o, mark, local_ref, kv, q2, do2, acc, lse2, dlt2, s, d, ds, there, begun, sem, sem2 = refs[5 + 2 * nb :]
    mark[...] = jnp.zeros_like(mark)
    count, width = dq_o.shape
    span = 2 * nb * count
    pairs = width // 128
    kv[span:, :] = jnp.zeros((kv.shape[0] - span, 2 * width), BF)
    there[0] = 0

    def copies(block, src=own[0]):
        return [(src.at[:, pl.ds(width, 2 * width)], kv.at[rows_of(block, count), :])]

    local = pltpu.make_async_copy(own[SIDE].at[:, pl.ds(0, width)], local_ref, sem2.at[0])
    local.start()
    begun[0] = 0
    sources = [(block, copies(block, src)) for block, src in window(sc, own, sib)]

    def ahead(upto):
        start_copies(sc, sources, sem, count, begun, upto)

    ahead(sc[1] // count + 3)
    local.wait()

    def wait(end):
        wait_until(sc, end, copies, sem, count, there, ahead)

    low = lax.broadcasted_iota(jnp.int32, (QB, 128), 1) < 64

    def one(i, _):
        rows = pl.ds(pl.multiple_of(i * QB, QB), QB)
        lse, dlt = lse_ref[rows, :], dlt_ref[rows, :]
        for p in range(pairs):
            q2[p] = halves(local_ref[rows, p * 128 : (p + 1) * 128], low) * jnp.asarray(0.125, BF)
            do2[p] = halves(pay_ref[rows, p * 128 : (p + 1) * 128], low)
            acc[p] = jnp.zeros_like(acc[p])
            for h in range(2):
                part = pl.ds(h * QB, QB)
                lse2[p, part, :] = jnp.broadcast_to(lse[:, 2 * p + h : 2 * p + h + 1], (QB, 128))
                dlt2[p, part, :] = jnp.broadcast_to(dlt[:, 2 * p + h : 2 * p + h + 1], (QB, 128))
        lo, hi = span_ref[rows, 0:1], span_ref[rows, 1:2]

        def step(n, parts):
            start = sc[4 + 2 * i] + n * KB
            keys = [pl.ds(pl.multiple_of(start + u * KB, 128), KB) for u in range(parts)]
            for u in range(parts):
                bias = tall(in_range(lo, hi, start + u * KB))
                for p in range(pairs):
                    s[u, p] = nt(q2[p], kv[keys[u], p * 128 : (p + 1) * 128]) + bias
                    d[u, p] = nt(do2[p], kv[keys[u], width + p * 128 : width + (p + 1) * 128])
            for u in range(parts):
                for p in range(pairs):
                    e = jnp.exp(s[u, p] - wide(lse2[p]))
                    ds[u, p] = (e * (d[u, p] - wide(dlt2[p]))).astype(BF)
            for p in range(pairs):
                more = [nn(ds[u, p], kv[keys[u], p * 128 : (p + 1) * 128]) for u in range(parts)]
                acc[p] = acc[p] + functools.reduce(jnp.add, more)

        chunks(sc[4 + 2 * i], sc[5 + 2 * i], step, wait)
        for p in range(pairs):
            dq_o[rows, p * 128 : (p + 1) * 128] = (pick(acc[p], low) * 0.125).astype(BF)
        return 0

    lax.fori_loop(0, count // QB, one, 0)
    wait(span)


def key_kernel(*refs):
    nb = 2 * SIDE + 1
    sc, span_ref, dq_ref, w_ref, lin_ref, gm_ref, gain, dstride_ref = refs[:8]
    own, sib = refs[8 : 8 + nb], refs[8 + nb : 8 + 2 * nb]
    ownp, sibp = refs[8 + 2 * nb : 8 + 3 * nb], refs[8 + 3 * nb : 8 + 4 * nb]
    gp_o, gsp_o, sums_o, kvl, q, do, stat, lse, dlt, k2, v2, dk, dv, s, d, e, ds, there, begun, sem, sem2, sem3 = refs[8 + 4 * nb :]
    count, width = gsp_o.shape
    span = 2 * nb * count
    pairs = width // 128
    rest = q.shape[0] - span
    q[span:, :] = jnp.zeros((rest, width), BF)
    do[span:, :] = jnp.zeros((rest, width), BF)
    stat[:, span:] = jnp.zeros((stat.shape[0], rest), BF)
    there[0] = 0

    def copies(block, src=own[0], pay=ownp[0]):
        return [
            (src.at[:, pl.ds(0, width)], q.at[rows_of(block, count), :]),
            (pay.at[pl.ds(0, count), :], do.at[rows_of(block, count), :]),
        ]

    def side(block, pay=ownp[0]):
        return [(pay.at[pl.ds(count, 48), pl.ds(0, count)], stat.at[:, rows_of(block, count)])]

    local = pltpu.make_async_copy(own[SIDE].at[:, pl.ds(width, 2 * width)], kvl, sem3.at[0])
    local.start()
    pairs_of = list(zip(window(sc, own, sib), window(sc, ownp, sibp)))
    begun[0] = 0
    start_copies(sc, [(block, side(block, pay)) for _, (block, pay) in pairs_of], sem2, count, begun, 2 * nb)
    begun[0] = 0
    sources = [(block, copies(block, src, pay)) for (block, src), (_, pay) in pairs_of]

    def ahead(upto):
        start_copies(sc, sources, sem, count, begun, upto)

    ahead(sc[1] // count + 3)

    def wait(end):
        wait_until(sc, end, copies, sem, count, there, ahead)

    local.wait()
    wait_until(sc, span, side, sem2, count, there)
    there[0] = 0
    lse[...] = stat[0:8, :].astype(F32) + stat[8:16, :].astype(F32) + stat[16:24, :].astype(F32)
    dlt[...] = stat[24:32, :].astype(F32) + stat[32:40, :].astype(F32) + stat[40:48, :].astype(F32)
    low = lax.broadcasted_iota(jnp.int32, (QB, 128), 1) < 64

    def one(i, _):
        rows = pl.ds(pl.multiple_of(i * QB, QB), QB)
        for p in range(pairs):
            k2[p] = halves(kvl[rows, p * 128 : (p + 1) * 128], low) * jnp.asarray(0.125, BF)
            v2[p] = halves(kvl[rows, width + p * 128 : width + (p + 1) * 128], low)
            dk[p] = jnp.zeros_like(dk[p])
            dv[p] = jnp.zeros_like(dv[p])
        lo, hi = span_ref[rows, 2:3], span_ref[rows, 3:4]

        def step(n, parts):
            start = sc[4 + 2 * i] + n * KB
            queries = [pl.ds(pl.multiple_of(start + u * KB, 128), KB) for u in range(parts)]
            for u in range(parts):
                for p in range(pairs):
                    lanes = slice(p * 128, (p + 1) * 128)
                    s[u, p] = nt(k2[p], q[queries[u], lanes])
                    d[u, p] = nt(v2[p], do[queries[u], lanes])
            for u in range(parts):
                bias = in_range(lo, hi, start + u * KB)
                for p in range(pairs):
                    for h in range(2):
                        part = slice(h * QB, (h + 1) * QB)
                        head = slice(2 * p + h, 2 * p + h + 1)
                        grown = jnp.exp(s[u, p, part] + (bias - lse[head, queries[u]]))
                        e[u, p, part] = grown.astype(BF)
                        ds[u, p, part] = (grown * (d[u, p, part] - dlt[head, queries[u]])).astype(BF)
            for p in range(pairs):
                lanes = slice(p * 128, (p + 1) * 128)
                dv[p] = dv[p] + functools.reduce(jnp.add, [nn(e[u, p], do[queries[u], lanes]) for u in range(parts)])
                dk[p] = dk[p] + functools.reduce(jnp.add, [nn(ds[u, p], q[queries[u], lanes]) for u in range(parts)])

        chunks(sc[4 + 2 * i], sc[5 + 2 * i], step, wait)
        for p in range(pairs):
            gp_o[rows, width + p * 128 : width + (p + 1) * 128] = (pick(dk[p], low) * 0.125).astype(BF)
            gp_o[rows, 2 * width + p * 128 : 2 * width + (p + 1) * 128] = pick(dv[p], low).astype(BF)
        return 0

    lax.fori_loop(0, count // QB, one, 0)
    wait(span)
    gp_o[:, :width] = dq_ref[...]
    grad = nt(gp_o[...], w_ref[...])
    xhat, rstd = norm_parts(lin_ref[...])
    total = gm_ref[...] + norm_back(grad, xhat, rstd, vector(gain))
    gsp_o[...] = (total * dstride_ref[...]).astype(BF)
    sums_o[0:1, :] = colsum(grad * xhat)
    sums_o[1:2, :] = colsum(grad)
    sums_o[2:3, :] = colsum(gp_o[:, :width].astype(F32))
    sums_o[3:4, :] = colsum(gp_o[:, 2 * width :].astype(F32))
    sums_o[4:8, :] = jnp.zeros((4, width), F32)


def pieces(x, n):
    out = []
    for _ in range(n):
        part = x.astype(BF)
        out.append(part)
        x = x - part.astype(F32)
    return out


def mlp(
    core, ctx, lse, lin, dy, wo, w1, w2, bo, b1, b2, gain_ref, shift,
    out_o, keep_o, send_o, gm_o, pay_o, dlt_o, sums_o, out_acc, gmi_acc, roles, sem,
):
    count, width = lin.shape
    ff = w1.shape[1]

    copies = []

    def give(role, at, size, value):
        cols = slice(at, at + size)
        roles[role, :, cols] = value
        number = len(copies)
        source = roles.at[role, :, pl.ds(at, size)]
        here = pltpu.make_async_copy(source, keep_o.at[:, pl.ds(at, size)], sem.at[number])
        there = pltpu.make_async_copy(source, send_o.at[:, pl.ds(at, size)], sem.at[number])
        copies.append(here)

        @pl.when(core[0] == role)
        def _():
            here.start()

        @pl.when(core[0] != role)
        def _():
            there.start()

        return roles.at[role, :, cols]

    context = ctx[...]
    ctx_b = context.astype(BF)
    for role in range(2):
        give(role, ff + 2 * width, width // 2, ctx_b[:, role * width // 2 : (role + 1) * width // 2])
    give(0, ff, width, dy[...])
    middle = lin[...] + nn(ctx_b, wo[...]) + vector(bo)
    xhat, rstd = norm_parts(middle)
    gain = vector(gain_ref)
    mi = give(1, ff, width, (xhat * gain + vector(shift)).astype(BF))
    grad_out = dy[...].astype(F32)
    sums_o[7:8, :] = colsum(grad_out)
    for f in range(ff // width):
        cols = slice(f * width, (f + 1) * width)
        act, dact = gelu_pair(nn(mi[...], w1[:, cols]) + vector(b1.at[cols]))
        act = give(0, f * width, width, act.astype(BF))
        ghp = (nt(dy[...], w2[cols, :]) * dact).astype(BF)
        ghp_ref = give(1, f * width, width, ghp)
        sums_o[3 + f : 4 + f, :] = colsum(ghp.astype(F32))
        more = nn(act[...], w2[cols, :])
        gmore = nt(ghp_ref[...], w1[:, cols])
        if f == 0:
            out_acc[...] = middle + vector(b2) + more
            gmi_acc[...] = gmore
        else:
            out_acc[...] = out_acc[...] + more
            gmi_acc[...] = gmi_acc[...] + gmore
    out_o[...] = out_acc[...].astype(BF)
    gmi = gmi_acc[...]
    sums_o[1:2, :] = colsum(gmi * xhat)
    sums_o[2:3, :] = colsum(gmi)
    grad_middle = grad_out + norm_back(gmi, xhat, rstd, gain)
    gm_o[...] = grad_middle
    branch = grad_middle.astype(BF)
    for role in range(2):
        give(role, ff + width, width, branch)
    sums_o[0:1, :] = colsum(branch.astype(F32))
    gctx = nt(branch, wo[...]).astype(BF)
    pay_o[:count, :] = gctx
    prod = pieces(gctx.astype(F32) * context, 3)
    head = width // HEADS

    def is_head(shape, feature, number):
        feature, number = (lax.broadcasted_iota(jnp.int32, shape, n) for n in (feature, number))
        return jnp.where(feature // head == number, 1.0, 0.0).astype(BF)

    onehot, onehot_t = is_head((width, 128), 0, 1), is_head((16, width), 1, 0)
    eye = lax.broadcasted_iota(jnp.int32, (16, 128), 0) == lax.broadcasted_iota(jnp.int32, (16, 128), 1)
    eye = jnp.where(eye, 1.0, 0.0).astype(BF)
    dlt_o[...] = nn(prod[0], onehot) + nn(prod[1], onehot) + nn(prod[2], onehot)
    across = nt(onehot_t, prod[0]) + nt(onehot_t, prod[1]) + nt(onehot_t, prod[2])
    pay_o[count:, :] = jnp.zeros((48, width), BF)
    lse_t = [nt(eye, part)[:8].astype(BF) for part in pieces(lse[...], 3)]
    pay_o[count : count + 24, :count] = jnp.concatenate(lse_t, axis=0)
    pay_o[count + 24 : count + 48, :count] = jnp.concatenate(pieces(across[:8], 3), axis=0)
    for copy in copies:
        copy.wait()


def put_tiles(out, block, value):
    groups = out.shape[0]
    for n in range(value.shape[1] // 128):
        tile = block * (value.shape[1] // 128) + n
        each = (out.shape[2] - 16) // 16
        rows = pl.ds(pl.multiple_of(tile % each * 16, 16), 16)
        out[:, tile // each, rows, :] = value[:, n * 128 : (n + 1) * 128].astype(BF).reshape(groups, 16, 128)


def put_last(out, value):
    lanes = value.shape[1] // 128
    for row in range(value.shape[0] // 16):
        for n in range(lanes):
            chip = row * lanes + n
            tile = value[row * 16 : (row + 1) * 16, n * 128 : (n + 1) * 128]
            out[chip // 2, chip % 2, out.shape[2] - 16 :, :] = tile.astype(BF)


def mlp_weights_kernel(core, big, small, branch, ctx, big2, small2, branch2, ctx2, *rest):
    out_o = rest[-1]
    step = pl.program_id(0)
    last = step == pl.num_programs(0) - 1

    @pl.when(jnp.logical_not(last) & (core[0] == 0))
    def _():
        put_tiles(out_o, step, tn(big[...], small[...]) + tn(big2[...], small2[...]))

    @pl.when(jnp.logical_not(last) & (core[0] != 0))
    def _():
        put_tiles(out_o, step, tn(small[...], big[...]) + tn(small2[...], big2[...]))

    @pl.when(last)
    def _():
        put_last(out_o, tn(ctx[...], branch[...]) + tn(ctx2[...], branch2[...]))


def last_weights_kernel(core, ain, gp, columns, gsp, ain2, gp2, columns2, gsp2, out_o):
    step = pl.program_id(0)

    @pl.when(core[0] == 0)
    def _():
        put_tiles(out_o, step, tn(ain[...], gp[...]) + tn(ain2[...], gp2[...]))

    @pl.when(core[0] != 0)
    def _():
        put_tiles(out_o, step, tn(columns[...], gsp[...]) + tn(columns2[...], gsp2[...]))


def stem_back_kernel(gsp, left, right, vw, dstem, x, pack, sums1, sums2, rows_in, gpre, rows_o, g, gext, gup, stem, tiles, sem):
    count, width = gsp.shape
    ext = gext.shape[0]
    inner = slice(PAD, PAD + count)
    even, odd = slice(0, width), slice(width, 2 * width)
    g[...] = jnp.zeros_like(g)
    g[inner, :] = gsp[...].astype(F32)
    g[PAD - 1 : PAD, :] = left[...].astype(F32)
    g[PAD + count : PAD + count + 1, :] = right[...].astype(F32)
    gext[...] = g[:ext, :].astype(BF)
    gup[...] = (g[1 : ext + 1, :] * pack[:, 1:2]).astype(BF)
    gpre[:, even] = (nt(gext[...], vw[width : 2 * width, :]) * dstem[:, even]).astype(BF)
    grad_odd = nt(gext[...], vw[2 * width :, :]) + nt(gup[...], vw[:width, :])
    gpre[:, odd] = (grad_odd * dstem[:, odd]).astype(BF)
    taps = tn(x[inner, : 3 * SLOT], gpre[inner, even]) + tn(x[inner, SLOT:], gpre[inner, odd])
    mels = (stem.shape[0] - 16) // 3
    for t in range(3):
        stem[t * mels : (t + 1) * mels, :] = taps[t * SLOT : t * SLOT + mels, :]
    stem_sum = colsum(gpre[inner, even].astype(F32)) + colsum(gpre[inner, odd].astype(F32))
    stride_sum = colsum(gsp[...].astype(F32))
    rows = [stem_sum, stride_sum, sums2[0:4, :], sums1[...], jnp.zeros((2, width), F32)]
    stem[3 * mels :, :] = jnp.concatenate(rows, axis=0)
    put_last(tiles, stem[...])
    share = rows_o.shape[2]
    copy = pltpu.make_async_copy(tiles, rows_o.at[:, :, pl.ds(share - 16, 16), :], sem.at[0])
    copy.start()
    copy.wait()


def mel_kernel(gpre, sw, pack, mel_o, wbig, gx):
    count = mel_o.shape[0] // 2
    mels = mel_o.shape[1]
    inner = slice(PAD, PAD + count)
    taps_of(wbig, sw)
    gx[...] = nt(gpre[...], wbig[...])
    on_even = gx[inner, SLOT : 2 * SLOT] + pack[inner, 0:1] * gx[PAD - 1 : PAD + count - 1, 3 * SLOT :]
    on_odd = gx[inner, 2 * SLOT : 3 * SLOT] + pack[inner, 1:2] * gx[PAD + 1 : PAD + count + 1, :SLOT]
    mel_o[pl.ds(0, count, stride=2), :] = on_even[:, :mels]
    mel_o[pl.ds(1, count, stride=2), :] = on_odd[:, :mels]


def summed(parts):
    def more(n, total):
        return total + parts[n].astype(F32)

    return lax.fori_loop(1, parts.shape[0], more, parts[0].astype(F32)).astype(BF)


def spread_kernel(parts, *rest):
    out_o = rest[-1]
    total = summed(parts)

    def put(n, _):
        out_o[n] = total
        return 0

    lax.fori_loop(0, out_o.shape[0], put, 0)


def both_halves(core, mine, theirs, group, part, rows):
    a, b = mine[group, part, rows, :].astype(F32), theirs[group, part, rows, :].astype(F32)
    return jnp.where(core[0] == 0, a, b), jnp.where(core[0] == 0, b, a)


def unpack_mlp_kernel(core, mine, theirs, return_o, hidden_o, output_o):
    width = return_o.shape[1]
    lanes = width // 128
    each = (mine.shape[2] - 16) // 16

    def one(group, _):
        for tile in range(2 * each):
            rows = slice(tile % each * 16, tile % each * 16 + 16)
            first, second = both_halves(core, mine, theirs, group, tile // each, rows)
            block, n = divmod(tile, lanes)
            here = pl.ds(pl.multiple_of(block * width + group * 16, 16), 16)
            return_o[here, n * 128 : (n + 1) * 128] = first
            here = pl.ds(pl.multiple_of(group * 16, 16), 16)
            hidden_o[here, block * width + n * 128 : block * width + (n + 1) * 128] = second
        return 0

    lax.fori_loop(0, width // 16, one, 0)
    half = width // 2

    def last(row, _):
        for n in range(lanes):
            chip = slice(each * 16, each * 16 + 16)
            first, second = both_halves(core, mine, theirs, row * (lanes // 2) + n // 2, n % 2, chip)
            output_o[pl.ds(pl.multiple_of(row * 16, 16), 16), n * 128 : (n + 1) * 128] = first
            output_o[pl.ds(pl.multiple_of(half + row * 16, 16), 16), n * 128 : (n + 1) * 128] = second
        return 0

    lax.fori_loop(0, half // 16, last, 0)


def unpack_kernel(core, mine, theirs, attn_o, stride_o, stem_o, *rest):
    vectors, ends = rest[:-1], rest[-1]
    width = stride_o.shape[1]
    lanes = width // 128
    each = (mine.shape[2] - 16) // 16

    def run(first_of, second_of):
        def one(group, _):
            at = group * 16
            for tile in range(2 * each):
                rows = slice(tile % each * 16, tile % each * 16 + 16)
                first = first_of[group, tile // each, rows, :].astype(F32)
                second = second_of[group, tile // each, rows, :].astype(F32)
                attn_o[pl.ds(pl.multiple_of(at, 16), 16), tile * 128 : (tile + 1) * 128] = first
                block, n = divmod(tile, lanes)
                stride_o[pl.ds(pl.multiple_of(block * width + at, 16), 16), n * 128 : (n + 1) * 128] = second
            return 0

        lax.fori_loop(0, mine.shape[0], one, 0)

    @pl.when(core[0] == 0)
    def _():
        run(mine, theirs)

    @pl.when(core[0] != 0)
    def _():
        run(theirs, mine)

    last = slice(each * 16, each * 16 + 16)
    for row in range(ends.shape[0] // 16):
        for n in range(lanes):
            chip = row * lanes + n
            first, second = both_halves(core, mine, theirs, chip // 2, chip % 2, last)
            ends[row * 16 : row * 16 + 16, n * 128 : (n + 1) * 128] = first + second
    mels = stem_o.shape[0]
    stem_o[...] = ends[:mels, :]
    row = mels
    for out in vectors:
        for n in range(out.shape[0] // width):
            out[n * width : (n + 1) * width] = ends[row + n : row + n + 1, :].reshape(width)
        row += out.shape[0] // width


def move(block, distance):
    count = lax.axis_size("frames")
    return lax.ppermute(block, "frames", [(d, (d + distance) % count) for d in range(count)])


def trade(block, odd):
    count = lax.axis_size("frames")

    def partner(device):
        chip, core = device // 2, device % 2
        other = chip + 1 if chip % 2 == odd else chip - 1
        return 2 * other + core if 0 <= other < count // 2 else device

    return lax.ppermute(block, "frames", [(d, partner(d)) for d in range(count)])


def swap(block):
    count = lax.axis_size("frames")
    return lax.ppermute(block, "frames", [(d, d ^ 1) for d in range(count)])


def cost(us):
    return pl.CostEstimate(flops=int(us * 1.1e9), bytes_accessed=int(us * 2e6), transcendentals=0)


def call(kernel, outs, args, scratch=(), specs=None, limit=56, us=10, out_specs=None):
    vmem = pl.BlockSpec(memory_space=pltpu.VMEM)
    return pl.pallas_call(
        kernel,
        out_shape=[jax.ShapeDtypeStruct(s, d) for s, d in outs],
        in_specs=specs if specs is not None else [vmem] * len(args),
        out_specs=out_specs if out_specs is not None else [vmem] * len(outs),
        scratch_shapes=list(scratch),
        compiler_params=pltpu.CompilerParams(vmem_limit_bytes=limit * MIB),
        cost_estimate=cost(us),
    )(*args)


MARK = ((8, 128), F32)


def chip_groups():
    chips = lax.axis_size("frames") // 2
    return [[2 * n + core for n in range(chips)] for core in range(2)]


def follow(value, other):
    hbm = pl.BlockSpec(memory_space=pl.ANY)
    return pl.pallas_call(
        lambda value_in, other_in, value_out: None,
        out_shape=jax.ShapeDtypeStruct(value.shape, value.dtype),
        in_specs=[hbm, hbm],
        out_specs=hbm,
        input_output_aliases={0: 0},
        cost_estimate=cost(1),
    )(value, other)


def over_chips(block):
    parts = block.reshape((-1,) + block.shape[2:])
    return lax.all_to_all(parts, "frames", 0, 0, axis_index_groups=chip_groups(), tiled=True)


def local(
    mel_frames, clip_lengths, valid_keys, stem_weight, stem_bias, stride_weight, stride_bias, attn_gain, attn_shift,
    attn_weight, query_bias, value_bias, output_weight, output_bias, mlp_gain, mlp_shift, hidden_weight, hidden_bias,
    return_weight, return_bias, cotangent,
):
    count, width = cotangent.shape
    ff = hidden_weight.shape[1]
    mels = mel_frames.shape[1]
    devices = lax.axis_size("frames")
    device = lax.axis_index("frames")
    core = device % 2
    nb = 2 * SIDE + 1
    ext = count + 2 * PAD
    base = (device - core - 2 * SIDE) * count

    left, right = move(mel_frames[-2:], 1), move(mel_frames[:2], -1)

    smem = pl.BlockSpec(memory_space=pltpu.SMEM)
    vmem = pl.BlockSpec(memory_space=pltpu.VMEM)
    hbm = pl.BlockSpec(memory_space=pl.ANY)
    whole = pltpu.VMEM((count, 128), jnp.int32)
    spans, pack, table, key_plan, query_plan = pl.pallas_call(
        functools.partial(tables_kernel, total=devices * count),
        out_shape=[
            jax.ShapeDtypeStruct(s, d)
            for s, d in (
                ((count, 128), jnp.int32), ((ext, 128), F32), ((count, width), F32), ((16,), jnp.int32), ((16,), jnp.int32)
            )
        ],
        in_specs=[smem] * 3,
        out_specs=[vmem] * 3 + [smem] * 2,
        scratch_shapes=[whole] * 3,
        cost_estimate=cost(4),
    )(device[None].astype(jnp.int32), clip_lengths, valid_keys)

    x, columns, dstem, dstride, layer_in, attn_in = call(
        stem_kernel,
        [
            ((ext, 4 * SLOT), BF), ((count, 3 * width), BF), ((ext, 2 * width), F32), ((count, width), F32), ((count, width), F32),
            ((count, width), BF),
        ],
        (
            mel_frames, left, right, stem_weight, stem_bias, stride_weight, stride_bias, attn_gain, attn_shift, pack, table,
        ),
        [pltpu.VMEM((2 * ext + 16, SLOT), F32), pltpu.VMEM((4 * SLOT, 2 * width), BF), pltpu.VMEM((ext, width), F32)],
        us=7,
        limit=24,
    )

    joint = jnp.concatenate([query_bias.astype(F32), jnp.zeros((width,), F32), value_bias.astype(F32)])

    def project(block):
        return (nn(block, attn_weight) + joint).astype(BF)

    def after(value, *others):
        return lax.optimization_barrier((value, *others))[0]

    def gather(block, pair):
        own, sib = {0: project(block)}, {0: project(pair)}
        ends = block, block
        done = [own[0], sib[0]]
        for k in range(1, SIDE + 1):
            ends = trade(ends[1], 1), trade(ends[0], 0)
            if k == 1:
                ends = after(ends[0], *done), after(ends[1], *done)
            here, there = dict(zip((-k, k), ends)), {n: swap(b) for n, b in zip((-k, k), ends)}
            for n in (-k, k):
                own[n] = project(after(here[n], *(done if k == SIDE else there.values())))
            for n in (-k, k):
                sib[n] = project(after(there[n], own[-k], own[k]))
            done += [v[n] for v in (own, sib) for n in (-k, k)]
        order = range(-SIDE, SIDE + 1)
        return [own[n] for n in order], [sib[n] for n in order]

    pair_in = swap(attn_in)
    own, sib = gather(attn_in, pair_in)
    pair_columns = lax.ppermute(columns, "frames", [(d, d + 1) for d in range(0, devices, 2)])
    reach = 2 * nb * count + KB
    pairs = width // 128
    sems = pltpu.SemaphoreType.DMA((2 * nb, 2))
    count_of = pltpu.SMEM((1,), jnp.int32)

    stacked = pltpu.VMEM((pairs, 2 * QB, 128), BF)
    summed = pltpu.VMEM((pairs, 2 * QB, 128), F32)
    score = pltpu.VMEM((2, pairs, 2 * QB, KB), F32)
    weight = pltpu.VMEM((2, pairs, 2 * QB, KB), BF)
    one_sem = pltpu.SemaphoreType.DMA((1,))
    local_query = pltpu.VMEM((count, width), BF)

    core1 = core[None].astype(jnp.int32)
    bundle = ff + 2 * width + width // 2
    block_f32 = pltpu.VMEM((count, width), F32)
    lse, layer_out, keep, send, grad_middle, pay, dlt, sums1 = call(
        layer_kernel,
        [
            ((count, 128), F32), ((count, width), BF), ((count, bundle), BF), ((count, bundle), BF), ((count, width), F32),
            ((count + 48, width), BF), ((count, 128), F32), ((8, width), F32),
        ],
        (
            key_plan, spans, *own, *sib, layer_in, cotangent, output_weight, hidden_weight, return_weight, output_bias,
            hidden_bias, return_bias, mlp_gain, mlp_shift,
        ),
        [
            block_f32, local_query, pltpu.VMEM((reach, 2 * width), BF), stacked, summed, summed, summed, summed, score, weight,
            count_of, count_of, sems, pltpu.SemaphoreType.DMA((6,)),
            block_f32, local_query, pltpu.VMEM((width, width), BF), pltpu.VMEM((width, ff), BF), pltpu.VMEM((ff, width), BF),
            block_f32, block_f32, pltpu.VMEM((2, count, bundle), BF), pltpu.SemaphoreType.DMA((2 * (ff // width) + 6,)),
        ],
        [smem, vmem] + [hbm] * (2 * nb + 5) + [vmem] * 5,
        out_specs=[vmem, vmem, hbm, hbm] + [vmem] * 4,
        us=26,
    )

    got = swap(send)
    near = {-1: trade(pay, 1), 1: trade(pay, 0)}

    grad_query, query_mark = call(
        query_kernel,
        [((count, width), BF), MARK],
        (key_plan, spans, pay, lse, dlt, *own, *sib),
        [
            local_query, pltpu.VMEM((reach, 2 * width), BF), stacked, stacked, summed, summed, summed, score, score, weight,
            count_of, count_of, sems, one_sem,
        ],
        [smem] + [vmem] * 4 + [hbm] * (2 * nb),
        us=15,
        limit=56,
    )
    near = {k: follow(b, query_mark) for k, b in near.items()}
    far = {-2: trade(near[1], 1), 2: trade(near[-1], 0)}

    blocks = ff // width
    groups = width // 16
    tiles = (groups, 2, 16 * (blocks * pairs // 2 + 1), 128)

    def at(n):
        return pl.BlockSpec((count, width), lambda i, core: (0, n))

    def each(i, core):
        return (0, jnp.minimum(i, blocks - 1))

    bundle_specs = [
        pl.BlockSpec((count, width), each), at(blocks), at(blocks + 1),
        pl.BlockSpec((count, width // 2), lambda i, core: (0, 2 * (blocks + 2))),
    ]
    mlp_both = pl.pallas_call(
        mlp_weights_kernel,
        out_shape=jax.ShapeDtypeStruct(tiles, BF),
        grid_spec=pltpu.PrefetchScalarGridSpec(
            num_scalar_prefetch=1,
            grid=(blocks + 1,),
            in_specs=bundle_specs * 2 + [hbm] * 2,
            out_specs=pl.BlockSpec(tiles, lambda i, core: (0, 0, 0, 0)),
        ),
        compiler_params=pltpu.CompilerParams(vmem_limit_bytes=60 * MIB),
        cost_estimate=cost(5.0),
    )(core1, keep, keep, keep, keep, got, got, got, got, near[-1], near[1])

    travel = {0: pay, **near, **{k: follow(b, mlp_both) for k, b in far.items()}}
    sib_pay = {k: swap(travel[k]) for k in travel}
    own_pay, sib_pay = ([v[k] for k in range(-SIDE, SIDE + 1)] for v in (travel, sib_pay))

    grad_projected, gsp, sums2 = call(
        key_kernel,
        [((count, 3 * width), BF), ((count, width), BF), ((8, width), F32)],
        (
            query_plan, spans, grad_query, attn_weight, layer_in, grad_middle, attn_gain,
            dstride, *own, *sib, *own_pay, *sib_pay,
        ),
        [
            pltpu.VMEM((count, 2 * width), BF), pltpu.VMEM((reach, width), BF), pltpu.VMEM((reach, width), BF),
            pltpu.VMEM((48, reach), BF), pltpu.VMEM((8, reach), F32), pltpu.VMEM((8, reach), F32), stacked, stacked, summed, summed, score, score, weight,
            weight, count_of, count_of, sems, pltpu.SemaphoreType.DMA((2 * nb, 1)),
            one_sem,
        ],
        [smem] + [vmem] * 7 + [hbm] * (4 * nb),
        us=18,
        limit=56,
    )
    mlp_parts = over_chips(mlp_both)
    (mlp_spread,) = call(
        spread_kernel, [(mlp_parts.shape, BF)], (mlp_parts, sums2), specs=[vmem, hbm], us=3, limit=12
    )
    mlp_mine = over_chips(mlp_spread[:, None]).reshape(tiles)

    left, right = move(gsp[-1:], 1), move(gsp[:1], -1)

    gp_pair, gsp_pair = swap(grad_projected), swap(gsp)
    def whole_block(i, core):
        return (0, 0)

    def column_block(i, core):
        return (0, i)

    last_tiles = (groups, 2, 16 * (3 * pairs // 2 + 1), 128)
    last_specs = [pl.BlockSpec((count, width), m) for m in (whole_block, column_block, column_block, whole_block)]
    both = pl.pallas_call(
        last_weights_kernel,
        out_shape=jax.ShapeDtypeStruct(last_tiles, BF),
        grid_spec=pltpu.PrefetchScalarGridSpec(
            num_scalar_prefetch=1,
            grid=(3,),
            in_specs=last_specs * 2,
            out_specs=pl.BlockSpec(last_tiles, lambda i, core: (0, 0, 0, 0)),
        ),
        compiler_params=pltpu.CompilerParams(vmem_limit_bytes=20 * MIB),
        cost_estimate=cost(3),
    )(core1, attn_in, grad_projected, columns, gsp, pair_in, gp_pair, pair_columns, gsp_pair)
    gpre, both = pl.pallas_call(
        stem_back_kernel,
        out_shape=[jax.ShapeDtypeStruct((ext, 2 * width), BF), jax.ShapeDtypeStruct(last_tiles, BF)],
        in_specs=[vmem] * 9 + [hbm],
        out_specs=[vmem, hbm],
        scratch_shapes=[
            pltpu.VMEM((ext + 8, width), F32), pltpu.VMEM((ext, width), BF), pltpu.VMEM((ext, width), BF),
            pltpu.VMEM((3 * mels + 16, width), F32), pltpu.VMEM((groups, 2, 16, 128), BF), one_sem,
        ],
        input_output_aliases={9: 1},
        compiler_params=pltpu.CompilerParams(vmem_limit_bytes=20 * MIB),
        cost_estimate=cost(4),
    )(gsp, left, right, stride_weight, dstem, x, pack, sums1, sums2, both)

    (mel_grad,) = call(
        mel_kernel,
        [((2 * count, mels), F32)],
        (gpre, stem_weight, pack),
        [pltpu.VMEM((4 * SLOT, 2 * width), BF), pltpu.VMEM((ext, 4 * SLOT), F32)],
        us=3,
        limit=16,
    )

    mlp_mine = follow(mlp_mine, both)
    grad_return_weight, grad_hidden_weight, grad_output_weight = call(
        unpack_mlp_kernel,
        [((ff, width), F32), ((width, ff), F32), ((width, width), F32)],
        (core1, mlp_mine, swap(mlp_mine)),
        specs=[smem, vmem, vmem],
        us=5,
        limit=24,
    )
    parts = over_chips(both)
    (spread,) = call(
        spread_kernel, [(parts.shape, BF)], (parts, mel_grad, grad_output_weight), specs=[vmem, hbm, hbm], us=3, limit=12
    )
    mine = over_chips(spread[:, None]).reshape(last_tiles)
    sizes = [width] * 9 + [ff, width]
    grad_attn_weight, grad_stride_weight, grad_stem_weight, *bias = call(
        unpack_kernel,
        [((width, 3 * width), F32), ((3 * width, width), F32), ((3 * mels, width), F32)] + [((n,), F32) for n in sizes],
        (core1, mine, swap(mine)),
        [pltpu.VMEM((3 * mels + 16, width), F32)],
        [smem, vmem, vmem],
        us=6,
        limit=22,
    )
    return (
        layer_out, mel_grad, grad_stem_weight, bias[0], grad_stride_weight, bias[1], bias[2], bias[3], grad_attn_weight,
        bias[4], bias[5], grad_output_weight, bias[6], bias[7], bias[8], grad_hidden_weight, bias[9],
        grad_return_weight, bias[10],
    )


def solution(mesh):
    split = P("frames", None)
    in_specs = (split,) + (P(),) * 19 + (split,)
    out_specs = (split, split) + (P(),) * 17
    return jax.shard_map(local, mesh=mesh, in_specs=in_specs, out_specs=out_specs, check_vma=False)
```
